128 devices in a mesh: shot: 4 (over x_lo, core), aper: 32 (over z, y, x_hi).
Axes of the slice: x: 4 (x_hi: 2, x_lo: 2; x = x_hi * 2 + x_lo), y: 4, z: 4, core: 2. Of those that a mesh axis runs over, the one named last changes fastest.
Arguments:
- velocity: float32 [512, 32, 256], P(('shot', 'aper')), may hold values from 0.15 to 0.32
- thomsen_epsilon: float32 [512, 32, 256], P(('shot', 'aper')), may hold values from 0.12 to 0.3
- thomsen_delta: float32 [512, 32, 256], P(('shot', 'aper')), may hold values from -0.1 to 0.1
- tilt_angle: float32 [512, 32, 256], P(('shot', 'aper')), may hold values from -1 to 1
- fwd_now: float32 [4, 2, 128, 32, 256], P('shot', None, 'aper'), may hold values from -6 to 6
- fwd_before: float32 [4, 2, 128, 32, 256], P('shot', None, 'aper'), may hold values from -6 to 6
- adj_now: float32 [4, 2, 128, 32, 256], P('shot', None, 'aper'), may hold values from -6 to 6
- adj_before: float32 [4, 2, 128, 32, 256], P('shot', None, 'aper'), may hold values from -6 to 6
- wavelet: float32 [4, 4], replicated, may hold values from -12 to 12
- traces: float32 [4, 4, 256], replicated, may hold values from -10 to 10
- offsets: int32 [4], replicated, may hold values from 0 to 96, as said below
- source_cell: int32 [4, 3], replicated, may hold values from 0 to 255, as said below
- receiver_cell: int32 [4, 256, 3], replicated, may hold values from 0 to 127, as said below
Outputs:
- image_sum: float32 [512, 32, 256], P(('shot', 'aper'))
The draws below stay inside these ranges and needn't reach their ends.
Inputs may be any that keep to these rules, and one draw needn't show every extreme that they name: `offsets`: model tiles are 4 cells long; in every draw one group has offset 0, one has (3) * 32, and one leaves the remainder 32 - 1 modulo 32. `source_cell`: first index below 128, second below 32, third below 256. `receiver_cell`: first index below 128, second below 32, third from 2 to 5; cells may coincide.
All inputs are finite; a program needn't handle non-finite values.
Results may differ from the reference program's by a relative error of at most 0.00002.
Values sent between devices are 32-bit elements; how exact they have to be, the bound alone decides.
No kernel may reach another device: no remote copies, remote signals or barrier semaphores. Data moves between devices by JAX's collectives and lax.ppermute only.
A program may use at most 64 MiB of HBM per device.

```python
import jax
import jax.numpy as jnp
from jax import lax

TX = 4
AY = 32
AZ = 256
ITERS = 4
NREC = 256
NXA = 128
MX = 512
N_SHOT = 4
N_APER = 32


def draw_offsets(key, part):
    key = jax.random.fold_in(key, 11)
    first_key, second_key, third_key = jax.random.split(key, 3)
    spread = (N_SHOT - 1) * N_APER
    chosen = jax.random.randint(first_key, (N_SHOT,), 0, spread + 1)
    order = jax.random.permutation(second_key, N_SHOT)
    leftover_row = jax.random.randint(third_key, (), 0, N_SHOT - 1)
    chosen = chosen.at[order[0]].set(0)
    chosen = chosen.at[order[1]].set(spread)
    chosen = chosen.at[order[2]].set(leftover_row * N_APER + N_APER - 1)
    return chosen.astype(jnp.int32)


def draw_source_cell(key, part):
    key = jax.random.fold_in(key, 12)
    first_key, second_key, third_key = jax.random.split(key, 3)
    first_index = jax.random.randint(first_key, (N_SHOT,), 0, NXA)
    second_index = jax.random.randint(second_key, (N_SHOT,), 0, AY)
    third_index = jax.random.randint(third_key, (N_SHOT,), 0, AZ)
    first_index = first_index.at[0].set(NXA - 1).at[1].set(0)
    second_index = second_index.at[0].set(AY - 1).at[1].set(0)
    third_index = third_index.at[0].set(AZ - 1).at[1].set(0)
    return jnp.stack([first_index, second_index, third_index], axis=1).astype(jnp.int32)


def draw_receiver_cell(key, part):
    key = jax.random.fold_in(key, 13)
    first_key, second_key, third_key = jax.random.split(key, 3)
    first_index = jax.random.randint(first_key, (N_SHOT, NREC), 0, NXA)
    second_index = jax.random.randint(second_key, (N_SHOT, NREC), 0, AY)
    third_index = jax.random.randint(third_key, (N_SHOT, NREC), 2, 6)
    first_index = first_index.at[0, 0].set(NXA - 1).at[0, 1].set(0)
    second_index = second_index.at[0, 0].set(AY - 1).at[0, 1].set(0)
    third_index = third_index.at[0, 0].set(5).at[0, 1].set(2)
    return jnp.stack([first_index, second_index, third_index], axis=2).astype(jnp.int32)


def steps_of(rng, dims, cuts, low, top_value):
    def one(axis_at, blocks):
        steps = jax.random.uniform(jax.random.fold_in(jax.random.fold_in(rng, 6), axis_at), (blocks,), jnp.float32, low / len(cuts), top_value / len(cuts))
        return jnp.repeat(jnp.exp(steps), dims[axis_at] // blocks).reshape((-1,) + (1,) * (len(dims) - axis_at - 1))

    gain = one(*cuts[0])
    for cut in cuts[1:]:
        gain = gain * one(*cut)
    return gain


def bell_draw(rng, dims, scale, reach, cuts=(), dtype=jnp.bfloat16):
    drawn = scale * jax.random.normal(rng, dims, jnp.float32)
    if cuts:
        drawn = drawn * steps_of(rng, dims, cuts, -0.22, 0.18)
    return jnp.clip(drawn, -reach, reach).astype(dtype)


def setup_inputs(seed: int = 0) -> dict:
    arg_keys = jax.random.split(jax.random.key(seed), 14)
    return {
        "velocity": jnp.clip(0.15 + 0.16999999 * jax.random.uniform(arg_keys[0], (MX, AY, AZ), jnp.float32) ** steps_of(arg_keys[0], (MX, AY, AZ), ((0, 128),), -0.2, 0.2), 0.15, 0.32),
        "thomsen_epsilon": jnp.clip(0.12 + 0.18 * jax.random.uniform(arg_keys[1], (MX, AY, AZ), jnp.float32) ** steps_of(arg_keys[1], (MX, AY, AZ), ((0, 128),), -0.2, 0.2), 0.12, 0.3),
        "thomsen_delta": jnp.clip(jax.random.uniform(arg_keys[2], (MX, AY, AZ), jnp.float32, -0.1, 0.1) * steps_of(arg_keys[2], (MX, AY, AZ), ((0, 128),), -0.4, 0.0), -0.1, 0.1),
        "tilt_angle": jnp.clip(jax.random.uniform(arg_keys[3], (MX, AY, AZ), jnp.float32, -1.0, 1.0) * steps_of(arg_keys[3], (MX, AY, AZ), ((0, 128),), -0.4, 0.0), -1.0, 1.0),
        "fwd_now": bell_draw(arg_keys[4], (N_SHOT, 2, NXA, AY, AZ), 1.0, 6.0, ((0, 4), (2, 32)), jnp.float32),
        "fwd_before": bell_draw(arg_keys[5], (N_SHOT, 2, NXA, AY, AZ), 1.0, 6.0, ((0, 4), (2, 32)), jnp.float32),
        "adj_now": bell_draw(arg_keys[6], (N_SHOT, 2, NXA, AY, AZ), 1.0, 6.0, ((0, 4), (2, 32)), jnp.float32),
        "adj_before": bell_draw(arg_keys[7], (N_SHOT, 2, NXA, AY, AZ), 1.0, 6.0, ((0, 4), (2, 32)), jnp.float32),
        "wavelet": bell_draw(arg_keys[8], (N_SHOT, ITERS), 3.0, 12.0, (), jnp.float32),
        "traces": bell_draw(arg_keys[9], (N_SHOT, ITERS, NREC), 2.0, 10.0, (), jnp.float32),
        "offsets": draw_offsets(jax.random.fold_in(arg_keys[13], 71), 0),
        "source_cell": draw_source_cell(jax.random.fold_in(arg_keys[13], 71), 0),
        "receiver_cell": draw_receiver_cell(jax.random.fold_in(arg_keys[13], 71), 0),
    }


second_coef = (-205.0 / 72.0, 8.0 / 5.0, -1.0 / 5.0, 8.0 / 315.0, -1.0 / 560.0)
first_coef = (4.0 / 5.0, -1.0 / 5.0, 4.0 / 105.0, -1.0 / 280.0)

def window(padded, axis_dim, offset, length):
    return lax.slice_in_dim(padded, 4 + offset, 4 + offset + length, axis=axis_dim)

def second_diff(padded, axis_dim):
    length = padded.shape[axis_dim] - 8
    result = second_coef[0] * window(padded, axis_dim, 0, length)
    for distance in range(1, 5):
        result = result + second_coef[distance] * (window(padded, axis_dim, distance, length) + window(padded, axis_dim, -distance, length))
    return result

def first_diff(padded, axis_dim):
    length = padded.shape[axis_dim] - 8
    result = first_coef[0] * (window(padded, axis_dim, 1, length) - window(padded, axis_dim, -1, length))
    for distance in range(2, 5):
        result = result + first_coef[distance - 1] * (window(padded, axis_dim, distance, length) - window(padded, axis_dim, -distance, length))
    return result

def pad_axis(array_in, axis_dim):
    widths = [(0, 0)] * array_in.ndim
    widths[axis_dim] = (4, 4)
    return jnp.pad(array_in, widths)

def coefficients(velocity, thomsen_epsilon, thomsen_delta, tilt_angle):
    square = velocity * velocity
    aniso_speed = square * (1.0 + 2.0 * thomsen_epsilon)
    coupled = square * jnp.sqrt(1.0 + 2.0 * thomsen_delta)
    return (aniso_speed, coupled, square, jnp.sin(tilt_angle) ** 2, jnp.cos(tilt_angle) ** 2, jnp.sin(2.0 * tilt_angle))

def update(wide_p, wide_q, before_p, before_q, coef_set):
    aniso_speed, coupled, square, sine_sq, cosine_sq, double_sin = coef_set
    core_p = wide_p[4:-4]
    core_q = wide_q[4:-4]
    curve_xp = second_diff(wide_p, 0)
    curve_yp = second_diff(pad_axis(core_p, 1), 1)
    curve_zp = second_diff(pad_axis(core_p, 2), 2)
    cross_p = first_diff(pad_axis(first_diff(wide_p, 0), 2), 2)
    axial_p = sine_sq * curve_xp + cosine_sq * curve_zp + double_sin * cross_p
    plane_p = curve_xp + curve_yp + curve_zp - axial_p
    curve_xq = second_diff(wide_q, 0)
    curve_zq = second_diff(pad_axis(core_q, 2), 2)
    cross_q = first_diff(pad_axis(first_diff(wide_q, 0), 2), 2)
    axial_q = sine_sq * curve_xq + cosine_sq * curve_zq + double_sin * cross_q
    new_p = 2.0 * core_p - before_p + aniso_speed * plane_p + coupled * axial_q
    new_q = 2.0 * core_q - before_q + coupled * plane_p + square * axial_q
    return (new_p, new_q)

def march(current, before, coef_set, grid_cells, amounts):
    saved_list = []
    for moment in range(ITERS):
        new_p, new_q = update(pad_axis(current[0], 0), pad_axis(current[1], 0), before[0], before[1], coef_set)
        fresh_pair = jnp.stack([new_p, new_q])
        fresh_pair = fresh_pair.at[:, grid_cells[:, 0], grid_cells[:, 1], grid_cells[:, 2]].add(amounts[moment])
        before, current = (current, fresh_pair)
        saved_list.append(fresh_pair[0])
    return saved_list

def reference(velocity, thomsen_epsilon, thomsen_delta, tilt_angle, fwd_now, fwd_before, adj_now, adj_before, wavelet, traces, offsets, source_cell, receiver_cell):
    image_sum = jnp.zeros((MX, AY, AZ), jnp.float32)
    for group_id in range(N_SHOT):
        start_row = (offsets[group_id] * TX).astype(jnp.int32)
        coef_set = coefficients(lax.dynamic_slice_in_dim(velocity, start_row, NXA, 0), lax.dynamic_slice_in_dim(thomsen_epsilon, start_row, NXA, 0), lax.dynamic_slice_in_dim(thomsen_delta, start_row, NXA, 0), lax.dynamic_slice_in_dim(tilt_angle, start_row, NXA, 0))
        forward_saved = march(fwd_now[group_id], fwd_before[group_id], coef_set, source_cell[group_id][None, :], wavelet[group_id][:, None])
        adjoint_saved = march(adj_now[group_id], adj_before[group_id], coef_set, receiver_cell[group_id], traces[group_id])
        contrib = jnp.zeros((NXA, AY, AZ), jnp.float32)
        for moment in range(ITERS):
            contrib = contrib + forward_saved[ITERS - 1 - moment] * adjoint_saved[moment]
        current_rows = lax.dynamic_slice_in_dim(image_sum, start_row, NXA, 0)
        image_sum = lax.dynamic_update_slice_in_dim(image_sum, current_rows + contrib, start_row, 0)
    return image_sum
```

```python
import jax
import jax.numpy as jnp
from jax import lax
from jax.experimental import pallas as pl
from jax.experimental.pallas import tpu as pltpu
from jax.sharding import PartitionSpec as P

second_coef = (-205.0 / 72.0, 8.0 / 5.0, -1.0 / 5.0, 8.0 / 315.0, -1.0 / 560.0)
first_coef = (4.0 / 5.0, -1.0 / 5.0, 4.0 / 105.0, -1.0 / 280.0)

AXES = ("shot", "aper")
STEPS = 4
TX = 4
AY = 32
AZ = 256
HALF = 128
F32 = jnp.float32
VMEM = pl.BlockSpec(memory_space=pltpu.VMEM)
SMEM = pl.BlockSpec(memory_space=pltpu.SMEM)


def device(x, core, y, z):
    return ((x % 2) * 2 + core) * 32 + ((z % 4) * 4 + y % 4) * 2 + x // 2


def everyone():
    return [(x, c, y, z) for x in range(4) for c in range(2) for y in range(4) for z in range(4)]


def flipped(y, z):
    return 3 - y if z % 2 else y


def on_path(j):
    j = j % 16
    return flipped(j % 4, j // 4), j // 4


def path_place(y, z):
    return 4 * z + flipped(y, z)


def pairs_of(rule):
    pairs = [(device(*d), device(*rule(*d))) for d in everyone()]
    assert sorted(t for _, t in pairs) == list(range(128))
    assert all(s != t for s, t in pairs)
    return pairs


def send(value, pairs):
    return lax.ppermute(value, AXES, pairs)


def other_core():
    return pairs_of(lambda x, c, y, z: (x, 1 - c, y, z))


def along_path(by):
    def rule(x, c, y, z):
        return (x, c) + on_path(path_place(y, z) + by)

    return pairs_of(rule)


def state_first():
    def rule(x, c, y, z):
        hi = x // 2
        t = {(0, 0): (0, 1), (0, 1): (1, 1), (1, 0): (0, 0), (1, 1): (1, 0)}[(hi, c)]
        return (2 * t[0] + x % 2, t[1], flipped(y, z), z)

    return pairs_of(rule)


def state_second():
    def rule(x, c, y, z):
        hi = x // 2
        if hi == c:
            return (x, c, 3 - y, z)
        return (2 * (1 - hi) + x % 2, 1 - c, flipped(y, z), z)

    return pairs_of(rule)


def model_back(by_low, by_high):
    def rule(x, c, y, z):
        j = (4 * z + y - (by_high if x // 2 else by_low)) % 16
        return (x, c, j % 4, j // 4)

    return pairs_of(rule)


def model_across(by):
    def rule(x, c, y, z):
        if by == 0:
            return (x, c, 3 - y, z)
        return ((x + by) % 4, c, flipped(y, z), z)

    return pairs_of(rule)


def image_turn(r):
    def rule(x, c, y, z):
        col = (2 * path_place(y, z) + c + r) % 32
        return (x, col % 2) + on_path(col // 2)

    return pairs_of(rule)


def image_across(by):
    def rule(x, c, y, z):
        q = (x + by) % 4
        target = (2 * c + q // 2, q % 2)
        if target == (x, c):
            return (x, c, 3 - y, z)
        return target + (flipped(y, z), z)

    return pairs_of(rule)


def z_plus(pair, d, lane):
    a, b = pair
    ra, rb = pltpu.roll(a, HALF - d, 1), pltpu.roll(b, HALF - d, 1)
    keep = lane < HALF - d
    return jnp.where(keep, ra, rb), jnp.where(keep, rb, 0.0)


def z_minus(pair, d, lane):
    a, b = pair
    ra, rb = pltpu.roll(a, d, 1), pltpu.roll(b, d, 1)
    keep = lane >= d
    return jnp.where(keep, ra, 0.0), jnp.where(keep, rb, ra)


def second_z(pair, lane):
    out = [second_coef[0] * v for v in pair]
    for d in range(1, 5):
        up, down = z_plus(pair, d, lane), z_minus(pair, d, lane)
        out = [o + second_coef[d] * (u + w) for o, u, w in zip(out, up, down)]
    return out


def first_z(pair, lane):
    out = None
    for d in range(1, 5):
        up, down = z_plus(pair, d, lane), z_minus(pair, d, lane)
        term = [first_coef[d - 1] * (u - w) for u, w in zip(up, down)]
        out = term if out is None else [o + t for o, t in zip(out, term)]
    return out


def second_y(pair, row):
    out = []
    for f in pair:
        acc = second_coef[0] * f
        for d in range(1, 5):
            up = jnp.where(row < AY - d, pltpu.roll(f, AY - d, 0), 0.0)
            down = jnp.where(row >= d, pltpu.roll(f, d, 0), 0.0)
            acc = acc + second_coef[d] * (up + down)
        out.append(acc)
    return out


def x_parts(rows):
    second, first = [], []
    for s in range(2):
        acc = second_coef[0] * rows[4][s]
        der = None
        for d in range(1, 5):
            acc = acc + second_coef[d] * (rows[4 + d][s] + rows[4 - d][s])
            term = first_coef[d - 1] * (rows[4 + d][s] - rows[4 - d][s])
            der = term if der is None else der + term
        second.append(acc)
        first.append(der)
    return second, first


def place(ids_ref):
    shot, aper = ids_ref[0], ids_ref[1]
    core = lax.rem(shot, 2)
    x_lo = lax.div(shot, 2)
    x_hi = lax.rem(aper, 2)
    z = lax.div(aper, 8)
    y = lax.rem(lax.div(aper, 2), 4)
    j = 4 * z + jnp.where(lax.rem(z, 2) == 1, 3 - y, y)
    return core, x_lo, x_hi, z, y, j


def step_kernel(ids, lo, hi, lo_b, hi_b, low, high, coef, inj, new_lo, new_hi, *rest):
    packed, ext = (rest[0], rest[1]) if len(rest) == 2 else (None, rest[0])
    outs = (new_lo, new_hi)
    core, _, _, _, _, j = place(ids)
    first, last = j == 0, j == 15
    for p in range(2):
        for i in range(TX):
            ext[p, i] = jnp.where(first, 0.0, low[p, i])
            ext[p, TX + i] = lo[p, i]
            ext[p, 2 * TX + i] = hi[p, i]
            ext[p, 3 * TX + i] = jnp.where(last, 0.0, high[p, i])
    for t, back in enumerate((lo_b, hi_b)):

        def tile(i, carry, t=t, back=back):
            def emit(h, new_p, new_q):
                outs[t][0, i, :, h] = new_p
                outs[t][1, i, :, h] = new_q
                if packed is not None:
                    packed[t, i, :, h] = new_p

            one_row(ext, t * TX + i, lambda p, h: back[p, i, :, h], coef, inj, emit)
            return carry

        lax.fori_loop(0, TX, tile, 0)


def one_row(ext, i, before, coef, inj, emit):
    lane = lax.broadcasted_iota(jnp.int32, (AY, HALF), 1)
    row = lax.broadcasted_iota(jnp.int32, (AY, HALF), 0)
    halves = (pl.ds(0, HALF), pl.ds(HALF, HALF))
    parts = []
    for p in range(2):
        rows = [[ext[p, i + d, :, h] for h in halves] for d in range(9)]
        curve_x, slope_x = x_parts(rows)
        parts.append((rows[4], curve_x, second_z(rows[4], lane), first_z(slope_x, lane)))
    (mid_p, xp, zp, cp), (mid_q, xq, zq, cq) = parts
    yp = second_y(mid_p, row)
    for s, h in enumerate(halves):
        aniso, coupled, square = coef[0, i, :, h], coef[1, i, :, h], coef[2, i, :, h]
        sine, cosine, double = coef[3, i, :, h], coef[4, i, :, h], coef[5, i, :, h]
        axial_p = sine * xp[s] + cosine * zp[s] + double * cp[s]
        plane_p = xp[s] + yp[s] + zp[s] - axial_p
        axial_q = sine * xq[s] + cosine * zq[s] + double * cq[s]
        add = inj[i, :, h]
        new_p = 2.0 * mid_p[s] - before(0, h) + aniso * plane_p + coupled * axial_q + add
        new_q = 2.0 * mid_q[s] - before(1, h) + coupled * plane_p + square * axial_q + add
        emit(h, new_p, new_q)


def last_kernel(ids, lo, hi, lo_b, hi_b, low, high, coef, inj, other_1, other_2, keep, give, ext):
    core, _, _, _, _, j = place(ids)
    first, last = j == 0, j == 15
    for p in range(2):
        for i in range(TX):
            ext[p, i] = jnp.where(first, 0.0, low[p, i])
            ext[p, TX + i] = lo[p, i]
            ext[p, 2 * TX + i] = hi[p, i]
            ext[p, 3 * TX + i] = jnp.where(last, 0.0, high[p, i])
    for t, back in enumerate((lo_b, hi_b)):
        mid = (lo, hi)[t]

        def tile(i, carry, t=t, back=back, mid=mid):
            def emit(h, new_p, new_q):
                part = new_p * other_1[t, i, :, h] + mid[0, i, :, h] * other_2[t, i, :, h]

                @pl.when(core == t)
                def _():
                    keep[i, :, h] = part

                @pl.when(core != t)
                def _():
                    give[i, :, h] = part

            one_row(ext, t * TX + i, lambda p, h: back[p, i, :, h], coef, inj, emit)
            return carry

        lax.fori_loop(0, TX, tile, 0)


def inject_kernel(ids, cells, amounts, out):
    _, _, _, _, _, j = place(ids)
    x = cells[0:1, :] - 8 * j
    here = (x >= 0) & (x < 8)
    spot = jnp.where(here, x * AY + cells[1:2, :], -1)
    depth = cells[2:3, :]
    count = cells.shape[1]
    which = (lax.broadcasted_iota(jnp.int32, (8 * AY, count), 0) == spot).astype(F32)
    level = lax.broadcasted_iota(jnp.int32, (AZ, count), 0) == depth
    for k in range(STEPS):
        values = jnp.where(level, amounts[k : k + 1, :], 0.0)
        flat = lax.dot_general(
            which,
            values,
            (((1,), (1,)), ((), ())),
            precision=lax.Precision.HIGHEST,
            preferred_element_type=F32,
        )
        for i in range(8):
            out[k, i] = flat[i * AY : (i + 1) * AY, :]


def sine_cosine(angle):
    sq = angle * angle
    sine = -1.0 / 39916800.0
    for c in (1.0 / 362880.0, -1.0 / 5040.0, 1.0 / 120.0, -1.0 / 6.0, 1.0):
        sine = sine * sq + c
    cosine = 1.0 / 479001600.0
    for c in (-1.0 / 3628800.0, 1.0 / 40320.0, -1.0 / 720.0, 1.0 / 24.0, -0.5, 1.0):
        cosine = cosine * sq + c
    return sine * angle, cosine


def coef_kernel(ids, own, other, out):
    core, _, _, _, _, _ = place(ids)
    for t in range(2):

        def tile(i, carry, t=t):
            mine = [own[t, f, i] for f in range(2)]
            theirs = [other[t, f, i] for f in range(2)]
            velocity = jnp.where(core == 0, mine[0], theirs[0])
            epsilon = jnp.where(core == 0, mine[1], theirs[1])
            delta = jnp.where(core == 0, theirs[0], mine[0])
            angle = jnp.where(core == 0, theirs[1], mine[1])
            square = velocity * velocity
            sine, cosine = sine_cosine(angle)
            k = t * TX + i
            out[0, k] = square * (1.0 + 2.0 * epsilon)
            out[1, k] = square * jnp.sqrt(1.0 + 2.0 * delta)
            out[2, k] = square
            out[3, k] = sine * sine
            out[4, k] = cosine * cosine
            out[5, k] = 2.0 * sine * cosine
            return carry

        lax.fori_loop(0, TX, tile, 0)


def call(kernel, n_in, outs, scratch=()):
    return pl.pallas_call(
        kernel,
        out_shape=[jax.ShapeDtypeStruct(s, F32) for s in outs],
        in_specs=[SMEM] + [VMEM] * n_in,
        out_specs=[VMEM] * len(outs),
        scratch_shapes=[pltpu.VMEM(s, F32) for s in scratch],
        compiler_params=pltpu.CompilerParams(vmem_limit_bytes=32 * 1024 * 1024),
    )


TILE = (2, TX, AY, AZ)


def local(
    velocity,
    thomsen_epsilon,
    thomsen_delta,
    tilt_angle,
    fwd_now,
    fwd_before,
    adj_now,
    adj_before,
    wavelet,
    traces,
    offsets,
    source_cell,
    receiver_cell,
):
    shot, aper = lax.axis_index("shot"), lax.axis_index("aper")
    core, x_lo, x_hi = shot % 2, shot // 2, aper % 2
    x = 2 * x_hi + x_lo
    z, y = aper // 8, (aper // 2) % 4
    odd_z = z % 2 == 1
    block = 4 * z + jnp.where(odd_z, 3 - y, y)
    group = 2 * x_lo + x_hi
    offset = offsets[group]
    turn = offset % 32
    ids = jnp.stack([shot, aper]).astype(jnp.int32)
    turns = offsets % 32
    free_turn = jnp.max(jnp.where((turns == 0) | (turns == 31), 0, turns))

    def pick(first, a, b):
        return jnp.where(first, a, b)

    first_pairs, second_pairs = state_first(), state_second()
    low_side = x_hi == 0
    stays = (x_hi == core) & ~odd_z
    own = []
    for fwd, adj in ((fwd_now[0], adj_now[0]), (fwd_before[0], adj_before[0])):
        one = send(pick(low_side, adj, fwd), first_pairs)
        kept = pick(low_side, fwd, adj)
        two = pick(stays, kept, send(kept, second_pairs))
        own.append((pick(core == 0, two, one), pick(core == 0, one, two)))
    (lo, hi), (lo_b, hi_b) = own

    swap = other_core()
    fields_a = jnp.stack([velocity, thomsen_epsilon])
    fields_b = jnp.stack([thomsen_delta, tilt_angle])
    own_fields = pick(core == 0, fields_a, fields_b)
    came = send(pick(core == 0, fields_b, fields_a), swap)
    both = jnp.stack([pick(core == 0, own_fields, came), pick(core == 0, came, own_fields)])
    both_last = pick(x_hi == 1, send(both, model_back(15, 15)), both)

    def turned(r):
        if r in (0, 31):
            return lambda v: v
        if r == 1:
            return lambda v: pick(x_hi == 1, v, send(v, model_back(1, 1)))
        return lambda v: send(v, model_back((r + 1) // 2, r // 2))

    both_free = lax.switch(free_turn, [turned(r) for r in range(32)], both)
    came = []
    for by in range(4):
        x_to = (x + by) % 4
        to = 2 * (x_to % 2) + x_to // 2
        o = offsets[to]
        r = o % 32
        h = x_hi ^ (o % 2)
        tile_row = (o + 2 * (4 * z + y) + h) // 32
        choice = jnp.where(r == 0, 0, jnp.where(r == 31, 1, 2)) * 2 + tile_row % 2
        payload = lax.select_n(
            choice, both[0], both[1], both_last[0], both_last[1], both_free[0], both_free[1]
        )
        got = send(payload, model_across(by))
        came.append(pick(odd_z, got, payload) if by == 0 else got)
    tiles = []
    for h in range(2):
        tile_row = (offset + 2 * block + h) // 32
        x_from = 2 * (h ^ (offset % 2)) + tile_row // 2
        tiles.append(lax.select_n((x - x_from) % 4, *came))
    half_fields = jnp.stack(tiles)
    other_fields = send(half_fields, swap)
    coef = call(coef_kernel, 2, [(6, 8, AY, AZ)])(ids, half_fields, other_fields)[0]

    n_rec = receiver_cell.shape[1]
    rec = receiver_cell[group].T
    src = jnp.where(jnp.arange(n_rec)[None, :] == 0, source_cell[group][:, None], -1000)
    pulse = jnp.where(jnp.arange(n_rec)[None, :] == 0, wavelet[group][:, None], 0.0)
    cells = pick(core == 0, src, rec)
    amounts = pick(core == 0, pulse, traces[group])
    inj = call(inject_kernel, 2, [(STEPS, 8, AY, AZ)])(ids, cells, amounts)[0]

    up, down = along_path(1), along_path(-1)
    shared = []
    for k in range(STEPS - 1):
        low, high = send(hi, up), send(lo, down)
        outs = [TILE, TILE] + ([(2, TX, AY, AZ)] if k < 2 else [])
        new = call(step_kernel, 8, outs, [(2, 4 * TX, AY, AZ)])(
            ids, lo, hi, lo_b, hi_b, low, high, coef, inj[k]
        )
        if k < 2:
            shared.append(send(new[2], swap))
        lo_b, hi_b, lo, hi = lo, hi, new[0], new[1]
    low, high = send(hi, up), send(lo, down)
    keep, give = call(last_kernel, 10, [(TX, AY, AZ)] * 2, [(2, 4 * TX, AY, AZ)])(
        ids, lo, hi, lo_b, hi_b, low, high, coef, inj[STEPS - 1], shared[0], shared[1]
    )
    total = keep + send(give, swap)

    total_last = send(total, image_turn(31))

    def image_turned(r):
        if r in (0, 31):
            return lambda v: v
        return lambda v: send(v, image_turn(r))

    total_free = lax.switch(free_turn, [image_turned(r) for r in range(32)], total)
    column = 2 * block + core
    aligned = pick(turn == 0, total, pick(turn == 31, total_last, total_free))
    to_row = offset // 32 + (column < turn).astype(jnp.int32)
    mine = x_hi == core
    image = None
    for by in range(4):
        row = (x + by) % 4
        payload = pick(to_row == row, aligned, 0.0)
        got = send(payload, image_across(by))
        to_self = mine & ~odd_z & (row == 2 * x_lo + core)
        got = pick(to_self, payload, got)
        image = got if image is None else image + got
    return image


def solution(mesh):
    model = P(("shot", "aper"), None, None)
    field = P("shot", None, "aper", None, None)
    return jax.shard_map(
        local,
        mesh=mesh,
        in_specs=(model,) * 4 + (field,) * 4 + (P(),) * 5,
        out_specs=model,
        check_vma=False,
    )
```

```python
import jax
import jax.numpy as jnp
from jax import lax
from jax.experimental import pallas as pl
from jax.experimental.pallas import tpu as pltpu
from jax.sharding import PartitionSpec as P

second_coef = (-205.0 / 72.0, 8.0 / 5.0, -1.0 / 5.0, 8.0 / 315.0, -1.0 / 560.0)
first_coef = (4.0 / 5.0, -1.0 / 5.0, 4.0 / 105.0, -1.0 / 280.0)

AXES = ("shot", "aper")
STEPS = 4
TX = 4
AY = 32
AZ = 256
HALF = 128
HALF_Y = AY // 2
F32 = jnp.float32
VMEM = pl.BlockSpec(memory_space=pltpu.VMEM)
SMEM = pl.BlockSpec(memory_space=pltpu.SMEM)


def device(x, core, y, z):
    return ((x % 2) * 2 + core) * 32 + ((z % 4) * 4 + y % 4) * 2 + x // 2


def everyone():
    return [(x, c, y, z) for x in range(4) for c in range(2) for y in range(4) for z in range(4)]


def flipped(y, z):
    return 3 - y if z % 2 else y


def on_path(j):
    j = j % 16
    return flipped(j % 4, j // 4), j // 4


def path_place(y, z):
    return 4 * z + flipped(y, z)


def pairs_of(rule):
    pairs = [(device(*d), device(*rule(*d))) for d in everyone()]
    assert sorted(t for _, t in pairs) == list(range(128))
    assert all(s != t for s, t in pairs)
    return pairs


def send(value, pairs):
    return lax.ppermute(value, AXES, pairs)


def other_core():
    return pairs_of(lambda x, c, y, z: (x, 1 - c, y, z))


def along_path(by):
    def rule(x, c, y, z):
        return (x, c) + on_path(path_place(y, z) + by)

    return pairs_of(rule)


def state_first():
    def rule(x, c, y, z):
        hi = x // 2
        t = {(0, 0): (0, 1), (0, 1): (1, 1), (1, 0): (0, 0), (1, 1): (1, 0)}[(hi, c)]
        return (2 * t[0] + x % 2, t[1], flipped(y, z), z)

    return pairs_of(rule)


def state_second():
    def rule(x, c, y, z):
        hi = x // 2
        if hi == c:
            return (x, c, 3 - y, z)
        return (2 * (1 - hi) + x % 2, 1 - c, flipped(y, z), z)

    return pairs_of(rule)


def across(by):
    def rule(x, c, y, z):
        if by == 0:
            return (x, c, 3 - y, z)
        return ((x + by) % 4, c, flipped(y, z), z)

    return pairs_of(rule)


def z_plus(pair, d, lane):
    a, b = pair
    ra, rb = pltpu.roll(a, HALF - d, 1), pltpu.roll(b, HALF - d, 1)
    keep = lane < HALF - d
    return jnp.where(keep, ra, rb), jnp.where(keep, rb, 0.0)


def z_minus(pair, d, lane):
    a, b = pair
    ra, rb = pltpu.roll(a, d, 1), pltpu.roll(b, d, 1)
    keep = lane >= d
    return jnp.where(keep, ra, 0.0), jnp.where(keep, rb, ra)


def second_z(pair, lane):
    out = [second_coef[0] * v for v in pair]
    for d in range(1, 5):
        up, down = z_plus(pair, d, lane), z_minus(pair, d, lane)
        out = [o + second_coef[d] * (u + w) for o, u, w in zip(out, up, down)]
    return out


def first_z(pair, lane):
    out = None
    for d in range(1, 5):
        up, down = z_plus(pair, d, lane), z_minus(pair, d, lane)
        term = [first_coef[d - 1] * (u - w) for u, w in zip(up, down)]
        out = term if out is None else [o + t for o, t in zip(out, term)]
    return out


def second_y(pair, row):
    out = []
    for f in pair:
        acc = second_coef[0] * f
        for d in range(1, 5):
            up = jnp.where(row < AY - d, pltpu.roll(f, AY - d, 0), 0.0)
            down = jnp.where(row >= d, pltpu.roll(f, d, 0), 0.0)
            acc = acc + second_coef[d] * (up + down)
        out.append(acc)
    return out


def x_parts(rows):
    second, first = [], []
    for s in range(2):
        acc = second_coef[0] * rows[4][s]
        der = None
        for d in range(1, 5):
            acc = acc + second_coef[d] * (rows[4 + d][s] + rows[4 - d][s])
            term = first_coef[d - 1] * (rows[4 + d][s] - rows[4 - d][s])
            der = term if der is None else der + term
        second.append(acc)
        first.append(der)
    return second, first


CORE, X_HI, BLOCK, ROLE, FREE, STAYS, PARITY, SOURCE, OWNER, SIDE = 0, 1, 2, 3, 4, 5, 8, 12, 16, 20


def plan_values(ids, offsets):
    shot, aper = ids[0], ids[1]
    core, x_lo, x_hi = shot & 1, shot >> 1, aper & 1
    x = 2 * x_hi + x_lo
    z, y = aper >> 3, (aper >> 1) & 3
    even_z = 1 - (z & 1)
    block = 4 * z + jnp.where(even_z == 1, y, 3 - y)
    column = 2 * (4 * z + y) + x_hi
    turns = [offsets[g] & 31 for g in range(4)]

    def of(values, g):
        return jnp.where(g < 2, jnp.where(g == 0, values[0], values[1]), jnp.where(g == 2, values[2], values[3]))

    def row_of(g, col):
        return (of(offsets, g) >> 5) + (col < of(turns, g)).astype(jnp.int32)

    def group_of(x):
        return 2 * (x & 1) + (x >> 1)

    group = group_of(x)
    turn = of(turns, group)
    free = [jnp.where((t == 0) | (t == 31), 0, t) for t in turns]
    out = {
        CORE: core,
        X_HI: x_hi,
        BLOCK: block,
        ROLE: jnp.where(turn == 0, 0, jnp.where(turn == 31, 1, 2)),
        FREE: jnp.maximum(jnp.maximum(free[0], free[1]), jnp.maximum(free[2], free[3])),
        STAYS: (x_hi == core).astype(jnp.int32) * even_z,
        STAYS + 1: even_z,
    }
    for by in range(4):
        to, came = (x + by) & 3, (x - by) & 3
        out[PARITY + by] = row_of(group_of(to), column) & 1
        out[OWNER + by] = row_of(group_of(came), column) - 2 * x_lo
        out[SIDE + by] = to >> 1
    for h in range(2):
        out[SOURCE + h] = (x - (2 * h + (row_of(group, 2 * block + h) >> 1))) & 3
    return out


def plan_kernel(ids, offsets, velocity, epsilon, delta, angle, plan, other):
    values = plan_values(ids, [offsets[g] for g in range(4)])
    for k, v in values.items():
        plan[k] = v
    first = values[CORE] == 0
    for i in range(TX):
        other[0, i] = jnp.where(first, delta[i], velocity[i])
        other[1, i] = jnp.where(first, angle[i], epsilon[i])


def state_kernel(plan, fwd_now, adj_now, fwd_before, adj_before, one_now, two_now, one_before, two_before):
    low = plan[X_HI] == 0
    for fwd, adj, one, two in (
        (fwd_now, adj_now, one_now, two_now),
        (fwd_before, adj_before, one_before, two_before),
    ):
        for p in range(2):
            for i in range(TX):
                f, a = fwd[p, i], adj[p, i]
                one[p, i] = jnp.where(low, a, f)
                two[p, i] = jnp.where(low, f, a)


def block_kernel(plan, kept, one, two, lo, hi):
    first, stays = plan[CORE] == 0, plan[STAYS] == 1
    for p in range(2):
        for i in range(TX):
            a, b = one[p, i], jnp.where(stays, kept[p, i], two[p, i])
            lo[p, i] = jnp.where(first, b, a)
            hi[p, i] = jnp.where(first, a, b)


def rows_kernel(plan, velocity, epsilon, delta, angle, came, *outs):
    first = plan[CORE] == 0
    mine = [plan[PARITY + by] == plan[CORE] for by in range(4)]
    for i in range(TX):
        own = (jnp.where(first, velocity[i], delta[i]), jnp.where(first, epsilon[i], angle[i]))
        for f in range(2):
            theirs = came[f, i]
            for by in range(4):
                outs[by][f, i] = jnp.where(mine[by], own[f], theirs)


def tiles_kernel(plan, kept, got_0, got_1, got_2, got_3, out):
    even = plan[STAYS + 1] == 1
    source = [plan[SOURCE + h] for h in range(2)]
    for f in range(2):
        for i in range(TX):
            rows = [jnp.where(even, kept[f, i], got_0[f, i]), got_1[f, i], got_2[f, i], got_3[f, i]]
            for h in range(2):
                a = jnp.where(source[h] == 0, rows[0], rows[1])
                b = jnp.where(source[h] == 2, rows[2], rows[3])
                out[h, f, i] = jnp.where(source[h] < 2, a, b)


def turned_kernel(plan, tiles, low, free_lo, free_hi, out):
    role = plan[ROLE]
    for f in range(2):
        for i in range(TX):
            lo, hi = tiles[0, f, i], tiles[1, f, i]
            a = jnp.where(role == 0, lo, jnp.where(role == 1, low[f, i], free_lo[f, i]))
            b = jnp.where(role == 0, hi, jnp.where(role == 1, lo, free_hi[f, i]))
            out[0, f, i] = a
            out[1, f, i] = b


def fill_rows(plan, lo, hi, low, high, ext):
    first, last = plan[BLOCK] == 0, plan[BLOCK] == 15
    for p in range(2):
        for i in range(TX):
            ext[p, i] = jnp.where(first, 0.0, low[p, i])
            ext[p, TX + i] = lo[p, i]
            ext[p, 2 * TX + i] = hi[p, i]
            ext[p, 3 * TX + i] = jnp.where(last, 0.0, high[p, i])


def step_kernel(plan, lo, hi, lo_b, hi_b, low, high, coef, inj, new_lo, new_hi, *rest):
    packed, ext = (rest[0], rest[1]) if len(rest) == 2 else (None, rest[0])
    fill_rows(plan, lo, hi, low, high, ext)
    for t, (back, mid, out) in enumerate(((lo_b, lo, new_lo), (hi_b, hi, new_hi))):

        def tile(i, carry, t=t, back=back, mid=mid, out=out):
            def emit(h, new_p, new_q):
                out[0, i, :, h] = new_p
                out[1, i, :, h] = new_q
                if packed is not None:
                    packed[0, t, i, :, h] = mid[0, i, :, h]
                    packed[1, t, i, :, h] = new_p

            one_row(ext, t * TX + i, lambda p, h: back[p, i, :, h], coef, inj, emit)
            return carry

        lax.fori_loop(0, TX, tile, 0)


def one_row(ext, i, before, coef, inj, emit):
    lane = lax.broadcasted_iota(jnp.int32, (AY, HALF), 1)
    row = lax.broadcasted_iota(jnp.int32, (AY, HALF), 0)
    halves = (pl.ds(0, HALF), pl.ds(HALF, HALF))
    parts = []
    for p in range(2):
        rows = [[ext[p, i + d, :, h] for h in halves] for d in range(9)]
        curve_x, slope_x = x_parts(rows)
        parts.append((rows[4], curve_x, second_z(rows[4], lane), first_z(slope_x, lane)))
    (mid_p, xp, zp, cp), (mid_q, xq, zq, cq) = parts
    yp = second_y(mid_p, row)
    for s, h in enumerate(halves):
        aniso, coupled, square = coef[0, i, :, h], coef[1, i, :, h], coef[2, i, :, h]
        sine, cosine, double = coef[3, i, :, h], coef[4, i, :, h], coef[5, i, :, h]
        axial_p = sine * xp[s] + cosine * zp[s] + double * cp[s]
        plane_p = xp[s] + yp[s] + zp[s] - axial_p
        axial_q = sine * xq[s] + cosine * zq[s] + double * cq[s]
        add = inj[i, :, h]
        new_p = 2.0 * mid_p[s] - before(0, h) + aniso * plane_p + coupled * axial_q + add
        new_q = 2.0 * mid_q[s] - before(1, h) + coupled * plane_p + square * axial_q + add
        emit(h, new_p, new_q)


def last_kernel(plan, lo, hi, lo_b, hi_b, low, high, coef, inj, other, keep, give, ext, part):
    fill_rows(plan, lo, hi, low, high, ext)
    for t, (back, mid) in enumerate(((lo_b, lo), (hi_b, hi))):

        def tile(i, carry, t=t, back=back, mid=mid):
            def emit(h, new_p, new_q):
                part[t, i, :, h] = new_p * other[0, t, i, :, h] + mid[0, i, :, h] * other[1, t, i, :, h]

            one_row(ext, t * TX + i, lambda p, h: back[p, i, :, h], coef, inj, emit)
            return carry

        lax.fori_loop(0, TX, tile, 0)
    first = plan[CORE] == 0
    for t in range(2):
        for i in range(TX):
            low_y, high_y = part[t, i, :HALF_Y], part[t, i, HALF_Y:]
            keep[t, i] = jnp.where(first, low_y, high_y)
            give[t, i] = jnp.where(first, high_y, low_y)


def total_kernel(keep, came, lo, hi):
    for i in range(TX):
        lo[i] = keep[0, i] + came[0, i]
        hi[i] = keep[1, i] + came[1, i]


def image_kernel(plan, lo, hi, high, free_lo, free_hi, *outs):
    role = plan[ROLE]
    for i in range(TX):
        a, b = lo[i], hi[i]
        new_lo = jnp.where(role == 0, a, jnp.where(role == 1, b, free_lo[i]))
        new_hi = jnp.where(role == 0, b, jnp.where(role == 1, high[i], free_hi[i]))
        for by in range(4):
            outs[by][i] = jnp.where(plan[SIDE + by] == 0, new_lo, new_hi)


def owners_kernel(plan, kept, got_0, got_1, got_2, got_3, keep, give):
    even, core = plan[STAYS + 1] == 1, plan[CORE]
    for i in range(TX):
        parts = [jnp.where(even, kept[i], got_0[i]), got_1[i], got_2[i], got_3[i]]
        for target, out in ((core, keep), (1 - core, give)):
            acc = jnp.zeros_like(parts[0])
            for by in range(4):
                acc = acc + jnp.where(plan[OWNER + by] == target, parts[by], 0.0)
            out[i] = acc


def join_kernel(plan, keep, came, out):
    first = plan[CORE] == 0
    for i in range(TX):
        out[i, :HALF_Y] = jnp.where(first, keep[i], came[i])
        out[i, HALF_Y:] = jnp.where(first, came[i], keep[i])


def inject_kernel(plan, cells, amounts, out):
    x = cells[0:1, :] - 8 * plan[BLOCK]
    here = (x >= 0) & (x < 8)
    spot = jnp.where(here, x * AY + cells[1:2, :], -1)
    depth = cells[2:3, :]
    count = cells.shape[1]
    which = (lax.broadcasted_iota(jnp.int32, (8 * AY, count), 0) == spot).astype(F32)
    level = lax.broadcasted_iota(jnp.int32, (AZ, count), 0) == depth
    for k in range(STEPS):
        values = jnp.where(level, amounts[k : k + 1, :], 0.0)
        flat = lax.dot_general(
            which,
            values,
            (((1,), (1,)), ((), ())),
            precision=lax.Precision.HIGHEST,
            preferred_element_type=F32,
        )
        for i in range(8):
            out[k, i] = flat[i * AY : (i + 1) * AY, :]


def sine_cosine(angle):
    sq = angle * angle
    sine = -1.0 / 39916800.0
    for c in (1.0 / 362880.0, -1.0 / 5040.0, 1.0 / 120.0, -1.0 / 6.0, 1.0):
        sine = sine * sq + c
    cosine = 1.0 / 479001600.0
    for c in (-1.0 / 3628800.0, 1.0 / 40320.0, -1.0 / 720.0, 1.0 / 24.0, -0.5, 1.0):
        cosine = cosine * sq + c
    return sine * angle, cosine


def coef_kernel(plan, own, other, out):
    core = plan[CORE]
    for t in range(2):

        def tile(i, carry, t=t):
            mine = [own[t, f, i] for f in range(2)]
            theirs = [other[t, f, i] for f in range(2)]
            velocity = jnp.where(core == 0, mine[0], theirs[0])
            epsilon = jnp.where(core == 0, mine[1], theirs[1])
            delta = jnp.where(core == 0, theirs[0], mine[0])
            angle = jnp.where(core == 0, theirs[1], mine[1])
            square = velocity * velocity
            sine, cosine = sine_cosine(angle)
            k = t * TX + i
            out[0, k] = square * (1.0 + 2.0 * epsilon)
            out[1, k] = square * jnp.sqrt(1.0 + 2.0 * delta)
            out[2, k] = square
            out[3, k] = sine * sine
            out[4, k] = cosine * cosine
            out[5, k] = 2.0 * sine * cosine
            return carry

        lax.fori_loop(0, TX, tile, 0)


def call(kernel, n_in, outs, scratch=(), n_smem=1):
    return pl.pallas_call(
        kernel,
        out_shape=[jax.ShapeDtypeStruct(s, F32) for s in outs],
        in_specs=[SMEM] * n_smem + [VMEM] * n_in,
        out_specs=[VMEM] * len(outs),
        scratch_shapes=[pltpu.VMEM(s, F32) for s in scratch],
        compiler_params=pltpu.CompilerParams(vmem_limit_bytes=32 * 1024 * 1024),
    )


TILE = (2, TX, AY, AZ)
PART = (TX, HALF_Y, AZ)


def turn_tiles(tiles, r):
    if r in (0, 31):
        return tiles[0], tiles[1]
    if r % 2 == 0:
        moved = moved_along(tiles, -(r // 2))
        return moved[0], moved[1]
    return moved_along(tiles[1], -(r // 2)), moved_along(tiles[0], -((r + 1) // 2))


def turn_image(lo, hi, r):
    if r in (0, 31):
        return lo, hi
    if r % 2 == 0:
        moved = moved_along(jnp.stack([lo, hi]), r // 2)
        return moved[0], moved[1]
    return moved_along(hi, (r + 1) // 2), moved_along(lo, r // 2)


def moved_along(value, by):
    by = by % 16
    if by == 0:
        return value
    if by in (1, 15):
        return moved_along(moved_along(value, 9), by - 9)
    return send(value, along_path(by))


def local(
    velocity,
    thomsen_epsilon,
    thomsen_delta,
    tilt_angle,
    fwd_now,
    fwd_before,
    adj_now,
    adj_before,
    wavelet,
    traces,
    offsets,
    source_cell,
    receiver_cell,
):
    shot, aper = lax.axis_index("shot"), lax.axis_index("aper")
    ids = jnp.stack([shot, aper]).astype(jnp.int32)
    swap, up, down = other_core(), along_path(1), along_path(-1)
    model = (velocity, thomsen_epsilon, thomsen_delta, tilt_angle)

    plan, other = pl.pallas_call(
        plan_kernel,
        out_shape=[jax.ShapeDtypeStruct((32,), jnp.int32), jax.ShapeDtypeStruct(TILE, F32)],
        in_specs=[SMEM] * 2 + [VMEM] * 4,
        out_specs=[SMEM, VMEM],
        compiler_params=pltpu.CompilerParams(vmem_limit_bytes=32 * 1024 * 1024),
    )(ids, offsets, *model)

    came = send(other, swap)
    one, two, one_b, two_b = call(state_kernel, 4, [TILE] * 4)(
        plan, fwd_now[0], adj_now[0], fwd_before[0], adj_before[0]
    )
    got_one, got_two = send(one, state_first()), send(two, state_second())
    rows = call(rows_kernel, 5, [TILE] * 4)(plan, *model, came)
    got = [send(rows[by], across(by)) for by in range(4)]
    tiles = call(tiles_kernel, 5, [(2,) + TILE])(plan, rows[0], *got)[0]

    lo, hi = call(block_kernel, 3, [TILE] * 2)(plan, two, got_one, got_two)
    got_one, got_two = send(one_b, state_first()), send(two_b, state_second())
    lo_b, hi_b = call(block_kernel, 3, [TILE] * 2)(plan, two_b, got_one, got_two)

    low = send(tiles[1], up)
    free_lo, free_hi = lax.switch(
        plan[FREE], [lambda v, r=r: turn_tiles(v, r) for r in range(32)], tiles
    )
    turned = call(turned_kernel, 4, [(2,) + TILE])(plan, tiles, low, free_lo, free_hi)[0]
    coef = call(coef_kernel, 2, [(6, 8, AY, AZ)])(plan, turned, send(turned, swap))[0]

    n_rec = receiver_cell.shape[1]
    group = 2 * (shot // 2) + aper % 2
    rec = receiver_cell[group].T
    at_first = jnp.arange(n_rec)[None, :] == 0
    src = jnp.where(at_first, source_cell[group][:, None], -1000)
    pulse = jnp.where(at_first, wavelet[group][:, None], 0.0)
    forward = shot % 2 == 0
    cells = jnp.where(forward, src, rec)
    amounts = jnp.where(forward, pulse, traces[group])
    inj = call(inject_kernel, 2, [(STEPS, 8, AY, AZ)])(plan, cells, amounts)[0]

    shared = None
    for k in range(STEPS - 1):
        low, high = send(hi, up), send(lo, down)
        outs = [TILE, TILE] + ([(2, 2, TX, AY, AZ)] if k == 1 else [])
        new = call(step_kernel, 8, outs, [(2, 4 * TX, AY, AZ)])(
            plan, lo, hi, lo_b, hi_b, low, high, coef, inj[k]
        )
        if k == 1:
            shared = send(new[2], swap)
        lo_b, hi_b, lo, hi = lo, hi, new[0], new[1]
    low, high = send(hi, up), send(lo, down)
    keep, give = call(
        last_kernel, 9, [(2,) + PART] * 2, [(2, 4 * TX, AY, AZ), (2, TX, AY, AZ)]
    )(plan, lo, hi, lo_b, hi_b, low, high, coef, inj[STEPS - 1], shared)

    lo, hi = call(total_kernel, 2, [PART] * 2, n_smem=0)(keep, send(give, swap))
    high = send(lo, down)
    free_lo, free_hi = lax.switch(
        plan[FREE], [lambda a, b, r=r: turn_image(a, b, r) for r in range(32)], lo, hi
    )
    parts = call(image_kernel, 5, [PART] * 4)(plan, lo, hi, high, free_lo, free_hi)
    got = [send(parts[by], across(by)) for by in range(4)]
    keep, give = call(owners_kernel, 5, [PART] * 2)(plan, parts[0], *got)
    return call(join_kernel, 2, [(TX, AY, AZ)])(plan, keep, send(give, swap))[0]


def solution(mesh):
    model = P(("shot", "aper"), None, None)
    field = P("shot", None, "aper", None, None)
    return jax.shard_map(
        local,
        mesh=mesh,
        in_specs=(model,) * 4 + (field,) * 4 + (P(),) * 5,
        out_specs=model,
        check_vma=False,
    )
```

```python
import jax
import jax.numpy as jnp
from jax import lax
from jax.experimental import pallas as pl
from jax.experimental.pallas import tpu as pltpu
from jax.sharding import PartitionSpec as P

second_coef = (-205.0 / 72.0, 8.0 / 5.0, -1.0 / 5.0, 8.0 / 315.0, -1.0 / 560.0)
first_coef = (4.0 / 5.0, -1.0 / 5.0, 4.0 / 105.0, -1.0 / 280.0)

AXES = ("shot", "aper")
STEPS = 4
TX = 4
AY = 32
AZ = 256
HALF = 128
HALF_Y = AY // 2
F32 = jnp.float32
VMEM = pl.BlockSpec(memory_space=pltpu.VMEM)
SMEM = pl.BlockSpec(memory_space=pltpu.SMEM)


def device(x, core, y, z):
    return ((x % 2) * 2 + core) * 32 + ((z % 4) * 4 + y % 4) * 2 + x // 2


def everyone():
    return [(x, c, y, z) for x in range(4) for c in range(2) for y in range(4) for z in range(4)]


def flipped(y, z):
    return 3 - y if z % 2 else y


def on_path(j):
    j = j % 16
    return flipped(j % 4, j // 4), j // 4


def path_place(y, z):
    return 4 * z + flipped(y, z)


def pairs_of(rule):
    pairs = [(device(*d), device(*rule(*d))) for d in everyone()]
    assert sorted(t for _, t in pairs) == list(range(128))
    assert all(s != t for s, t in pairs)
    return pairs


def send(value, pairs):
    return lax.ppermute(value, AXES, pairs)


def other_core():
    return pairs_of(lambda x, c, y, z: (x, 1 - c, y, z))


def along_path(by):
    def rule(x, c, y, z):
        return (x, c) + on_path(path_place(y, z) + by)

    return pairs_of(rule)


def state_first():
    def rule(x, c, y, z):
        hi = x // 2
        t = {(0, 0): (0, 1), (0, 1): (1, 1), (1, 0): (0, 0), (1, 1): (1, 0)}[(hi, c)]
        return (2 * t[0] + x % 2, t[1], flipped(y, z), z)

    return pairs_of(rule)


def state_second():
    def rule(x, c, y, z):
        hi = x // 2
        if hi == c:
            return (x, c, 3 - y, z)
        return (2 * (1 - hi) + x % 2, 1 - c, flipped(y, z), z)

    return pairs_of(rule)


def across(by):
    def rule(x, c, y, z):
        if by == 0:
            return (x, c, 3 - y, z)
        return ((x + by) % 4, c, flipped(y, z), z)

    return pairs_of(rule)


def rolled(by_low, by_high):
    def rule(x, c, y, z):
        j = (4 * z + y + (by_high if x // 2 else by_low)) % 16
        return (x, c, j % 4, j // 4)

    return pairs_of(rule)


def z_plus(pair, d, lane):
    a, b = pair
    ra, rb = pltpu.roll(a, HALF - d, 1), pltpu.roll(b, HALF - d, 1)
    keep = lane < HALF - d
    return jnp.where(keep, ra, rb), jnp.where(keep, rb, 0.0)


def z_minus(pair, d, lane):
    a, b = pair
    ra, rb = pltpu.roll(a, d, 1), pltpu.roll(b, d, 1)
    keep = lane >= d
    return jnp.where(keep, ra, 0.0), jnp.where(keep, rb, ra)


def second_z(pair, lane):
    out = [second_coef[0] * v for v in pair]
    for d in range(1, 5):
        up, down = z_plus(pair, d, lane), z_minus(pair, d, lane)
        out = [o + second_coef[d] * (u + w) for o, u, w in zip(out, up, down)]
    return out


def first_z(pair, lane):
    out = None
    for d in range(1, 5):
        up, down = z_plus(pair, d, lane), z_minus(pair, d, lane)
        term = [first_coef[d - 1] * (u - w) for u, w in zip(up, down)]
        out = term if out is None else [o + t for o, t in zip(out, term)]
    return out


def second_y(pair, row):
    out = []
    for f in pair:
        acc = second_coef[0] * f
        for d in range(1, 5):
            up = jnp.where(row < AY - d, pltpu.roll(f, AY - d, 0), 0.0)
            down = jnp.where(row >= d, pltpu.roll(f, d, 0), 0.0)
            acc = acc + second_coef[d] * (up + down)
        out.append(acc)
    return out


def x_parts(rows):
    second, first = [], []
    for s in range(2):
        acc = second_coef[0] * rows[4][s]
        der = None
        for d in range(1, 5):
            acc = acc + second_coef[d] * (rows[4 + d][s] + rows[4 - d][s])
            term = first_coef[d - 1] * (rows[4 + d][s] - rows[4 - d][s])
            der = term if der is None else der + term
        second.append(acc)
        first.append(der)
    return second, first


CORE, X_HI, BLOCK, FREE, STAYS, EVEN, KEEP, PARITY_LAST, PARITY_FREE = range(9)
PARITY, ROLE_TO, SIDE, SOURCE, OWNER, ROLE_FROM = 12, 16, 20, 24, 28, 32


def plan_values(ids, offsets):
    shot, aper = ids[0], ids[1]
    core, x_lo, x_hi = shot & 1, shot >> 1, aper & 1
    x = 2 * x_hi + x_lo
    z, y = aper >> 3, (aper >> 1) & 3
    even_z = 1 - (z & 1)
    block = 4 * z + jnp.where(even_z == 1, y, 3 - y)
    straight = 4 * z + y
    turns = [o & 31 for o in offsets]

    def of(values, g):
        return jnp.where(g < 2, jnp.where(g == 0, values[0], values[1]), jnp.where(g == 2, values[2], values[3]))

    def first(flags):
        return jnp.where(flags[0], 0, jnp.where(flags[1], 1, jnp.where(flags[2], 2, 3)))

    def group_of(x):
        return 2 * (x & 1) + (x >> 1)

    last = first([t == 31 for t in turns])
    free = 6 - first([o == 0 for o in offsets]) - first([o == 96 for o in offsets]) - last
    free_turn = of(turns, free)

    def role_of(g):
        return jnp.where(g == last, 1, jnp.where((g == free) & (free_turn != 0), 2, 0))

    def row_of(g):
        o = of(offsets, g)
        return (o + 2 * straight + (x_hi ^ (o & 1))) >> 5

    def parity_before(g):
        o = of(offsets, g)
        return ((o >> 5) + (2 * straight + x_hi < (o & 31)).astype(jnp.int32)) & 1

    group = group_of(x)
    offset = of(offsets, group)
    out = {
        CORE: core,
        X_HI: x_hi,
        BLOCK: block,
        FREE: free_turn,
        STAYS: (x_hi == core).astype(jnp.int32) * even_z,
        EVEN: even_z,
        KEEP: jnp.where(free_turn == 31, 1 - x_hi, jnp.where(free_turn == 1, x_hi, 0)),
        PARITY_LAST: parity_before(last),
        PARITY_FREE: parity_before(free),
    }
    for by in range(4):
        to, came = group_of((x + by) & 3), group_of((x - by) & 3)
        out[PARITY + by] = parity_before(to)
        out[ROLE_TO + by] = role_of(to)
        out[SIDE + by] = (((x + by) & 3) >> 1) ^ (offset & 1)
        out[OWNER + by] = row_of(came) - 2 * x_lo
        out[ROLE_FROM + by] = role_of(came)
    for h in range(2):
        row = (offset + 2 * block + h) >> 5
        out[SOURCE + h] = (x - (2 * (h ^ (offset & 1)) + (row >> 1))) & 3
    return out


def fetch(which, choices, sems):
    for k, (a, b, out) in enumerate(choices):

        @pl.when(which)
        def _(a=a, out=out, k=k):
            pltpu.make_async_copy(a, out, sems.at[k]).start()

        @pl.when(jnp.logical_not(which))
        def _(b=b, out=out, k=k):
            pltpu.make_async_copy(b, out, sems.at[k]).start()

    for k, (a, _, out) in enumerate(choices):
        pltpu.make_async_copy(a, out, sems.at[k]).wait()


def plan_kernel(ids, offsets, velocity, epsilon, delta, angle, plan, own, other, sems):
    values = plan_values(ids, [offsets[g] for g in range(4)])
    for k, v in values.items():
        plan[k] = v
    fetch(
        values[CORE] == 0,
        (
            (velocity, delta, own.at[0]),
            (epsilon, angle, own.at[1]),
            (delta, velocity, other.at[0]),
            (angle, epsilon, other.at[1]),
        ),
        sems,
    )


def state_kernel(plan, fwd_now, adj_now, fwd_before, adj_before, one, two, sems):
    fetch(
        plan[X_HI] == 0,
        (
            (adj_now.at[0], fwd_now.at[0], one.at[0]),
            (fwd_now.at[0], adj_now.at[0], two.at[0]),
            (adj_before.at[0], fwd_before.at[0], one.at[1]),
            (fwd_before.at[0], adj_before.at[0], two.at[1]),
        ),
        sems,
    )


def rows_kernel(plan, own, came, last, free):
    mine_last, mine_free = plan[PARITY_LAST] == plan[CORE], plan[PARITY_FREE] == plan[CORE]
    for f in range(2):
        for i in range(TX):
            a, b = own[f, i], came[f, i]
            last[f, i] = jnp.where(mine_last, a, b)
            free[f, i] = jnp.where(mine_free, a, b)


def send_kernel(plan, own, came, last, last_came, free, free_came, kept, one, two, *outs):
    first, stays = plan[CORE] == 0, plan[STAYS] == 1
    for t in range(2):
        lo, hi = outs[4 + 2 * t : 6 + 2 * t]
        for p in range(2):
            for i in range(TX):
                a, b = one[t, p, i], jnp.where(stays, kept[t, p, i], two[t, p, i])
                lo[p, i] = jnp.where(first, b, a)
                hi[p, i] = jnp.where(first, a, b)
    high = plan[X_HI] == 1
    keep = plan[KEEP] == 1
    mine = [plan[PARITY + by] == plan[CORE] for by in range(4)]
    role = [plan[ROLE_TO + by] for by in range(4)]
    for f in range(2):
        for i in range(TX):
            a, b = own[f, i], came[f, i]
            turned_last = jnp.where(high, last_came[f, i], last[f, i])
            turned_free = jnp.where(keep, free[f, i], free_came[f, i])
            for by in range(4):
                straight = jnp.where(mine[by], a, b)
                turned = jnp.where(role[by] == 1, turned_last, turned_free)
                outs[by][f, i] = jnp.where(role[by] == 0, straight, turned)


def tiles_kernel(plan, kept, got_0, got_1, got_2, got_3, out):
    even = plan[EVEN] == 1
    source = [plan[SOURCE + h] for h in range(2)]
    for f in range(2):
        for i in range(TX):
            rows = [jnp.where(even, kept[f, i], got_0[f, i]), got_1[f, i], got_2[f, i], got_3[f, i]]
            for h in range(2):
                a = jnp.where(source[h] == 0, rows[0], rows[1])
                b = jnp.where(source[h] == 2, rows[2], rows[3])
                out[h, f, i] = jnp.where(source[h] < 2, a, b)


def fill_rows(plan, lo, hi, low, high, ext):
    first, last = plan[BLOCK] == 0, plan[BLOCK] == 15
    for p in range(2):
        for i in range(TX):
            ext[p, i] = jnp.where(first, 0.0, low[p, i])
            ext[p, TX + i] = lo[p, i]
            ext[p, 2 * TX + i] = hi[p, i]
            ext[p, 3 * TX + i] = jnp.where(last, 0.0, high[p, i])


def step_kernel(plan, lo, hi, lo_b, hi_b, low, high, coef, inj, new_lo, new_hi, *rest):
    packed, ext = (rest[0], rest[1]) if len(rest) == 2 else (None, rest[0])
    fill_rows(plan, lo, hi, low, high, ext)
    for t, (back, mid, out) in enumerate(((lo_b, lo, new_lo), (hi_b, hi, new_hi))):

        def tile(i, carry, t=t, back=back, mid=mid, out=out):
            def emit(h, new_p, new_q):
                out[0, i, :, h] = new_p
                out[1, i, :, h] = new_q
                if packed is not None:
                    packed[0, t, i, :, h] = mid[0, i, :, h]
                    packed[1, t, i, :, h] = new_p

            one_row(ext, t * TX + i, lambda p, h: back[p, i, :, h], coef, inj, emit)
            return carry

        lax.fori_loop(0, TX, tile, 0)


def one_row(ext, i, before, coef, inj, emit):
    lane = lax.broadcasted_iota(jnp.int32, (AY, HALF), 1)
    row = lax.broadcasted_iota(jnp.int32, (AY, HALF), 0)
    halves = (pl.ds(0, HALF), pl.ds(HALF, HALF))
    parts = []
    for p in range(2):
        rows = [[ext[p, i + d, :, h] for h in halves] for d in range(9)]
        curve_x, slope_x = x_parts(rows)
        parts.append((rows[4], curve_x, second_z(rows[4], lane), first_z(slope_x, lane)))
    (mid_p, xp, zp, cp), (mid_q, xq, zq, cq) = parts
    yp = second_y(mid_p, row)
    for s, h in enumerate(halves):
        aniso, coupled, square = coef[0, i, :, h], coef[1, i, :, h], coef[2, i, :, h]
        sine, cosine, double = coef[3, i, :, h], coef[4, i, :, h], coef[5, i, :, h]
        axial_p = sine * xp[s] + cosine * zp[s] + double * cp[s]
        plane_p = xp[s] + yp[s] + zp[s] - axial_p
        axial_q = sine * xq[s] + cosine * zq[s] + double * cq[s]
        add = inj[i, :, h]
        new_p = 2.0 * mid_p[s] - before(0, h) + aniso * plane_p + coupled * axial_q + add
        new_q = 2.0 * mid_q[s] - before(1, h) + coupled * plane_p + square * axial_q + add
        emit(h, new_p, new_q)


def last_kernel(plan, lo, hi, lo_b, hi_b, low, high, coef, inj, other, keep, give, ext, part):
    fill_rows(plan, lo, hi, low, high, ext)
    for t, (back, mid) in enumerate(((lo_b, lo), (hi_b, hi))):

        def tile(i, carry, t=t, back=back, mid=mid):
            def emit(h, new_p, new_q):
                part[t, i, :, h] = new_p * other[0, t, i, :, h] + mid[0, i, :, h] * other[1, t, i, :, h]

            one_row(ext, t * TX + i, lambda p, h: back[p, i, :, h], coef, inj, emit)
            return carry

        lax.fori_loop(0, TX, tile, 0)
    first = plan[CORE] == 0
    for t in range(2):
        for i in range(TX):
            low_y, high_y = part[t, i, :HALF_Y], part[t, i, HALF_Y:]
            keep[t, i] = jnp.where(first, low_y, high_y)
            give[t, i] = jnp.where(first, high_y, low_y)


def total_kernel(plan, keep, came, *outs):
    for i in range(TX):
        lo = keep[0, i] + came[0, i]
        hi = keep[1, i] + came[1, i]
        for by in range(4):
            outs[by][i] = jnp.where(plan[SIDE + by] == 0, lo, hi)


def owners_kernel(plan, kept, got_0, got_1, got_2, got_3, straight, last, free):
    even = plan[EVEN] == 1
    for i in range(TX):
        parts = [jnp.where(even, kept[i], got_0[i]), got_1[i], got_2[i], got_3[i]]
        for k, out in enumerate((straight, last, free)):
            for core in range(2):
                acc = jnp.zeros_like(parts[0])
                for by in range(4):
                    ours = (plan[OWNER + by] == core) & (plan[ROLE_FROM + by] == k)
                    acc = acc + jnp.where(ours, parts[by], 0.0)
                out[core, i] = acc


def image_kernel(plan, straight, last, last_came, free_low, free_high, keep, give):
    high, first = plan[X_HI] == 1, plan[CORE] == 0
    for i in range(TX):
        sums = []
        for core in range(2):
            turned = jnp.where(high, last_came[core, i], last[core, i])
            free = jnp.where(high, free_high[core, i], free_low[core, i])
            sums.append(straight[core, i] + turned + free)
        keep[i] = jnp.where(first, sums[0], sums[1])
        give[i] = jnp.where(first, sums[1], sums[0])


def join_kernel(plan, keep, came, out):
    first = plan[CORE] == 0
    for i in range(TX):
        out[i, :HALF_Y] = jnp.where(first, keep[i], came[i])
        out[i, HALF_Y:] = jnp.where(first, came[i], keep[i])


def inject_kernel(plan, cells, amounts, out):
    x = cells[0:1, :] - 8 * plan[BLOCK]
    here = (x >= 0) & (x < 8)
    spot = jnp.where(here, x * AY + cells[1:2, :], -1)
    depth = cells[2:3, :]
    count = cells.shape[1]
    which = (lax.broadcasted_iota(jnp.int32, (8 * AY, count), 0) == spot).astype(F32)
    level = lax.broadcasted_iota(jnp.int32, (AZ, count), 0) == depth
    for k in range(STEPS):
        values = jnp.where(level, amounts[k : k + 1, :], 0.0)
        flat = lax.dot_general(
            which,
            values,
            (((1,), (1,)), ((), ())),
            precision=lax.Precision.HIGHEST,
            preferred_element_type=F32,
        )
        for i in range(8):
            out[k, i] = flat[i * AY : (i + 1) * AY, :]


def sine_cosine(angle):
    sq = angle * angle
    sine = -1.0 / 39916800.0
    for c in (1.0 / 362880.0, -1.0 / 5040.0, 1.0 / 120.0, -1.0 / 6.0, 1.0):
        sine = sine * sq + c
    cosine = 1.0 / 479001600.0
    for c in (-1.0 / 3628800.0, 1.0 / 40320.0, -1.0 / 720.0, 1.0 / 24.0, -0.5, 1.0):
        cosine = cosine * sq + c
    return sine * angle, cosine


def coef_kernel(plan, own, other, out):
    core = plan[CORE]
    for t in range(2):

        def tile(i, carry, t=t):
            mine = [own[t, f, i] for f in range(2)]
            theirs = [other[t, f, i] for f in range(2)]
            velocity = jnp.where(core == 0, mine[0], theirs[0])
            epsilon = jnp.where(core == 0, mine[1], theirs[1])
            delta = jnp.where(core == 0, theirs[0], mine[0])
            angle = jnp.where(core == 0, theirs[1], mine[1])
            square = velocity * velocity
            sine, cosine = sine_cosine(angle)
            k = t * TX + i
            out[0, k] = square * (1.0 + 2.0 * epsilon)
            out[1, k] = square * jnp.sqrt(1.0 + 2.0 * delta)
            out[2, k] = square
            out[3, k] = sine * sine
            out[4, k] = cosine * cosine
            out[5, k] = 2.0 * sine * cosine
            return carry

        lax.fori_loop(0, TX, tile, 0)


ANY = pl.BlockSpec(memory_space=pl.ANY)
LIMIT = pltpu.CompilerParams(vmem_limit_bytes=32 * 1024 * 1024)


def call(kernel, n_in, outs, scratch=()):
    return pl.pallas_call(
        kernel,
        out_shape=[jax.ShapeDtypeStruct(s, F32) for s in outs],
        in_specs=[SMEM] + [VMEM] * n_in,
        out_specs=[VMEM] * len(outs),
        scratch_shapes=[pltpu.VMEM(s, F32) for s in scratch],
        compiler_params=LIMIT,
    )


TILE = (2, TX, AY, AZ)
PART = (TX, HALF_Y, AZ)


def roll(value, by, avoid):
    by = by % 16
    if by == 0:
        return value
    if by == avoid:
        return roll(roll(value, 8, avoid), by - 8, avoid)
    return send(value, rolled(by, by))


def turn_model(value, x_hi, r):
    low, high = -((r + 1) // 2), -(r // 2)
    if r in (0, 1, 31) or r % 2 == 0:
        return roll(value, high if r != 1 else low, 1)
    if r in (3, 5, 27, 29):
        return jnp.where(x_hi == 1, roll(value, high, 1), roll(value, low, 1))
    return send(value, rolled(low, high))


def turn_image(value, r):
    low = roll(value, (r + 1) // 2, 15)
    return low, low if r % 2 == 0 else roll(value, r // 2, 15)


def local(
    velocity,
    thomsen_epsilon,
    thomsen_delta,
    tilt_angle,
    fwd_now,
    fwd_before,
    adj_now,
    adj_before,
    wavelet,
    traces,
    offsets,
    source_cell,
    receiver_cell,
):
    shot, aper = lax.axis_index("shot"), lax.axis_index("aper")
    ids = jnp.stack([shot, aper]).astype(jnp.int32)
    swap, up, down = other_core(), along_path(1), along_path(-1)

    plan, own, other = pl.pallas_call(
        plan_kernel,
        out_shape=[jax.ShapeDtypeStruct((40,), jnp.int32)] + [jax.ShapeDtypeStruct(TILE, F32)] * 2,
        in_specs=[SMEM] * 2 + [ANY] * 4,
        out_specs=[SMEM, VMEM, VMEM],
        scratch_shapes=[pltpu.SemaphoreType.DMA((4,))],
        compiler_params=LIMIT,
    )(ids, offsets, velocity, thomsen_epsilon, thomsen_delta, tilt_angle)
    came = send(other, swap)
    one, two = pl.pallas_call(
        state_kernel,
        out_shape=[jax.ShapeDtypeStruct((2,) + TILE, F32)] * 2,
        in_specs=[SMEM] + [ANY] * 4,
        out_specs=[VMEM] * 2,
        scratch_shapes=[pltpu.SemaphoreType.DMA((4,))],
        compiler_params=LIMIT,
    )(plan, fwd_now, adj_now, fwd_before, adj_before)
    got_one, got_two = send(one, state_first()), send(two, state_second())

    last, free = call(rows_kernel, 2, [TILE] * 2)(plan, own, came)
    last_came = send(last, rolled(1, 1))
    free_came = lax.switch(
        plan[FREE], [lambda v, r=r: turn_model(v, aper % 2, r) for r in range(32)], free
    )
    *rows, lo, hi, lo_b, hi_b = call(send_kernel, 9, [TILE] * 8)(
        plan, own, came, last, last_came, free, free_came, two, got_one, got_two
    )
    got = [send(rows[by], across(by)) for by in range(4)]
    tiles = call(tiles_kernel, 5, [(2,) + TILE])(plan, rows[0], *got)[0]
    coef = call(coef_kernel, 2, [(6, 8, AY, AZ)])(plan, tiles, send(tiles, swap))[0]

    n_rec = receiver_cell.shape[1]
    group = 2 * (shot // 2) + aper % 2
    rec = receiver_cell[group].T
    at_first = jnp.arange(n_rec)[None, :] == 0
    src = jnp.where(at_first, source_cell[group][:, None], -1000)
    pulse = jnp.where(at_first, wavelet[group][:, None], 0.0)
    forward = shot % 2 == 0
    cells = jnp.where(forward, src, rec)
    amounts = jnp.where(forward, pulse, traces[group])
    inj = call(inject_kernel, 2, [(STEPS, 8, AY, AZ)])(plan, cells, amounts)[0]

    shared = None
    for k in range(STEPS - 1):
        low, high = send(hi, up), send(lo, down)
        outs = [TILE, TILE] + ([(2, 2, TX, AY, AZ)] if k == 1 else [])
        new = call(step_kernel, 8, outs, [(2, 4 * TX, AY, AZ)])(
            plan, lo, hi, lo_b, hi_b, low, high, coef, inj[k]
        )
        if k == 1:
            shared = send(new[2], swap)
        lo_b, hi_b, lo, hi = lo, hi, new[0], new[1]
    low, high = send(hi, up), send(lo, down)
    keep, give = call(
        last_kernel, 9, [(2,) + PART] * 2, [(2, 4 * TX, AY, AZ), (2, TX, AY, AZ)]
    )(plan, lo, hi, lo_b, hi_b, low, high, coef, inj[STEPS - 1], shared)

    parts = call(total_kernel, 2, [PART] * 4)(plan, keep, send(give, swap))
    got = [send(parts[by], across(by)) for by in range(4)]
    straight, last, free = call(owners_kernel, 5, [(2,) + PART] * 3)(plan, parts[0], *got)
    last_came = send(last, rolled(15, 15))
    free_low, free_high = lax.switch(plan[FREE], [lambda v, r=r: turn_image(v, r) for r in range(32)], free)
    keep, give = call(image_kernel, 5, [PART] * 2)(plan, straight, last, last_came, free_low, free_high)
    return call(join_kernel, 2, [(TX, AY, AZ)])(plan, keep, send(give, swap))[0]


def solution(mesh):
    model = P(("shot", "aper"), None, None)
    field = P("shot", None, "aper", None, None)
    return jax.shard_map(
        local,
        mesh=mesh,
        in_specs=(model,) * 4 + (field,) * 4 + (P(),) * 5,
        out_specs=model,
        check_vma=False,
    )
```

```python
import jax
import jax.numpy as jnp
from jax import lax
from jax.experimental import pallas as pl
from jax.experimental.pallas import tpu as pltpu
from jax.sharding import PartitionSpec as P

second_coef = (-205.0 / 72.0, 8.0 / 5.0, -1.0 / 5.0, 8.0 / 315.0, -1.0 / 560.0)
first_coef = (4.0 / 5.0, -1.0 / 5.0, 4.0 / 105.0, -1.0 / 280.0)

AXES = ("shot", "aper")
STEPS = 4
TX = 4
AY = 32
AZ = 256
HALF = 128
HALF_Y = AY // 2
F32 = jnp.float32
VMEM = pl.BlockSpec(memory_space=pltpu.VMEM)
SMEM = pl.BlockSpec(memory_space=pltpu.SMEM)


def device(x, core, y, z):
    return ((x % 2) * 2 + core) * 32 + ((z % 4) * 4 + y % 4) * 2 + x // 2


def everyone():
    return [(x, c, y, z) for x in range(4) for c in range(2) for y in range(4) for z in range(4)]


def pairs_of(rule):
    pairs = [(device(*d), device(*rule(*d))) for d in everyone()]
    assert sorted(t for _, t in pairs) == list(range(128))
    assert all(s != t for s, t in pairs)
    return pairs


def send(value, pairs):
    return lax.ppermute(value, AXES, pairs)


def other_core():
    return pairs_of(lambda x, c, y, z: (x, 1 - c, y, z))


def state_first():
    def rule(x, c, y, z):
        t = {(0, 0): (0, 1), (0, 1): (1, 1), (1, 0): (0, 0), (1, 1): (1, 0)}[(x // 2, c)]
        return (2 * t[0] + x % 2, t[1], y, z)

    return pairs_of(rule)


def state_second():
    return [
        (device(x, c, y, z), device((x + 2) % 4, 1 - c, y, z)) for x, c, y, z in everyone() if x // 2 != c
    ]


def across(by):
    return pairs_of(lambda x, c, y, z: ((x + by) % 4, c, y, z))


def rolled(by_low, by_high):
    def rule(x, c, y, z):
        j = (4 * z + y + (by_high if x // 2 else by_low)) % 16
        return (x, c, j % 4, j // 4)

    return pairs_of(rule)


def z_plus(pair, d, lane):
    a, b = pair
    ra, rb = pltpu.roll(a, HALF - d, 1), pltpu.roll(b, HALF - d, 1)
    keep = lane < HALF - d
    return jnp.where(keep, ra, rb), jnp.where(keep, rb, 0.0)


def z_minus(pair, d, lane):
    a, b = pair
    ra, rb = pltpu.roll(a, d, 1), pltpu.roll(b, d, 1)
    keep = lane >= d
    return jnp.where(keep, ra, 0.0), jnp.where(keep, rb, ra)


def second_z(pair, lane):
    out = [second_coef[0] * v for v in pair]
    for d in range(1, 5):
        up, down = z_plus(pair, d, lane), z_minus(pair, d, lane)
        out = [o + second_coef[d] * (u + w) for o, u, w in zip(out, up, down)]
    return out


def first_z(pair, lane):
    out = None
    for d in range(1, 5):
        up, down = z_plus(pair, d, lane), z_minus(pair, d, lane)
        term = [first_coef[d - 1] * (u - w) for u, w in zip(up, down)]
        out = term if out is None else [o + t for o, t in zip(out, term)]
    return out


def second_y(pair, row):
    out = []
    for f in pair:
        acc = second_coef[0] * f
        for d in range(1, 5):
            up = jnp.where(row < AY - d, pltpu.roll(f, AY - d, 0), 0.0)
            down = jnp.where(row >= d, pltpu.roll(f, d, 0), 0.0)
            acc = acc + second_coef[d] * (up + down)
        out.append(acc)
    return out


def x_parts(rows):
    second, first = [], []
    for s in range(2):
        acc = second_coef[0] * rows[4][s]
        der = None
        for d in range(1, 5):
            acc = acc + second_coef[d] * (rows[4 + d][s] + rows[4 - d][s])
            term = first_coef[d - 1] * (rows[4 + d][s] - rows[4 - d][s])
            der = term if der is None else der + term
        second.append(acc)
        first.append(der)
    return second, first


CORE, X_HI, BLOCK, STAYS, PARITY_LAST, PARITY_FREE = range(6)
PARITY, ROLE_TO, SIDE, SOURCE, OWNER, ROLE_FROM = 12, 16, 20, 24, 28, 32


def plan_values(ids, offsets):
    shot, aper = ids[0], ids[1]
    core, x_lo, x_hi = shot & 1, shot >> 1, aper & 1
    x = 2 * x_hi + x_lo
    z, y = aper >> 3, (aper >> 1) & 3
    block = 4 * z + y
    turns = [o & 31 for o in offsets]

    def of(values, g):
        return jnp.where(g < 2, jnp.where(g == 0, values[0], values[1]), jnp.where(g == 2, values[2], values[3]))

    def first(flags):
        return jnp.where(flags[0], 0, jnp.where(flags[1], 1, jnp.where(flags[2], 2, 3)))

    def group_of(x):
        return 2 * (x & 1) + (x >> 1)

    last = first([t == 31 for t in turns])
    free = 6 - first([o == 0 for o in offsets]) - first([o == 96 for o in offsets]) - last
    free_turn = of(turns, free)

    def role_of(g):
        return jnp.where(g == last, 1, jnp.where((g == free) & (free_turn != 0), 2, 0))

    def row_of(g):
        o = of(offsets, g)
        return (o + 2 * block + (x_hi ^ (o & 1))) >> 5

    def parity_before(g):
        o = of(offsets, g)
        return ((o >> 5) + (2 * block + x_hi < (o & 31)).astype(jnp.int32)) & 1

    group = group_of(x)
    offset = of(offsets, group)
    out = {
        CORE: core,
        X_HI: x_hi,
        BLOCK: block,
        STAYS: (x_hi == core).astype(jnp.int32),
        PARITY_LAST: parity_before(last),
        PARITY_FREE: parity_before(free),
    }
    for by in range(4):
        to, came = group_of((x + by) & 3), group_of((x - by) & 3)
        out[PARITY + by] = parity_before(to)
        out[ROLE_TO + by] = role_of(to)
        out[SIDE + by] = (((x + by) & 3) >> 1) ^ (offset & 1)
        out[OWNER + by] = row_of(came) - 2 * x_lo
        out[ROLE_FROM + by] = role_of(came)
    for h in range(2):
        row = (offset + 2 * block + h) >> 5
        out[SOURCE + h] = (x - (2 * (h ^ (offset & 1)) + (row >> 1))) & 3
    return out, free_turn


def fetch(which, choices, sems):
    for k, (a, b, out) in enumerate(choices):

        @pl.when(which)
        def _(a=a, out=out, k=k):
            pltpu.make_async_copy(a, out, sems.at[k]).start()

        @pl.when(jnp.logical_not(which))
        def _(b=b, out=out, k=k):
            pltpu.make_async_copy(b, out, sems.at[k]).start()

    for k, (a, _, out) in enumerate(choices):
        pltpu.make_async_copy(a, out, sems.at[k]).wait()


def plan_kernel(ids, offsets, velocity, epsilon, delta, angle, plan, turn_z, turn_y, own, other, sems):
    values, free_turn = plan_values(ids, [offsets[g] for g in range(4)])
    for k, v in values.items():
        plan[k] = v
    turn_z[0] = free_turn >> 3
    turn_y[0] = free_turn & 7
    fetch(
        values[CORE] == 0,
        (
            (velocity, delta, own.at[0]),
            (epsilon, angle, own.at[1]),
            (delta, velocity, other.at[0]),
            (angle, epsilon, other.at[1]),
        ),
        sems,
    )


def state_kernel(plan, fwd_now, adj_now, fwd_before, adj_before, one, two, sems):
    fetch(
        plan[X_HI] == 0,
        (
            (adj_now.at[0], fwd_now.at[0], one.at[0]),
            (fwd_now.at[0], adj_now.at[0], two.at[0]),
            (adj_before.at[0], fwd_before.at[0], one.at[1]),
            (fwd_before.at[0], adj_before.at[0], two.at[1]),
        ),
        sems,
    )


def rows_kernel(plan, own, came, last, free):
    mine_last, mine_free = plan[PARITY_LAST] == plan[CORE], plan[PARITY_FREE] == plan[CORE]
    for f in range(2):
        for i in range(TX):
            a, b = own[f, i], came[f, i]
            last[f, i] = jnp.where(mine_last, a, b)
            free[f, i] = jnp.where(mine_free, a, b)


def send_kernel(plan, own, came, last, last_came, free_came, kept, one, two, *outs):
    first, stays = plan[CORE] == 0, plan[STAYS] == 1
    for t in range(2):
        lo, hi = outs[4 + 2 * t : 6 + 2 * t]
        for p in range(2):
            for i in range(TX):
                a, b = one[t, p, i], jnp.where(stays, kept[t, p, i], two[t, p, i])
                lo[p, i] = jnp.where(first, b, a)
                hi[p, i] = jnp.where(first, a, b)
    high = plan[X_HI] == 1
    mine = [plan[PARITY + by] == plan[CORE] for by in range(4)]
    role = [plan[ROLE_TO + by] for by in range(4)]
    for f in range(2):
        for i in range(TX):
            a, b = own[f, i], came[f, i]
            turned_last = jnp.where(high, last_came[f, i], last[f, i])
            turned_free = free_came[f, i]
            for by in range(4):
                straight = jnp.where(mine[by], a, b)
                turned = jnp.where(role[by] == 1, turned_last, turned_free)
                outs[by][f, i] = jnp.where(role[by] == 0, straight, turned)


def tiles_kernel(plan, kept, got_1, got_2, got_3, out):
    source = [plan[SOURCE + h] for h in range(2)]
    for f in range(2):
        for i in range(TX):
            rows = [kept[f, i], got_1[f, i], got_2[f, i], got_3[f, i]]
            for h in range(2):
                a = jnp.where(source[h] == 0, rows[0], rows[1])
                b = jnp.where(source[h] == 2, rows[2], rows[3])
                out[h, f, i] = jnp.where(source[h] < 2, a, b)


def fill_rows(plan, lo, hi, low, high, ext):
    first, last = plan[BLOCK] == 0, plan[BLOCK] == 15
    for p in range(2):
        for i in range(TX):
            ext[p, i] = jnp.where(first, 0.0, low[p, i])
            ext[p, TX + i] = lo[p, i]
            ext[p, 2 * TX + i] = hi[p, i]
            ext[p, 3 * TX + i] = jnp.where(last, 0.0, high[p, i])


def step_kernel(plan, lo, hi, lo_b, hi_b, low, high, coef, inj, new_lo, new_hi, *rest):
    packed, ext = (rest[0], rest[1]) if len(rest) == 2 else (None, rest[0])
    fill_rows(plan, lo, hi, low, high, ext)
    for t, (back, mid, out) in enumerate(((lo_b, lo, new_lo), (hi_b, hi, new_hi))):

        def tile(i, carry, t=t, back=back, mid=mid, out=out):
            def emit(h, new_p, new_q):
                out[0, i, :, h] = new_p
                out[1, i, :, h] = new_q
                if packed is not None:
                    packed[0, t, i, :, h] = mid[0, i, :, h]
                    packed[1, t, i, :, h] = new_p

            one_row(ext, t * TX + i, lambda p, h: back[p, i, :, h], coef, inj, emit)
            return carry

        lax.fori_loop(0, TX, tile, 0)


def one_row(ext, i, before, coef, inj, emit):
    lane = lax.broadcasted_iota(jnp.int32, (AY, HALF), 1)
    row = lax.broadcasted_iota(jnp.int32, (AY, HALF), 0)
    halves = (pl.ds(0, HALF), pl.ds(HALF, HALF))
    parts = []
    for p in range(2):
        rows = [[ext[p, i + d, :, h] for h in halves] for d in range(9)]
        curve_x, slope_x = x_parts(rows)
        parts.append((rows[4], curve_x, second_z(rows[4], lane), first_z(slope_x, lane)))
    (mid_p, xp, zp, cp), (mid_q, xq, zq, cq) = parts
    yp = second_y(mid_p, row)
    for s, h in enumerate(halves):
        aniso, coupled, square = coef[0, i, :, h], coef[1, i, :, h], coef[2, i, :, h]
        sine, cosine, double = coef[3, i, :, h], coef[4, i, :, h], coef[5, i, :, h]
        axial_p = sine * xp[s] + cosine * zp[s] + double * cp[s]
        plane_p = xp[s] + yp[s] + zp[s] - axial_p
        axial_q = sine * xq[s] + cosine * zq[s] + double * cq[s]
        add = inj[i, :, h]
        new_p = 2.0 * mid_p[s] - before(0, h) + aniso * plane_p + coupled * axial_q + add
        new_q = 2.0 * mid_q[s] - before(1, h) + coupled * plane_p + square * axial_q + add
        emit(h, new_p, new_q)


def last_kernel(plan, lo, hi, lo_b, hi_b, low, high, coef, inj, other, keep, give, ext, part):
    fill_rows(plan, lo, hi, low, high, ext)
    for t, (back, mid) in enumerate(((lo_b, lo), (hi_b, hi))):

        def tile(i, carry, t=t, back=back, mid=mid):
            def emit(h, new_p, new_q):
                part[t, i, :, h] = new_p * other[0, t, i, :, h] + mid[0, i, :, h] * other[1, t, i, :, h]

            one_row(ext, t * TX + i, lambda p, h: back[p, i, :, h], coef, inj, emit)
            return carry

        lax.fori_loop(0, TX, tile, 0)
    first = plan[CORE] == 0
    for t in range(2):
        for i in range(TX):
            low_y, high_y = part[t, i, :HALF_Y], part[t, i, HALF_Y:]
            keep[t, i] = jnp.where(first, low_y, high_y)
            give[t, i] = jnp.where(first, high_y, low_y)


def total_kernel(plan, keep, came, *outs):
    for i in range(TX):
        lo = keep[0, i] + came[0, i]
        hi = keep[1, i] + came[1, i]
        for by in range(4):
            outs[by][i] = jnp.where(plan[SIDE + by] == 0, lo, hi)


def owners_kernel(plan, kept, got_1, got_2, got_3, straight, last, free):
    for i in range(TX):
        parts = [kept[i], got_1[i], got_2[i], got_3[i]]
        for k, out in enumerate((straight, last, free)):
            for core in range(2):
                acc = jnp.zeros_like(parts[0])
                for by in range(4):
                    ours = (plan[OWNER + by] == core) & (plan[ROLE_FROM + by] == k)
                    acc = acc + jnp.where(ours, parts[by], 0.0)
                out[core, i] = acc


def image_kernel(plan, straight, last, last_came, free_came, keep, give):
    high, first = plan[X_HI] == 1, plan[CORE] == 0
    for i in range(TX):
        sums = []
        for core in range(2):
            turned = jnp.where(high, last_came[core, i], last[core, i])
            sums.append(straight[core, i] + turned + free_came[core, i])
        keep[i] = jnp.where(first, sums[0], sums[1])
        give[i] = jnp.where(first, sums[1], sums[0])


def join_kernel(plan, keep, came, out):
    first = plan[CORE] == 0
    for i in range(TX):
        out[i, :HALF_Y] = jnp.where(first, keep[i], came[i])
        out[i, HALF_Y:] = jnp.where(first, came[i], keep[i])


def inject_kernel(plan, cells, amounts, out):
    x = cells[0:1, :] - 8 * plan[BLOCK]
    here = (x >= 0) & (x < 8)
    spot = jnp.where(here, x * AY + cells[1:2, :], -1)
    depth = cells[2:3, :]
    count = cells.shape[1]
    which = (lax.broadcasted_iota(jnp.int32, (8 * AY, count), 0) == spot).astype(F32)
    level = lax.broadcasted_iota(jnp.int32, (AZ, count), 0) == depth
    for k in range(STEPS):
        values = jnp.where(level, amounts[k : k + 1, :], 0.0)
        flat = lax.dot_general(
            which,
            values,
            (((1,), (1,)), ((), ())),
            precision=lax.Precision.HIGHEST,
            preferred_element_type=F32,
        )
        for i in range(8):
            out[k, i] = flat[i * AY : (i + 1) * AY, :]


def sine_cosine(angle):
    sq = angle * angle
    sine = -1.0 / 39916800.0
    for c in (1.0 / 362880.0, -1.0 / 5040.0, 1.0 / 120.0, -1.0 / 6.0, 1.0):
        sine = sine * sq + c
    cosine = 1.0 / 479001600.0
    for c in (-1.0 / 3628800.0, 1.0 / 40320.0, -1.0 / 720.0, 1.0 / 24.0, -0.5, 1.0):
        cosine = cosine * sq + c
    return sine * angle, cosine


def coef_kernel(plan, own, other, out):
    core = plan[CORE]
    for t in range(2):

        def tile(i, carry, t=t):
            mine = [own[t, f, i] for f in range(2)]
            theirs = [other[t, f, i] for f in range(2)]
            velocity = jnp.where(core == 0, mine[0], theirs[0])
            epsilon = jnp.where(core == 0, mine[1], theirs[1])
            delta = jnp.where(core == 0, theirs[0], mine[0])
            angle = jnp.where(core == 0, theirs[1], mine[1])
            square = velocity * velocity
            sine, cosine = sine_cosine(angle)
            k = t * TX + i
            out[0, k] = square * (1.0 + 2.0 * epsilon)
            out[1, k] = square * jnp.sqrt(1.0 + 2.0 * delta)
            out[2, k] = square
            out[3, k] = sine * sine
            out[4, k] = cosine * cosine
            out[5, k] = 2.0 * sine * cosine
            return carry

        lax.fori_loop(0, TX, tile, 0)


HBM = pl.BlockSpec(memory_space=pltpu.HBM)
LIMIT = pltpu.CompilerParams(vmem_limit_bytes=8 * 1024 * 1024)


def call(kernel, n_in, outs, scratch=()):
    return pl.pallas_call(
        kernel,
        out_shape=[jax.ShapeDtypeStruct(s, F32) for s in outs],
        in_specs=[SMEM] + [VMEM] * n_in,
        out_specs=[VMEM] * len(outs),
        scratch_shapes=[pltpu.VMEM(s, F32) for s in scratch],
        compiler_params=LIMIT,
    )


TILE = (2, TX, AY, AZ)
PART = (TX, HALF_Y, AZ)


def turn(value, x_hi, turn_z, turn_y, sign):
    def roll(v, by):
        return send(v, rolled(sign * by, sign * by)) if by else v

    def columns(v, r):
        if r == 1:
            return jnp.where(x_hi == 1, v, roll(v, 1))
        if r % 2 == 0:
            return roll(v, r // 2)
        return send(v, rolled(sign * (r // 2 + 1), sign * (r // 2)))

    value = lax.switch(turn_z[0], [lambda v, k=k: roll(v, 4 * k) for k in range(4)], value)
    return lax.switch(turn_y[0], [lambda v, r=r: columns(v, r) for r in range(8)], value)


def local(
    velocity,
    thomsen_epsilon,
    thomsen_delta,
    tilt_angle,
    fwd_now,
    fwd_before,
    adj_now,
    adj_before,
    wavelet,
    traces,
    offsets,
    source_cell,
    receiver_cell,
):
    shot, aper = lax.axis_index("shot"), lax.axis_index("aper")
    ids = jnp.stack([shot, aper]).astype(jnp.int32)
    swap, up, down = other_core(), rolled(1, 1), rolled(-1, -1)

    plan, turn_z, turn_y, own, other = pl.pallas_call(
        plan_kernel,
        out_shape=[jax.ShapeDtypeStruct((n,), jnp.int32) for n in (40, 1, 1)] + [jax.ShapeDtypeStruct(TILE, F32)] * 2,
        in_specs=[SMEM] * 2 + [HBM] * 4,
        out_specs=[SMEM] * 3 + [VMEM] * 2,
        scratch_shapes=[pltpu.SemaphoreType.DMA((4,))],
        compiler_params=LIMIT,
    )(ids, offsets, velocity, thomsen_epsilon, thomsen_delta, tilt_angle)
    came = send(other, swap)
    one, two = pl.pallas_call(
        state_kernel,
        out_shape=[jax.ShapeDtypeStruct((2,) + TILE, F32)] * 2,
        in_specs=[SMEM] + [HBM] * 4,
        out_specs=[VMEM] * 2,
        scratch_shapes=[pltpu.SemaphoreType.DMA((4,))],
        compiler_params=LIMIT,
    )(plan, fwd_now, adj_now, fwd_before, adj_before)
    got_one, got_two = send(one, state_first()), send(two, state_second())

    last, free = call(rows_kernel, 2, [TILE] * 2)(plan, own, came)
    last_came = send(last, up)
    free_came = turn(free, aper % 2, turn_z, turn_y, -1)
    *rows, lo, hi, lo_b, hi_b = call(send_kernel, 8, [TILE] * 8)(
        plan, own, came, last, last_came, free_came, two, got_one, got_two
    )
    got = [send(rows[by], across(by)) for by in range(1, 4)]
    tiles = call(tiles_kernel, 4, [(2,) + TILE])(plan, rows[0], *got)[0]
    coef = call(coef_kernel, 2, [(6, 8, AY, AZ)])(plan, tiles, send(tiles, swap))[0]

    n_rec = receiver_cell.shape[1]
    group = 2 * (shot // 2) + aper % 2
    rec = receiver_cell[group].T
    at_first = jnp.arange(n_rec)[None, :] == 0
    src = jnp.where(at_first, source_cell[group][:, None], -1000)
    pulse = jnp.where(at_first, wavelet[group][:, None], 0.0)
    forward = shot % 2 == 0
    cells = jnp.where(forward, src, rec)
    amounts = jnp.where(forward, pulse, traces[group])
    inj = call(inject_kernel, 2, [(STEPS, 8, AY, AZ)])(plan, cells, amounts)[0]

    shared = None
    for k in range(STEPS - 1):
        low, high = send(hi, up), send(lo, down)
        outs = [TILE, TILE] + ([(2, 2, TX, AY, AZ)] if k == 1 else [])
        new = call(step_kernel, 8, outs, [(2, 4 * TX, AY, AZ)])(
            plan, lo, hi, lo_b, hi_b, low, high, coef, inj[k]
        )
        if k == 1:
            shared = send(new[2], swap)
        lo_b, hi_b, lo, hi = lo, hi, new[0], new[1]
    low, high = send(hi, up), send(lo, down)
    keep, give = call(
        last_kernel, 9, [(2,) + PART] * 2, [(2, 4 * TX, AY, AZ), (2, TX, AY, AZ)]
    )(plan, lo, hi, lo_b, hi_b, low, high, coef, inj[STEPS - 1], shared)

    parts = call(total_kernel, 2, [PART] * 4)(plan, keep, send(give, swap))
    got = [send(parts[by], across(by)) for by in range(1, 4)]
    straight, last, free = call(owners_kernel, 4, [(2,) + PART] * 3)(plan, parts[0], *got)
    last_came = send(last, down)
    free_came = turn(free, aper % 2, turn_z, turn_y, 1)
    keep, give = call(image_kernel, 4, [PART] * 2)(plan, straight, last, last_came, free_came)
    return call(join_kernel, 2, [(TX, AY, AZ)])(plan, keep, send(give, swap))[0]


def solution(mesh):
    model = P(("shot", "aper"), None, None)
    field = P("shot", None, "aper", None, None)
    return jax.shard_map(
        local,
        mesh=mesh,
        in_specs=(model,) * 4 + (field,) * 4 + (P(),) * 5,
        out_specs=model,
        check_vma=False,
    )
```

```python
import jax
import jax.numpy as jnp
from jax import lax
from jax.experimental import pallas as pl
from jax.experimental.pallas import tpu as pltpu
from jax.sharding import PartitionSpec as P

second_coef = (-205.0 / 72.0, 8.0 / 5.0, -1.0 / 5.0, 8.0 / 315.0, -1.0 / 560.0)
first_coef = (4.0 / 5.0, -1.0 / 5.0, 4.0 / 105.0, -1.0 / 280.0)

AXES = ("shot", "aper")
STEPS = 4
TX = 4
AY = 32
AZ = 256
HALF = 128
HALF_Y = AY // 2
F32 = jnp.float32
VMEM = pl.BlockSpec(memory_space=pltpu.VMEM)
SMEM = pl.BlockSpec(memory_space=pltpu.SMEM)


def device(x, core, y, z):
    return ((x % 2) * 2 + core) * 32 + ((z % 4) * 4 + y % 4) * 2 + x // 2


def everyone():
    return [(x, c, y, z) for x in range(4) for c in range(2) for y in range(4) for z in range(4)]


def pairs_of(rule):
    pairs = [(device(*d), device(*rule(*d))) for d in everyone()]
    assert sorted(t for _, t in pairs) == list(range(128))
    assert all(s != t for s, t in pairs)
    return pairs


def send(value, pairs):
    return lax.ppermute(value, AXES, pairs)


def other_core():
    return pairs_of(lambda x, c, y, z: (x, 1 - c, y, z))


def state_first():
    def rule(x, c, y, z):
        t = {(0, 0): (0, 1), (0, 1): (1, 1), (1, 0): (0, 0), (1, 1): (1, 0)}[(x // 2, c)]
        return (2 * t[0] + x % 2, t[1], y, z)

    return pairs_of(rule)


def state_second():
    return [
        (device(x, c, y, z), device((x + 2) % 4, 1 - c, y, z)) for x, c, y, z in everyone() if x // 2 != c
    ]


def across(by):
    return pairs_of(lambda x, c, y, z: ((x + by) % 4, c, y, z))


def rolled(by_low, by_high):
    def rule(x, c, y, z):
        j = (4 * z + y + (by_high if x // 2 else by_low)) % 16
        return (x, c, j % 4, j // 4)

    return pairs_of(rule)


def z_plus(pair, d, lane):
    a, b = pair
    ra, rb = pltpu.roll(a, HALF - d, 1), pltpu.roll(b, HALF - d, 1)
    keep = lane < HALF - d
    return jnp.where(keep, ra, rb), jnp.where(keep, rb, 0.0)


def z_minus(pair, d, lane):
    a, b = pair
    ra, rb = pltpu.roll(a, d, 1), pltpu.roll(b, d, 1)
    keep = lane >= d
    return jnp.where(keep, ra, 0.0), jnp.where(keep, rb, ra)


def second_z(pair, lane):
    out = [second_coef[0] * v for v in pair]
    for d in range(1, 5):
        up, down = z_plus(pair, d, lane), z_minus(pair, d, lane)
        out = [o + second_coef[d] * (u + w) for o, u, w in zip(out, up, down)]
    return out


def first_z(pair, lane):
    out = None
    for d in range(1, 5):
        up, down = z_plus(pair, d, lane), z_minus(pair, d, lane)
        term = [first_coef[d - 1] * (u - w) for u, w in zip(up, down)]
        out = term if out is None else [o + t for o, t in zip(out, term)]
    return out


def second_y(pair, row):
    out = []
    for f in pair:
        acc = second_coef[0] * f
        for d in range(1, 5):
            up = jnp.where(row < AY - d, pltpu.roll(f, AY - d, 0), 0.0)
            down = jnp.where(row >= d, pltpu.roll(f, d, 0), 0.0)
            acc = acc + second_coef[d] * (up + down)
        out.append(acc)
    return out


def x_parts(rows):
    second, first = [], []
    for s in range(2):
        acc = second_coef[0] * rows[4][s]
        der = None
        for d in range(1, 5):
            acc = acc + second_coef[d] * (rows[4 + d][s] + rows[4 - d][s])
            term = first_coef[d - 1] * (rows[4 + d][s] - rows[4 - d][s])
            der = term if der is None else der + term
        second.append(acc)
        first.append(der)
    return second, first


CORE, X_HI, BLOCK, STAYS, PARITY_LAST, PARITY_FREE = range(6)
PARITY, ROLE_TO, SIDE, SOURCE, OWNER, ROLE_FROM = 12, 16, 20, 24, 28, 32


def plan_values(ids, offsets):
    shot, aper = ids[0], ids[1]
    core, x_lo, x_hi = shot & 1, shot >> 1, aper & 1
    x = 2 * x_hi + x_lo
    z, y = aper >> 3, (aper >> 1) & 3
    block = 4 * z + y
    turns = [o & 31 for o in offsets]

    def of(values, g):
        return jnp.where(g < 2, jnp.where(g == 0, values[0], values[1]), jnp.where(g == 2, values[2], values[3]))

    def first(flags):
        return jnp.where(flags[0], 0, jnp.where(flags[1], 1, jnp.where(flags[2], 2, 3)))

    def group_of(x):
        return 2 * (x & 1) + (x >> 1)

    last = first([t == 31 for t in turns])
    free = 6 - first([o == 0 for o in offsets]) - first([o == 96 for o in offsets]) - last
    free_turn = of(turns, free)

    def role_of(g):
        return jnp.where(g == last, 1, jnp.where((g == free) & (free_turn != 0), 2, 0))

    def row_of(g):
        o = of(offsets, g)
        return (o + 2 * block + (x_hi ^ (o & 1))) >> 5

    def parity_before(g):
        o = of(offsets, g)
        return ((o >> 5) + (2 * block + x_hi < (o & 31)).astype(jnp.int32)) & 1

    group = group_of(x)
    offset = of(offsets, group)
    out = {
        CORE: core,
        X_HI: x_hi,
        BLOCK: block,
        STAYS: (x_hi == core).astype(jnp.int32),
        PARITY_LAST: parity_before(last),
        PARITY_FREE: parity_before(free),
    }
    for by in range(4):
        to, came = group_of((x + by) & 3), group_of((x - by) & 3)
        out[PARITY + by] = parity_before(to)
        out[ROLE_TO + by] = role_of(to)
        out[SIDE + by] = (((x + by) & 3) >> 1) ^ (offset & 1)
        out[OWNER + by] = row_of(came) - 2 * x_lo
        out[ROLE_FROM + by] = role_of(came)
    for h in range(2):
        row = (offset + 2 * block + h) >> 5
        out[SOURCE + h] = (x - (2 * (h ^ (offset & 1)) + (row >> 1))) & 3
    return out, free_turn


def fetch(which, choices, sems):
    for k, (a, b, out) in enumerate(choices):

        @pl.when(which)
        def _(a=a, out=out, k=k):
            pltpu.make_async_copy(a, out, sems.at[k]).start()

        @pl.when(jnp.logical_not(which))
        def _(b=b, out=out, k=k):
            pltpu.make_async_copy(b, out, sems.at[k]).start()

    return [pltpu.make_async_copy(a, out, sems.at[k]) for k, (a, _, out) in enumerate(choices)]


def plan_kernel(ids, offsets, velocity, epsilon, delta, angle, plan, turn_z, turn_y, own, other, sems):
    copies = fetch(
        ids[0] & 1 == 0,
        (
            (delta, velocity, other.at[0]),
            (angle, epsilon, other.at[1]),
            (velocity, delta, own.at[0]),
            (epsilon, angle, own.at[1]),
        ),
        sems,
    )
    values, free_turn = plan_values(ids, [offsets[g] for g in range(4)])
    for k, v in values.items():
        plan[k] = v
    turn_z[0] = free_turn >> 3
    turn_y[0] = free_turn & 7
    for copy in copies:
        copy.wait()


def state_kernel(plan, fwd_now, adj_now, fwd_before, adj_before, one, two, sems):
    copies = fetch(
        plan[X_HI] == 0,
        (
            (adj_now.at[0], fwd_now.at[0], one.at[0]),
            (fwd_now.at[0], adj_now.at[0], two.at[0]),
            (adj_before.at[0], fwd_before.at[0], one.at[1]),
            (fwd_before.at[0], adj_before.at[0], two.at[1]),
        ),
        sems,
    )
    for copy in copies:
        copy.wait()


def rows_kernel(plan, own, came, last, free):
    mine_last, mine_free = plan[PARITY_LAST] == plan[CORE], plan[PARITY_FREE] == plan[CORE]
    for f in range(2):
        for i in range(TX):
            a, b = own[f, i], came[f, i]
            last[f, i] = jnp.where(mine_last, a, b)
            free[f, i] = jnp.where(mine_free, a, b)


def send_kernel(plan, own, came, last, last_came, free_came, kept, one, two, *outs):
    first, stays = plan[CORE] == 0, plan[STAYS] == 1
    for t in range(2):
        lo, hi = outs[4 + 2 * t : 6 + 2 * t]
        for p in range(2):
            for i in range(TX):
                a, b = one[t, p, i], jnp.where(stays, kept[t, p, i], two[t, p, i])
                lo[p, i] = jnp.where(first, b, a)
                hi[p, i] = jnp.where(first, a, b)
    high = plan[X_HI] == 1
    mine = [plan[PARITY + by] == plan[CORE] for by in range(4)]
    role = [plan[ROLE_TO + by] for by in range(4)]
    for f in range(2):
        for i in range(TX):
            a, b = own[f, i], came[f, i]
            turned_last = jnp.where(high, last_came[f, i], last[f, i])
            turned_free = free_came[f, i]
            for by in range(4):
                straight = jnp.where(mine[by], a, b)
                turned = jnp.where(role[by] == 1, turned_last, turned_free)
                outs[by][f, i] = jnp.where(role[by] == 0, straight, turned)


def tiles_kernel(plan, kept, got_1, got_2, got_3, low, high, out):
    del low, high
    source = [plan[SOURCE + h] for h in range(2)]
    for f in range(2):
        for i in range(TX):
            rows = [kept[f, i], got_1[f, i], got_2[f, i], got_3[f, i]]
            for h in range(2):
                a = jnp.where(source[h] == 0, rows[0], rows[1])
                b = jnp.where(source[h] == 2, rows[2], rows[3])
                out[h, f, i] = jnp.where(source[h] < 2, a, b)


def fill_rows(plan, lo, hi, low, high, ext):
    first, last = plan[BLOCK] == 0, plan[BLOCK] == 15
    for p in range(2):
        for i in range(TX):
            ext[p, i] = jnp.where(first, 0.0, low[p, i])
            ext[p, TX + i] = lo[p, i]
            ext[p, 2 * TX + i] = hi[p, i]
            ext[p, 3 * TX + i] = jnp.where(last, 0.0, high[p, i])


def step_kernel(plan, lo, hi, lo_b, hi_b, low, high, coef, inj, new_lo, new_hi, *rest):
    packed, ext = (rest[0], rest[1]) if len(rest) == 2 else (None, rest[0])
    fill_rows(plan, lo, hi, low, high, ext)
    for t, (back, mid, out) in enumerate(((lo_b, lo, new_lo), (hi_b, hi, new_hi))):

        def tile(i, carry, t=t, back=back, mid=mid, out=out):
            def emit(h, new_p, new_q):
                out[0, i, :, h] = new_p
                out[1, i, :, h] = new_q
                if packed is not None:
                    packed[0, t, i, :, h] = mid[0, i, :, h]
                    packed[1, t, i, :, h] = new_p

            one_row(ext, t * TX + i, lambda p, h: back[p, i, :, h], coef, inj, emit)
            return carry

        lax.fori_loop(0, TX, tile, 0)


def one_row(ext, i, before, coef, inj, emit):
    lane = lax.broadcasted_iota(jnp.int32, (AY, HALF), 1)
    row = lax.broadcasted_iota(jnp.int32, (AY, HALF), 0)
    halves = (pl.ds(0, HALF), pl.ds(HALF, HALF))
    parts = []
    for p in range(2):
        rows = [[ext[p, i + d, :, h] for h in halves] for d in range(9)]
        curve_x, slope_x = x_parts(rows)
        parts.append((rows[4], curve_x, second_z(rows[4], lane), first_z(slope_x, lane)))
    (mid_p, xp, zp, cp), (mid_q, xq, zq, cq) = parts
    yp = second_y(mid_p, row)
    for s, h in enumerate(halves):
        aniso, coupled, square = coef[0, i, :, h], coef[1, i, :, h], coef[2, i, :, h]
        sine, cosine, double = coef[3, i, :, h], coef[4, i, :, h], coef[5, i, :, h]
        axial_p = sine * xp[s] + cosine * zp[s] + double * cp[s]
        plane_p = xp[s] + yp[s] + zp[s] - axial_p
        axial_q = sine * xq[s] + cosine * zq[s] + double * cq[s]
        add = inj[i, :, h]
        new_p = 2.0 * mid_p[s] - before(0, h) + aniso * plane_p + coupled * axial_q + add
        new_q = 2.0 * mid_q[s] - before(1, h) + coupled * plane_p + square * axial_q + add
        emit(h, new_p, new_q)


def last_kernel(plan, lo, hi, lo_b, hi_b, low, high, coef, inj, other, keep, give, ext, part):
    fill_rows(plan, lo, hi, low, high, ext)
    for t, (back, mid) in enumerate(((lo_b, lo), (hi_b, hi))):

        def tile(i, carry, t=t, back=back, mid=mid):
            def emit(h, new_p, new_q):
                part[t, i, :, h] = new_p * other[0, t, i, :, h] + mid[0, i, :, h] * other[1, t, i, :, h]

            one_row(ext, t * TX + i, lambda p, h: back[p, i, :, h], coef, inj, emit)
            return carry

        lax.fori_loop(0, TX, tile, 0)
    first = plan[CORE] == 0
    for t in range(2):
        for i in range(TX):
            low_y, high_y = part[t, i, :HALF_Y], part[t, i, HALF_Y:]
            keep[t, i] = jnp.where(first, low_y, high_y)
            give[t, i] = jnp.where(first, high_y, low_y)


def total_kernel(plan, keep, came, *outs):
    for i in range(TX):
        lo = keep[0, i] + came[0, i]
        hi = keep[1, i] + came[1, i]
        for by in range(4):
            outs[by][i] = jnp.where(plan[SIDE + by] == 0, lo, hi)


def owners_kernel(plan, kept, got_1, got_2, got_3, straight, last, free):
    for i in range(TX):
        parts = [kept[i], got_1[i], got_2[i], got_3[i]]
        for k, out in enumerate((straight, last, free)):
            for core in range(2):
                acc = jnp.zeros_like(parts[0])
                for by in range(4):
                    ours = (plan[OWNER + by] == core) & (plan[ROLE_FROM + by] == k)
                    acc = acc + jnp.where(ours, parts[by], 0.0)
                out[core, i] = acc


def image_kernel(plan, straight, last, last_came, free_came, keep, give):
    high, first = plan[X_HI] == 1, plan[CORE] == 0
    for i in range(TX):
        sums = []
        for core in range(2):
            turned = jnp.where(high, last_came[core, i], last[core, i])
            sums.append(straight[core, i] + turned + free_came[core, i])
        keep[i] = jnp.where(first, sums[0], sums[1])
        give[i] = jnp.where(first, sums[1], sums[0])


def join_kernel(plan, keep, came, out):
    first = plan[CORE] == 0
    for i in range(TX):
        out[i, :HALF_Y] = jnp.where(first, keep[i], came[i])
        out[i, HALF_Y:] = jnp.where(first, came[i], keep[i])


def inject_kernel(plan, cells, amounts, out):
    x = cells[0:1, :] - 8 * plan[BLOCK]
    here = (x >= 0) & (x < 8)
    spot = jnp.where(here, x * AY + cells[1:2, :], -1)
    depth = cells[2:3, :]
    count = cells.shape[1]
    which = (lax.broadcasted_iota(jnp.int32, (8 * AY, count), 0) == spot).astype(F32)
    level = lax.broadcasted_iota(jnp.int32, (AZ, count), 0) == depth
    for k in range(STEPS):
        values = jnp.where(level, amounts[k : k + 1, :], 0.0)
        flat = lax.dot_general(
            which,
            values,
            (((1,), (1,)), ((), ())),
            precision=lax.Precision.HIGHEST,
            preferred_element_type=F32,
        )
        for i in range(8):
            out[k, i] = flat[i * AY : (i + 1) * AY, :]


def sine_cosine(angle):
    sq = angle * angle
    sine = -1.0 / 39916800.0
    for c in (1.0 / 362880.0, -1.0 / 5040.0, 1.0 / 120.0, -1.0 / 6.0, 1.0):
        sine = sine * sq + c
    cosine = 1.0 / 479001600.0
    for c in (-1.0 / 3628800.0, 1.0 / 40320.0, -1.0 / 720.0, 1.0 / 24.0, -0.5, 1.0):
        cosine = cosine * sq + c
    return sine * angle, cosine


def coef_kernel(plan, own, other, out):
    core = plan[CORE]
    for t in range(2):

        def tile(i, carry, t=t):
            mine = [own[t, f, i] for f in range(2)]
            theirs = [other[t, f, i] for f in range(2)]
            velocity = jnp.where(core == 0, mine[0], theirs[0])
            epsilon = jnp.where(core == 0, mine[1], theirs[1])
            delta = jnp.where(core == 0, theirs[0], mine[0])
            angle = jnp.where(core == 0, theirs[1], mine[1])
            square = velocity * velocity
            sine, cosine = sine_cosine(angle)
            k = t * TX + i
            out[0, k] = square * (1.0 + 2.0 * epsilon)
            out[1, k] = square * jnp.sqrt(1.0 + 2.0 * delta)
            out[2, k] = square
            out[3, k] = sine * sine
            out[4, k] = cosine * cosine
            out[5, k] = 2.0 * sine * cosine
            return carry

        lax.fori_loop(0, TX, tile, 0)


HBM = pl.BlockSpec(memory_space=pltpu.HBM)
LIMIT = pltpu.CompilerParams(vmem_limit_bytes=4 * 1024 * 1024)


def in_hbm(value):
    return pltpu.with_memory_space_constraint(value, pltpu.HBM)


def call(kernel, n_in, outs, scratch=()):
    return pl.pallas_call(
        kernel,
        out_shape=[jax.ShapeDtypeStruct(s, F32) for s in outs],
        in_specs=[SMEM] + [VMEM] * n_in,
        out_specs=[VMEM] * len(outs),
        scratch_shapes=[pltpu.VMEM(s, F32) for s in scratch],
        compiler_params=LIMIT,
    )


TILE = (2, TX, AY, AZ)
PART = (TX, HALF_Y, AZ)


def turn(value, x_hi, turn_z, turn_y, sign):
    def roll(v, by):
        return send(v, rolled(sign * by, sign * by)) if by else v

    def columns(v, r):
        if r == 1:
            return jnp.where(x_hi == 1, v, roll(v, 1))
        if r % 2 == 0:
            return roll(v, r // 2)
        return send(v, rolled(sign * (r // 2 + 1), sign * (r // 2)))

    value = lax.switch(turn_z[0], [lambda v, k=k: roll(v, 4 * k) for k in range(4)], value)
    return lax.switch(turn_y[0], [lambda v, r=r: columns(v, r) for r in range(8)], value)


def local(
    velocity,
    thomsen_epsilon,
    thomsen_delta,
    tilt_angle,
    fwd_now,
    fwd_before,
    adj_now,
    adj_before,
    wavelet,
    traces,
    offsets,
    source_cell,
    receiver_cell,
):
    shot, aper = lax.axis_index("shot"), lax.axis_index("aper")
    ids = jnp.stack([shot, aper]).astype(jnp.int32)
    swap, up, down = other_core(), rolled(1, 1), rolled(-1, -1)

    plan, turn_z, turn_y, own, other = pl.pallas_call(
        plan_kernel,
        out_shape=[jax.ShapeDtypeStruct((n,), jnp.int32) for n in (40, 1, 1)] + [jax.ShapeDtypeStruct(TILE, F32)] * 2,
        in_specs=[SMEM] * 2 + [HBM] * 4,
        out_specs=[SMEM] * 3 + [VMEM] * 2,
        scratch_shapes=[pltpu.SemaphoreType.DMA((4,))],
        compiler_params=LIMIT,
    )(ids, offsets, *(in_hbm(v) for v in (velocity, thomsen_epsilon, thomsen_delta, tilt_angle)))
    came = send(other, swap)
    one, two = pl.pallas_call(
        state_kernel,
        out_shape=[jax.ShapeDtypeStruct((2,) + TILE, F32)] * 2,
        in_specs=[SMEM] + [HBM] * 4,
        out_specs=[VMEM] * 2,
        scratch_shapes=[pltpu.SemaphoreType.DMA((4,))],
        compiler_params=LIMIT,
    )(plan, *(in_hbm(v) for v in (fwd_now, adj_now, fwd_before, adj_before)))
    got_one, got_two = send(one, state_first()), send(two, state_second())

    last, free = call(rows_kernel, 2, [TILE] * 2)(plan, own, came)
    last_came = send(last, up)
    free_came = turn(free, aper % 2, turn_z, turn_y, -1)
    *rows, lo, hi, lo_b, hi_b = call(send_kernel, 8, [TILE] * 8)(
        plan, own, came, last, last_came, free_came, two, got_one, got_two
    )
    got = [send(rows[by], across(by)) for by in range(1, 4)]
    low, high = send(hi, up), send(lo, down)
    tiles = call(tiles_kernel, 6, [(2,) + TILE])(plan, rows[0], *got, low, high)[0]
    coef = call(coef_kernel, 2, [(6, 8, AY, AZ)])(plan, tiles, send(tiles, swap))[0]

    n_rec = receiver_cell.shape[1]
    group = 2 * (shot // 2) + aper % 2
    rec = receiver_cell[group].T
    at_first = jnp.arange(n_rec)[None, :] == 0
    src = jnp.where(at_first, source_cell[group][:, None], -1000)
    pulse = jnp.where(at_first, wavelet[group][:, None], 0.0)
    forward = shot % 2 == 0
    cells = jnp.where(forward, src, rec)
    amounts = jnp.where(forward, pulse, traces[group])
    inj = call(inject_kernel, 2, [(STEPS, 8, AY, AZ)])(plan, cells, amounts)[0]

    shared = None
    for k in range(STEPS - 1):
        if k > 0:
            low, high = send(hi, up), send(lo, down)
        outs = [TILE, TILE] + ([(2, 2, TX, AY, AZ)] if k == 1 else [])
        new = call(step_kernel, 8, outs, [(2, 4 * TX, AY, AZ)])(
            plan, lo, hi, lo_b, hi_b, low, high, coef, inj[k]
        )
        if k == 1:
            shared = send(new[2], swap)
        lo_b, hi_b, lo, hi = lo, hi, new[0], new[1]
    low, high = send(hi, up), send(lo, down)
    keep, give = call(
        last_kernel, 9, [(2,) + PART] * 2, [(2, 4 * TX, AY, AZ), (2, TX, AY, AZ)]
    )(plan, lo, hi, lo_b, hi_b, low, high, coef, inj[STEPS - 1], shared)

    parts = call(total_kernel, 2, [PART] * 4)(plan, keep, send(give, swap))
    got = [send(parts[by], across(by)) for by in range(1, 4)]
    straight, last, free = call(owners_kernel, 4, [(2,) + PART] * 3)(plan, parts[0], *got)
    last_came = send(last, down)
    free_came = turn(free, aper % 2, turn_z, turn_y, 1)
    keep, give = call(image_kernel, 4, [PART] * 2)(plan, straight, last, last_came, free_came)
    return call(join_kernel, 2, [(TX, AY, AZ)])(plan, keep, send(give, swap))[0]


def solution(mesh):
    model = P(("shot", "aper"), None, None)
    field = P("shot", None, "aper", None, None)
    return jax.shard_map(
        local,
        mesh=mesh,
        in_specs=(model,) * 4 + (field,) * 4 + (P(),) * 5,
        out_specs=model,
        check_vma=False,
    )
```

```python
import jax
import jax.numpy as jnp
from jax import lax
from jax.experimental import pallas as pl
from jax.experimental.pallas import tpu as pltpu
from jax.sharding import PartitionSpec as P

second_coef = (-205.0 / 72.0, 8.0 / 5.0, -1.0 / 5.0, 8.0 / 315.0, -1.0 / 560.0)
first_coef = (4.0 / 5.0, -1.0 / 5.0, 4.0 / 105.0, -1.0 / 280.0)

AXES = ("shot", "aper")
STEPS = 4
TX = 4
AY = 32
AZ = 256
HALF = 128
HALF_Y = AY // 2
F32 = jnp.float32
VMEM = pl.BlockSpec(memory_space=pltpu.VMEM)
SMEM = pl.BlockSpec(memory_space=pltpu.SMEM)


def device(x, core, y, z):
    return ((x % 2) * 2 + core) * 32 + ((z % 4) * 4 + y % 4) * 2 + x // 2


def everyone():
    return [(x, c, y, z) for x in range(4) for c in range(2) for y in range(4) for z in range(4)]


def pairs_of(rule):
    pairs = [(device(*d), device(*rule(*d))) for d in everyone()]
    assert sorted(t for _, t in pairs) == list(range(128))
    assert all(s != t for s, t in pairs)
    return pairs


def send(value, pairs):
    return lax.ppermute(value, AXES, pairs)


def other_core():
    return pairs_of(lambda x, c, y, z: (x, 1 - c, y, z))


def state_first():
    def rule(x, c, y, z):
        t = {(0, 0): (0, 1), (0, 1): (1, 1), (1, 0): (0, 0), (1, 1): (1, 0)}[(x // 2, c)]
        return (2 * t[0] + x % 2, t[1], y, z)

    return pairs_of(rule)


def state_second():
    return [
        (device(x, c, y, z), device((x + 2) % 4, 1 - c, y, z)) for x, c, y, z in everyone() if x // 2 != c
    ]


def across(by):
    return pairs_of(lambda x, c, y, z: ((x + by) % 4, c, y, z))


def rolled(by_low, by_high):
    def rule(x, c, y, z):
        j = (4 * z + y + (by_high if x // 2 else by_low)) % 16
        return (x, c, j % 4, j // 4)

    return pairs_of(rule)


def z_plus(pair, d, lane):
    a, b = pair
    ra, rb = pltpu.roll(a, HALF - d, 1), pltpu.roll(b, HALF - d, 1)
    keep = lane < HALF - d
    return jnp.where(keep, ra, rb), jnp.where(keep, rb, 0.0)


def z_minus(pair, d, lane):
    a, b = pair
    ra, rb = pltpu.roll(a, d, 1), pltpu.roll(b, d, 1)
    keep = lane >= d
    return jnp.where(keep, ra, 0.0), jnp.where(keep, rb, ra)


def second_z(pair, lane):
    out = [second_coef[0] * v for v in pair]
    for d in range(1, 5):
        up, down = z_plus(pair, d, lane), z_minus(pair, d, lane)
        out = [o + second_coef[d] * (u + w) for o, u, w in zip(out, up, down)]
    return out


def first_z(pair, lane):
    out = None
    for d in range(1, 5):
        up, down = z_plus(pair, d, lane), z_minus(pair, d, lane)
        term = [first_coef[d - 1] * (u - w) for u, w in zip(up, down)]
        out = term if out is None else [o + t for o, t in zip(out, term)]
    return out


def second_y(pair, row):
    out = []
    for f in pair:
        acc = second_coef[0] * f
        for d in range(1, 5):
            up = jnp.where(row < AY - d, pltpu.roll(f, AY - d, 0), 0.0)
            down = jnp.where(row >= d, pltpu.roll(f, d, 0), 0.0)
            acc = acc + second_coef[d] * (up + down)
        out.append(acc)
    return out


def x_parts(rows):
    second, first = [], []
    for s in range(2):
        acc = second_coef[0] * rows[4][s]
        der = None
        for d in range(1, 5):
            acc = acc + second_coef[d] * (rows[4 + d][s] + rows[4 - d][s])
            term = first_coef[d - 1] * (rows[4 + d][s] - rows[4 - d][s])
            der = term if der is None else der + term
        second.append(acc)
        first.append(der)
    return second, first


CORE, X_HI, BLOCK, STAYS, PARITY_LAST, PARITY_FREE, GROUP = range(7)
PARITY, ROLE_TO, SIDE, SOURCE, OWNER, ROLE_FROM = 12, 16, 20, 24, 28, 32


def plan_values(ids, offsets):
    shot, aper = ids[0], ids[1]
    core, x_lo, x_hi = shot & 1, shot >> 1, aper & 1
    x = 2 * x_hi + x_lo
    z, y = aper >> 3, (aper >> 1) & 3
    block = 4 * z + y
    turns = [o & 31 for o in offsets]

    def of(values, g):
        return jnp.where(g < 2, jnp.where(g == 0, values[0], values[1]), jnp.where(g == 2, values[2], values[3]))

    def first(flags):
        return jnp.where(flags[0], 0, jnp.where(flags[1], 1, jnp.where(flags[2], 2, 3)))

    def group_of(x):
        return 2 * (x & 1) + (x >> 1)

    last = first([t == 31 for t in turns])
    free = 6 - first([o == 0 for o in offsets]) - first([o == 96 for o in offsets]) - last
    free_turn = of(turns, free)

    def role_of(g):
        return jnp.where(g == last, 1, jnp.where((g == free) & (free_turn != 0), 2, 0))

    def row_of(g):
        o = of(offsets, g)
        return (o + 2 * block + (x_hi ^ (o & 1))) >> 5

    def parity_before(g):
        o = of(offsets, g)
        return ((o >> 5) + (2 * block + x_hi < (o & 31)).astype(jnp.int32)) & 1

    group = group_of(x)
    offset = of(offsets, group)
    out = {
        CORE: core,
        X_HI: x_hi,
        BLOCK: block,
        GROUP: group,
        STAYS: (x_hi == core).astype(jnp.int32),
        PARITY_LAST: parity_before(last),
        PARITY_FREE: parity_before(free),
    }
    for by in range(4):
        to, came = group_of((x + by) & 3), group_of((x - by) & 3)
        out[PARITY + by] = parity_before(to)
        out[ROLE_TO + by] = role_of(to)
        out[SIDE + by] = (((x + by) & 3) >> 1) ^ (offset & 1)
        out[OWNER + by] = row_of(came) - 2 * x_lo
        out[ROLE_FROM + by] = role_of(came)
    for h in range(2):
        row = (offset + 2 * block + h) >> 5
        out[SOURCE + h] = (x - (2 * (h ^ (offset & 1)) + (row >> 1))) & 3
    return out, free_turn


def fetch(which, choices, sems):
    for k, (a, b, out) in enumerate(choices):

        @pl.when(which)
        def _(a=a, out=out, k=k):
            pltpu.make_async_copy(a, out, sems.at[k]).start()

        @pl.when(jnp.logical_not(which))
        def _(b=b, out=out, k=k):
            pltpu.make_async_copy(b, out, sems.at[k]).start()

    return [pltpu.make_async_copy(a, out, sems.at[k]) for k, (a, _, out) in enumerate(choices)]


def plan_kernel(ids, offsets, velocity, epsilon, delta, angle, plan, turn_z, turn_y, own, other, sems):
    copies = fetch(
        ids[0] & 1 == 0,
        (
            (delta, velocity, other.at[0]),
            (angle, epsilon, other.at[1]),
            (velocity, delta, own.at[0]),
            (epsilon, angle, own.at[1]),
        ),
        sems,
    )
    values, free_turn = plan_values(ids, [offsets[g] for g in range(4)])
    for k, v in values.items():
        plan[k] = v
    turn_z[0] = free_turn >> 3
    turn_y[0] = free_turn & 7
    for copy in copies:
        copy.wait()


def state_kernel(plan, fwd_now, adj_now, fwd_before, adj_before, one, two, sems):
    copies = fetch(
        plan[X_HI] == 0,
        (
            (adj_now.at[0], fwd_now.at[0], one.at[0]),
            (fwd_now.at[0], adj_now.at[0], two.at[0]),
            (adj_before.at[0], fwd_before.at[0], one.at[1]),
            (fwd_before.at[0], adj_before.at[0], two.at[1]),
        ),
        sems,
    )
    for copy in copies:
        copy.wait()


def rows_kernel(plan, own, came, last, free):
    mine_last, mine_free = plan[PARITY_LAST] == plan[CORE], plan[PARITY_FREE] == plan[CORE]
    for f in range(2):
        for i in range(TX):
            a, b = own[f, i], came[f, i]
            last[f, i] = jnp.where(mine_last, a, b)
            free[f, i] = jnp.where(mine_free, a, b)


def send_kernel(plan, own, came, last, last_came, free_came, kept, one, two, *outs):
    first, stays = plan[CORE] == 0, plan[STAYS] == 1
    for t in range(2):
        lo, hi = outs[4 + 2 * t : 6 + 2 * t]
        for p in range(2):
            for i in range(TX):
                a, b = one[t, p, i], jnp.where(stays, kept[t, p, i], two[t, p, i])
                lo[p, i] = jnp.where(first, b, a)
                hi[p, i] = jnp.where(first, a, b)
    high = plan[X_HI] == 1
    mine = [plan[PARITY + by] == plan[CORE] for by in range(4)]
    role = [plan[ROLE_TO + by] for by in range(4)]
    for f in range(2):
        for i in range(TX):
            a, b = own[f, i], came[f, i]
            turned_last = jnp.where(high, last_came[f, i], last[f, i])
            turned_free = free_came[f, i]
            for by in range(4):
                straight = jnp.where(mine[by], a, b)
                turned = jnp.where(role[by] == 1, turned_last, turned_free)
                outs[by][f, i] = jnp.where(role[by] == 0, straight, turned)


def tiles_kernel(plan, kept, got_1, got_2, got_3, low, high, out):
    del low, high
    source = [plan[SOURCE + h] for h in range(2)]
    for f in range(2):
        for i in range(TX):
            rows = [kept[f, i], got_1[f, i], got_2[f, i], got_3[f, i]]
            for h in range(2):
                a = jnp.where(source[h] == 0, rows[0], rows[1])
                b = jnp.where(source[h] == 2, rows[2], rows[3])
                out[h, f, i] = jnp.where(source[h] < 2, a, b)


def fill_rows(plan, lo, hi, low, high, ext):
    first, last = plan[BLOCK] == 0, plan[BLOCK] == 15
    for p in range(2):
        for i in range(TX):
            ext[p, i] = jnp.where(first, 0.0, low[p, i])
            ext[p, TX + i] = lo[p, i]
            ext[p, 2 * TX + i] = hi[p, i]
            ext[p, 3 * TX + i] = jnp.where(last, 0.0, high[p, i])


def step_kernel(plan, lo, hi, lo_b, hi_b, low, high, coef, inj, new_lo, new_hi, *rest):
    packed, ext = (rest[0], rest[1]) if len(rest) == 2 else (None, rest[0])
    fill_rows(plan, lo, hi, low, high, ext)
    for t, (back, mid, out) in enumerate(((lo_b, lo, new_lo), (hi_b, hi, new_hi))):

        def tile(i, carry, t=t, back=back, mid=mid, out=out):
            def emit(h, new_p, new_q):
                out[0, i, :, h] = new_p
                out[1, i, :, h] = new_q
                if packed is not None:
                    packed[0, t, i, :, h] = mid[0, i, :, h]
                    packed[1, t, i, :, h] = new_p

            one_row(ext, t * TX + i, lambda p, h: back[p, i, :, h], coef, inj, emit)
            return carry

        lax.fori_loop(0, TX, tile, 0)


def one_row(ext, i, before, coef, inj, emit):
    lane = lax.broadcasted_iota(jnp.int32, (AY, HALF), 1)
    row = lax.broadcasted_iota(jnp.int32, (AY, HALF), 0)
    halves = (pl.ds(0, HALF), pl.ds(HALF, HALF))
    parts = []
    for p in range(2):
        rows = [[ext[p, i + d, :, h] for h in halves] for d in range(9)]
        curve_x, slope_x = x_parts(rows)
        parts.append((rows[4], curve_x, second_z(rows[4], lane), first_z(slope_x, lane)))
    (mid_p, xp, zp, cp), (mid_q, xq, zq, cq) = parts
    yp = second_y(mid_p, row)
    for s, h in enumerate(halves):
        aniso, coupled, square = coef[0, i, :, h], coef[1, i, :, h], coef[2, i, :, h]
        sine, cosine, double = coef[3, i, :, h], coef[4, i, :, h], coef[5, i, :, h]
        axial_p = sine * xp[s] + cosine * zp[s] + double * cp[s]
        plane_p = xp[s] + yp[s] + zp[s] - axial_p
        axial_q = sine * xq[s] + cosine * zq[s] + double * cq[s]
        add = inj[i, :, h]
        new_p = 2.0 * mid_p[s] - before(0, h) + aniso * plane_p + coupled * axial_q + add
        new_q = 2.0 * mid_q[s] - before(1, h) + coupled * plane_p + square * axial_q + add
        emit(h, new_p, new_q)


def last_kernel(plan, lo, hi, lo_b, hi_b, low, high, coef, inj, other, keep, give, ext, part):
    fill_rows(plan, lo, hi, low, high, ext)
    for t, (back, mid) in enumerate(((lo_b, lo), (hi_b, hi))):

        def tile(i, carry, t=t, back=back, mid=mid):
            def emit(h, new_p, new_q):
                part[t, i, :, h] = new_p * other[0, t, i, :, h] + mid[0, i, :, h] * other[1, t, i, :, h]

            one_row(ext, t * TX + i, lambda p, h: back[p, i, :, h], coef, inj, emit)
            return carry

        lax.fori_loop(0, TX, tile, 0)
    first = plan[CORE] == 0
    for t in range(2):
        for i in range(TX):
            low_y, high_y = part[t, i, :HALF_Y], part[t, i, HALF_Y:]
            keep[t, i] = jnp.where(first, low_y, high_y)
            give[t, i] = jnp.where(first, high_y, low_y)


def total_kernel(plan, keep, came, *outs):
    for i in range(TX):
        lo = keep[0, i] + came[0, i]
        hi = keep[1, i] + came[1, i]
        for by in range(4):
            outs[by][i] = jnp.where(plan[SIDE + by] == 0, lo, hi)


def owners_kernel(plan, kept, got_1, got_2, got_3, straight, last, free):
    for i in range(TX):
        parts = [kept[i], got_1[i], got_2[i], got_3[i]]
        for k, out in enumerate((straight, last, free)):
            for core in range(2):
                acc = jnp.zeros_like(parts[0])
                for by in range(4):
                    ours = (plan[OWNER + by] == core) & (plan[ROLE_FROM + by] == k)
                    acc = acc + jnp.where(ours, parts[by], 0.0)
                out[core, i] = acc


def image_kernel(plan, straight, last, last_came, free_came, keep, give):
    high, first = plan[X_HI] == 1, plan[CORE] == 0
    for i in range(TX):
        sums = []
        for core in range(2):
            turned = jnp.where(high, last_came[core, i], last[core, i])
            sums.append(straight[core, i] + turned + free_came[core, i])
        keep[i] = jnp.where(first, sums[0], sums[1])
        give[i] = jnp.where(first, sums[1], sums[0])


def join_kernel(plan, keep, came, out):
    first = plan[CORE] == 0
    for i in range(TX):
        out[i, :HALF_Y] = jnp.where(first, keep[i], came[i])
        out[i, HALF_Y:] = jnp.where(first, came[i], keep[i])


def inject_kernel(plan, source, wavelet, cells, traces, *outs):
    group, forward, base = plan[GROUP], plan[CORE] == 0, 8 * plan[BLOCK]
    count = cells.shape[2]
    lane = lax.broadcasted_iota(jnp.int32, (1, count), 1)
    x, y, depth = (
        jnp.where(
            forward,
            jnp.where(lane == 0, source[group, f], -1),
            cells[f, pl.ds(group, 1), :],
        )
        for f in range(3)
    )
    here = (x >= base) & (x < base + 8)
    spot = jnp.where(here, (x - base) * AY + y, -1)
    which = (lax.broadcasted_iota(jnp.int32, (8 * AY, count), 0) == spot).astype(F32)
    level = lax.broadcasted_iota(jnp.int32, (AZ, count), 0) == depth
    for k in range(STEPS):
        amounts = jnp.where(forward, wavelet[group, k], traces[group, pl.ds(k, 1), :])
        values = jnp.where(level, amounts, 0.0)
        flat = lax.dot_general(
            which,
            values,
            (((1,), (1,)), ((), ())),
            precision=lax.Precision.HIGHEST,
            preferred_element_type=F32,
        )
        for i in range(8):
            outs[k][i] = flat[i * AY : (i + 1) * AY, :]


def sine_cosine(angle):
    sq = angle * angle
    sine = -1.0 / 39916800.0
    for c in (1.0 / 362880.0, -1.0 / 5040.0, 1.0 / 120.0, -1.0 / 6.0, 1.0):
        sine = sine * sq + c
    cosine = 1.0 / 479001600.0
    for c in (-1.0 / 3628800.0, 1.0 / 40320.0, -1.0 / 720.0, 1.0 / 24.0, -0.5, 1.0):
        cosine = cosine * sq + c
    return sine * angle, cosine


def coef_kernel(plan, own, other, out):
    core = plan[CORE]
    for t in range(2):

        def tile(i, carry, t=t):
            mine = [own[t, f, i] for f in range(2)]
            theirs = [other[t, f, i] for f in range(2)]
            velocity = jnp.where(core == 0, mine[0], theirs[0])
            epsilon = jnp.where(core == 0, mine[1], theirs[1])
            delta = jnp.where(core == 0, theirs[0], mine[0])
            angle = jnp.where(core == 0, theirs[1], mine[1])
            square = velocity * velocity
            sine, cosine = sine_cosine(angle)
            k = t * TX + i
            out[0, k] = square * (1.0 + 2.0 * epsilon)
            out[1, k] = square * jnp.sqrt(1.0 + 2.0 * delta)
            out[2, k] = square
            out[3, k] = sine * sine
            out[4, k] = cosine * cosine
            out[5, k] = 2.0 * sine * cosine
            return carry

        lax.fori_loop(0, TX, tile, 0)


HBM = pl.BlockSpec(memory_space=pltpu.HBM)
LIMIT = pltpu.CompilerParams(vmem_limit_bytes=4 * 1024 * 1024)


def in_hbm(value):
    return pltpu.with_memory_space_constraint(value, pltpu.HBM)


def call(kernel, n_in, outs, scratch=()):
    return pl.pallas_call(
        kernel,
        out_shape=[jax.ShapeDtypeStruct(s, F32) for s in outs],
        in_specs=[SMEM] + [VMEM] * n_in,
        out_specs=[VMEM] * len(outs),
        scratch_shapes=[pltpu.VMEM(s, F32) for s in scratch],
        compiler_params=LIMIT,
    )


TILE = (2, TX, AY, AZ)
PART = (TX, HALF_Y, AZ)


def turn(value, x_hi, turn_z, turn_y, sign):
    def roll(v, by):
        return send(v, rolled(sign * by, sign * by)) if by else v

    def columns(v, r):
        if r == 1:
            return jnp.where(x_hi == 1, v, roll(v, 1))
        if r % 2 == 0:
            return roll(v, r // 2)
        return send(v, rolled(sign * (r // 2 + 1), sign * (r // 2)))

    value = lax.switch(turn_z[0], [lambda v, k=k: roll(v, 4 * k) for k in range(4)], value)
    return lax.switch(turn_y[0], [lambda v, r=r: columns(v, r) for r in range(8)], value)


def local(
    velocity,
    thomsen_epsilon,
    thomsen_delta,
    tilt_angle,
    fwd_now,
    fwd_before,
    adj_now,
    adj_before,
    wavelet,
    traces,
    offsets,
    source_cell,
    receiver_cell,
):
    shot, aper = lax.axis_index("shot"), lax.axis_index("aper")
    ids = jnp.stack([shot, aper]).astype(jnp.int32)
    swap, up, down = other_core(), rolled(1, 1), rolled(-1, -1)

    plan, turn_z, turn_y, own, other = pl.pallas_call(
        plan_kernel,
        out_shape=[jax.ShapeDtypeStruct((n,), jnp.int32) for n in (40, 1, 1)] + [jax.ShapeDtypeStruct(TILE, F32)] * 2,
        in_specs=[SMEM] * 2 + [HBM] * 4,
        out_specs=[SMEM] * 3 + [VMEM] * 2,
        scratch_shapes=[pltpu.SemaphoreType.DMA((4,))],
        compiler_params=LIMIT,
    )(ids, offsets, *(in_hbm(v) for v in (velocity, thomsen_epsilon, thomsen_delta, tilt_angle)))
    came = send(other, swap)
    one, two = pl.pallas_call(
        state_kernel,
        out_shape=[jax.ShapeDtypeStruct((2,) + TILE, F32)] * 2,
        in_specs=[SMEM] + [HBM] * 4,
        out_specs=[VMEM] * 2,
        scratch_shapes=[pltpu.SemaphoreType.DMA((4,))],
        compiler_params=LIMIT,
    )(plan, *(in_hbm(v) for v in (fwd_now, adj_now, fwd_before, adj_before)))
    got_one, got_two = send(one, state_first()), send(two, state_second())

    last, free = call(rows_kernel, 2, [TILE] * 2)(plan, own, came)
    last_came = send(last, up)
    free_came = turn(free, aper % 2, turn_z, turn_y, -1)
    *rows, lo, hi, lo_b, hi_b = call(send_kernel, 8, [TILE] * 8)(
        plan, own, came, last, last_came, free_came, two, got_one, got_two
    )
    got = [send(rows[by], across(by)) for by in range(1, 4)]
    low, high = send(hi, up), send(lo, down)
    tiles = call(tiles_kernel, 6, [(2,) + TILE])(plan, rows[0], *got, low, high)[0]
    coef = call(coef_kernel, 2, [(6, 8, AY, AZ)])(plan, tiles, send(tiles, swap))[0]

    inj = pl.pallas_call(
        inject_kernel,
        out_shape=[jax.ShapeDtypeStruct((8, AY, AZ), F32)] * STEPS,
        in_specs=[SMEM] * 3 + [VMEM] * 2,
        out_specs=[VMEM] * STEPS,
        compiler_params=LIMIT,
    )(plan, source_cell, wavelet, jnp.transpose(receiver_cell, (2, 0, 1)), traces)

    shared = None
    for k in range(STEPS - 1):
        if k > 0:
            low, high = send(hi, up), send(lo, down)
        outs = [TILE, TILE] + ([(2, 2, TX, AY, AZ)] if k == 1 else [])
        new = call(step_kernel, 8, outs, [(2, 4 * TX, AY, AZ)])(
            plan, lo, hi, lo_b, hi_b, low, high, coef, inj[k]
        )
        if k == 1:
            shared = send(new[2], swap)
        lo_b, hi_b, lo, hi = lo, hi, new[0], new[1]
    low, high = send(hi, up), send(lo, down)
    keep, give = call(
        last_kernel, 9, [(2,) + PART] * 2, [(2, 4 * TX, AY, AZ), (2, TX, AY, AZ)]
    )(plan, lo, hi, lo_b, hi_b, low, high, coef, inj[STEPS - 1], shared)

    parts = call(total_kernel, 2, [PART] * 4)(plan, keep, send(give, swap))
    got = [send(parts[by], across(by)) for by in range(1, 4)]
    straight, last, free = call(owners_kernel, 4, [(2,) + PART] * 3)(plan, parts[0], *got)
    last_came = send(last, down)
    free_came = turn(free, aper % 2, turn_z, turn_y, 1)
    keep, give = call(image_kernel, 4, [PART] * 2)(plan, straight, last, last_came, free_came)
    return call(join_kernel, 2, [(TX, AY, AZ)])(plan, keep, send(give, swap))[0]


def solution(mesh):
    model = P(("shot", "aper"), None, None)
    field = P("shot", None, "aper", None, None)
    return jax.shard_map(
        local,
        mesh=mesh,
        in_specs=(model,) * 4 + (field,) * 4 + (P(),) * 5,
        out_specs=model,
        check_vma=False,
    )
```

```python
import jax
import jax.numpy as jnp
from jax import lax
from jax.experimental import pallas as pl
from jax.experimental.pallas import tpu as pltpu
from jax.sharding import PartitionSpec as P

second_coef = (-205.0 / 72.0, 8.0 / 5.0, -1.0 / 5.0, 8.0 / 315.0, -1.0 / 560.0)
first_coef = (4.0 / 5.0, -1.0 / 5.0, 4.0 / 105.0, -1.0 / 280.0)

AXES = ("shot", "aper")
STEPS = 4
TX = 4
AY = 32
AZ = 256
HALF = 128
HALF_Y = AY // 2
F32 = jnp.float32
VMEM = pl.BlockSpec(memory_space=pltpu.VMEM)
SMEM = pl.BlockSpec(memory_space=pltpu.SMEM)


def device(x, core, y, z):
    return ((x % 2) * 2 + core) * 32 + ((z % 4) * 4 + y % 4) * 2 + x // 2


def everyone():
    return [(x, c, y, z) for x in range(4) for c in range(2) for y in range(4) for z in range(4)]


def pairs_of(rule):
    pairs = [(device(*d), device(*rule(*d))) for d in everyone()]
    assert sorted(t for _, t in pairs) == list(range(128))
    assert all(s != t for s, t in pairs)
    return pairs


def send(value, pairs):
    return lax.ppermute(value, AXES, pairs)


def other_core():
    return pairs_of(lambda x, c, y, z: (x, 1 - c, y, z))


def state_first():
    def rule(x, c, y, z):
        t = {(0, 0): (0, 1), (0, 1): (1, 1), (1, 0): (0, 0), (1, 1): (1, 0)}[(x // 2, c)]
        return (2 * t[0] + x % 2, t[1], y, z)

    return pairs_of(rule)


def state_second():
    return [
        (device(x, c, y, z), device((x + 2) % 4, 1 - c, y, z)) for x, c, y, z in everyone() if x // 2 != c
    ]


def across(by):
    return pairs_of(lambda x, c, y, z: ((x + by) % 4, c, y, z))


def rolled(by_low, by_high):
    def rule(x, c, y, z):
        j = (4 * z + y + (by_high if x // 2 else by_low)) % 16
        return (x, c, j % 4, j // 4)

    return pairs_of(rule)


def z_plus(pair, d, lane):
    a, b = pair
    ra, rb = pltpu.roll(a, HALF - d, 1), pltpu.roll(b, HALF - d, 1)
    keep = lane < HALF - d
    return jnp.where(keep, ra, rb), jnp.where(keep, rb, 0.0)


def z_minus(pair, d, lane):
    a, b = pair
    ra, rb = pltpu.roll(a, d, 1), pltpu.roll(b, d, 1)
    keep = lane >= d
    return jnp.where(keep, ra, 0.0), jnp.where(keep, rb, ra)


def second_z(pair, lane):
    out = [second_coef[0] * v for v in pair]
    for d in range(1, 5):
        up, down = z_plus(pair, d, lane), z_minus(pair, d, lane)
        out = [o + second_coef[d] * (u + w) for o, u, w in zip(out, up, down)]
    return out


def first_z(pair, lane):
    out = None
    for d in range(1, 5):
        up, down = z_plus(pair, d, lane), z_minus(pair, d, lane)
        term = [first_coef[d - 1] * (u - w) for u, w in zip(up, down)]
        out = term if out is None else [o + t for o, t in zip(out, term)]
    return out


def second_y(pair, row):
    out = []
    for f in pair:
        acc = second_coef[0] * f
        for d in range(1, 5):
            up = jnp.where(row < AY - d, pltpu.roll(f, AY - d, 0), 0.0)
            down = jnp.where(row >= d, pltpu.roll(f, d, 0), 0.0)
            acc = acc + second_coef[d] * (up + down)
        out.append(acc)
    return out


def x_parts(rows):
    second, first = [], []
    for s in range(2):
        acc = second_coef[0] * rows[4][s]
        der = None
        for d in range(1, 5):
            acc = acc + second_coef[d] * (rows[4 + d][s] + rows[4 - d][s])
            term = first_coef[d - 1] * (rows[4 + d][s] - rows[4 - d][s])
            der = term if der is None else der + term
        second.append(acc)
        first.append(der)
    return second, first


CORE, X_HI, BLOCK, STAYS, PARITY_LAST, PARITY_FREE, GROUP = range(7)
PARITY, ROLE_TO, SIDE, SOURCE, OWNER, ROLE_FROM = 12, 16, 20, 24, 28, 32


def plan_values(ids, offsets):
    shot, aper = ids[0], ids[1]
    core, x_lo, x_hi = shot & 1, shot >> 1, aper & 1
    x = 2 * x_hi + x_lo
    z, y = aper >> 3, (aper >> 1) & 3
    block = 4 * z + y
    turns = [o & 31 for o in offsets]

    def of(values, g):
        return jnp.where(g < 2, jnp.where(g == 0, values[0], values[1]), jnp.where(g == 2, values[2], values[3]))

    def first(flags):
        return jnp.where(flags[0], 0, jnp.where(flags[1], 1, jnp.where(flags[2], 2, 3)))

    def group_of(x):
        return 2 * (x & 1) + (x >> 1)

    last = first([t == 31 for t in turns])
    free = 6 - first([o == 0 for o in offsets]) - first([o == 96 for o in offsets]) - last
    free_turn = of(turns, free)

    def role_of(g):
        return jnp.where(g == last, 1, jnp.where((g == free) & (free_turn != 0), 2, 0))

    def row_of(g):
        o = of(offsets, g)
        return (o + 2 * block + (x_hi ^ (o & 1))) >> 5

    def parity_before(g):
        o = of(offsets, g)
        return ((o >> 5) + (2 * block + x_hi < (o & 31)).astype(jnp.int32)) & 1

    group = group_of(x)
    offset = of(offsets, group)
    out = {
        CORE: core,
        X_HI: x_hi,
        BLOCK: block,
        GROUP: group,
        STAYS: (x_hi == core).astype(jnp.int32),
        PARITY_LAST: parity_before(last),
        PARITY_FREE: parity_before(free),
    }
    for by in range(4):
        to, came = group_of((x + by) & 3), group_of((x - by) & 3)
        out[PARITY + by] = parity_before(to)
        out[ROLE_TO + by] = role_of(to)
        out[SIDE + by] = (((x + by) & 3) >> 1) ^ (offset & 1)
        out[OWNER + by] = row_of(came) - 2 * x_lo
        out[ROLE_FROM + by] = role_of(came)
    for h in range(2):
        row = (offset + 2 * block + h) >> 5
        out[SOURCE + h] = (x - (2 * (h ^ (offset & 1)) + (row >> 1))) & 3
    return out, free_turn


def fetch(which, choices, sems):
    for k, (a, b, out) in enumerate(choices):

        @pl.when(which)
        def _(a=a, out=out, k=k):
            pltpu.make_async_copy(a, out, sems.at[k]).start()

        @pl.when(jnp.logical_not(which))
        def _(b=b, out=out, k=k):
            pltpu.make_async_copy(b, out, sems.at[k]).start()

    return [pltpu.make_async_copy(a, out, sems.at[k]) for k, (a, _, out) in enumerate(choices)]


def plan_kernel(ids, offsets, velocity, epsilon, delta, angle, plan, turn_all, turn_z, turn_y, own, other, sems):
    copies = fetch(
        ids[0] & 1 == 0,
        (
            (delta, velocity, other.at[0]),
            (angle, epsilon, other.at[1]),
            (velocity, delta, own.at[0]),
            (epsilon, angle, own.at[1]),
        ),
        sems,
    )
    values, free_turn = plan_values(ids, [offsets[g] for g in range(4)])
    for k, v in values.items():
        plan[k] = v
    turn_all[0] = free_turn
    turn_z[0] = free_turn >> 3
    turn_y[0] = free_turn & 7
    for copy in copies:
        copy.wait()


def state_kernel(plan, fwd_now, adj_now, fwd_before, adj_before, one, two, sems):
    copies = fetch(
        plan[X_HI] == 0,
        (
            (adj_now.at[0], fwd_now.at[0], one.at[0]),
            (fwd_now.at[0], adj_now.at[0], two.at[0]),
            (adj_before.at[0], fwd_before.at[0], one.at[1]),
            (fwd_before.at[0], adj_before.at[0], two.at[1]),
        ),
        sems,
    )
    for copy in copies:
        copy.wait()


def rows_kernel(plan, own, came, last, free):
    mine_last, mine_free = plan[PARITY_LAST] == plan[CORE], plan[PARITY_FREE] == plan[CORE]
    for f in range(2):
        for i in range(TX):
            a, b = own[f, i], came[f, i]
            last[f, i] = jnp.where(mine_last, a, b)
            free[f, i] = jnp.where(mine_free, a, b)


def block_kernel(plan, kept, one, two, *outs):
    first, stays = plan[CORE] == 0, plan[STAYS] == 1
    for t in range(2):
        lo, hi = outs[2 * t : 2 + 2 * t]
        for p in range(2):
            for i in range(TX):
                a, b = one[t, p, i], jnp.where(stays, kept[t, p, i], two[t, p, i])
                lo[p, i] = jnp.where(first, b, a)
                hi[p, i] = jnp.where(first, a, b)


def send_kernel(plan, own, came, last, last_came, free_came, *outs):
    high = plan[X_HI] == 1
    mine = [plan[PARITY + by] == plan[CORE] for by in range(4)]
    role = [plan[ROLE_TO + by] for by in range(4)]
    for f in range(2):
        for i in range(TX):
            a, b = own[f, i], came[f, i]
            turned_last = jnp.where(high, last_came[f, i], last[f, i])
            turned_free = free_came[f, i]
            for by in range(4):
                straight = jnp.where(mine[by], a, b)
                turned = jnp.where(role[by] == 1, turned_last, turned_free)
                outs[by][f, i] = jnp.where(role[by] == 0, straight, turned)


def tiles_kernel(plan, kept, got_1, got_2, got_3, low, high, out):
    del low, high
    source = [plan[SOURCE + h] for h in range(2)]
    for f in range(2):
        for i in range(TX):
            rows = [kept[f, i], got_1[f, i], got_2[f, i], got_3[f, i]]
            for h in range(2):
                a = jnp.where(source[h] == 0, rows[0], rows[1])
                b = jnp.where(source[h] == 2, rows[2], rows[3])
                out[h, f, i] = jnp.where(source[h] < 2, a, b)


def fill_rows(plan, lo, hi, low, high, ext):
    first, last = plan[BLOCK] == 0, plan[BLOCK] == 15
    for p in range(2):
        for i in range(TX):
            ext[p, i] = jnp.where(first, 0.0, low[p, i])
            ext[p, TX + i] = lo[p, i]
            ext[p, 2 * TX + i] = hi[p, i]
            ext[p, 3 * TX + i] = jnp.where(last, 0.0, high[p, i])


def step_kernel(plan, lo, hi, lo_b, hi_b, low, high, coef, inj, new_lo, new_hi, *rest):
    packed, ext = (rest[0], rest[1]) if len(rest) == 2 else (None, rest[0])
    fill_rows(plan, lo, hi, low, high, ext)
    for t, (back, mid, out) in enumerate(((lo_b, lo, new_lo), (hi_b, hi, new_hi))):

        def tile(i, carry, t=t, back=back, mid=mid, out=out):
            def emit(h, new_p, new_q):
                out[0, i, :, h] = new_p
                out[1, i, :, h] = new_q
                if packed is not None:
                    packed[0, t, i, :, h] = mid[0, i, :, h]
                    packed[1, t, i, :, h] = new_p

            one_row(ext, t * TX + i, lambda p, h: back[p, i, :, h], coef, inj, emit)
            return carry

        lax.fori_loop(0, TX, tile, 0)


def one_row(ext, i, before, coef, inj, emit):
    lane = lax.broadcasted_iota(jnp.int32, (AY, HALF), 1)
    row = lax.broadcasted_iota(jnp.int32, (AY, HALF), 0)
    halves = (pl.ds(0, HALF), pl.ds(HALF, HALF))
    parts = []
    for p in range(2):
        rows = [[ext[p, i + d, :, h] for h in halves] for d in range(9)]
        curve_x, slope_x = x_parts(rows)
        parts.append((rows[4], curve_x, second_z(rows[4], lane), first_z(slope_x, lane)))
    (mid_p, xp, zp, cp), (mid_q, xq, zq, cq) = parts
    yp = second_y(mid_p, row)
    for s, h in enumerate(halves):
        aniso, coupled, square = coef[0, i, :, h], coef[1, i, :, h], coef[2, i, :, h]
        sine, cosine, double = coef[3, i, :, h], coef[4, i, :, h], coef[5, i, :, h]
        axial_p = sine * xp[s] + cosine * zp[s] + double * cp[s]
        plane_p = xp[s] + yp[s] + zp[s] - axial_p
        axial_q = sine * xq[s] + cosine * zq[s] + double * cq[s]
        add = inj[i, :, h]
        new_p = 2.0 * mid_p[s] - before(0, h) + aniso * plane_p + coupled * axial_q + add
        new_q = 2.0 * mid_q[s] - before(1, h) + coupled * plane_p + square * axial_q + add
        emit(h, new_p, new_q)


def last_kernel(plan, lo, hi, lo_b, hi_b, low, high, coef, inj, other, keep, give, ext, part):
    fill_rows(plan, lo, hi, low, high, ext)
    for t, (back, mid) in enumerate(((lo_b, lo), (hi_b, hi))):

        def tile(i, carry, t=t, back=back, mid=mid):
            def emit(h, new_p, new_q):
                part[t, i, :, h] = new_p * other[0, t, i, :, h] + mid[0, i, :, h] * other[1, t, i, :, h]

            one_row(ext, t * TX + i, lambda p, h: back[p, i, :, h], coef, inj, emit)
            return carry

        lax.fori_loop(0, TX, tile, 0)
    first = plan[CORE] == 0
    for t in range(2):
        for i in range(TX):
            low_y, high_y = part[t, i, :HALF_Y], part[t, i, HALF_Y:]
            keep[t, i] = jnp.where(first, low_y, high_y)
            give[t, i] = jnp.where(first, high_y, low_y)


def total_kernel(plan, keep, came, *outs):
    for i in range(TX):
        lo = keep[0, i] + came[0, i]
        hi = keep[1, i] + came[1, i]
        for by in range(4):
            outs[by][i] = jnp.where(plan[SIDE + by] == 0, lo, hi)


def owners_kernel(plan, kept, got_1, got_2, got_3, straight, last, free):
    for i in range(TX):
        parts = [kept[i], got_1[i], got_2[i], got_3[i]]
        for k, out in enumerate((straight, last, free)):
            for core in range(2):
                acc = jnp.zeros_like(parts[0])
                for by in range(4):
                    ours = (plan[OWNER + by] == core) & (plan[ROLE_FROM + by] == k)
                    acc = acc + jnp.where(ours, parts[by], 0.0)
                out[core, i] = acc


def image_kernel(plan, straight, last, last_came, free_came, keep, give):
    high, first = plan[X_HI] == 1, plan[CORE] == 0
    for i in range(TX):
        sums = []
        for core in range(2):
            turned = jnp.where(high, last_came[core, i], last[core, i])
            sums.append(straight[core, i] + turned + free_came[core, i])
        keep[i] = jnp.where(first, sums[0], sums[1])
        give[i] = jnp.where(first, sums[1], sums[0])


def join_kernel(plan, keep, came, out):
    first = plan[CORE] == 0
    for i in range(TX):
        out[i, :HALF_Y] = jnp.where(first, keep[i], came[i])
        out[i, HALF_Y:] = jnp.where(first, came[i], keep[i])


def inject_kernel(plan, source, wavelet, cells, traces, *outs):
    group, forward, base = plan[GROUP], plan[CORE] == 0, 8 * plan[BLOCK]
    count = cells.shape[2]
    lane = lax.broadcasted_iota(jnp.int32, (1, count), 1)
    x, y, depth = (
        jnp.where(
            forward,
            jnp.where(lane == 0, source[group, f], -1),
            cells[f, pl.ds(group, 1), :],
        )
        for f in range(3)
    )
    here = (x >= base) & (x < base + 8)
    spot = jnp.where(here, (x - base) * AY + y, -1)
    which = (lax.broadcasted_iota(jnp.int32, (8 * AY, count), 0) == spot).astype(F32)
    level = lax.broadcasted_iota(jnp.int32, (AZ, count), 0) == depth
    for k in range(STEPS):
        amounts = jnp.where(forward, wavelet[group, k], traces[group, pl.ds(k, 1), :])
        values = jnp.where(level, amounts, 0.0)
        flat = lax.dot_general(
            which,
            values,
            (((1,), (1,)), ((), ())),
            precision=lax.Precision.HIGHEST,
            preferred_element_type=F32,
        )
        for i in range(8):
            outs[k][i] = flat[i * AY : (i + 1) * AY, :]


def sine_cosine(angle):
    sq = angle * angle
    sine = -1.0 / 39916800.0
    for c in (1.0 / 362880.0, -1.0 / 5040.0, 1.0 / 120.0, -1.0 / 6.0, 1.0):
        sine = sine * sq + c
    cosine = 1.0 / 479001600.0
    for c in (-1.0 / 3628800.0, 1.0 / 40320.0, -1.0 / 720.0, 1.0 / 24.0, -0.5, 1.0):
        cosine = cosine * sq + c
    return sine * angle, cosine


def coef_kernel(plan, own, other, out):
    core = plan[CORE]
    for t in range(2):

        def tile(i, carry, t=t):
            mine = [own[t, f, i] for f in range(2)]
            theirs = [other[t, f, i] for f in range(2)]
            velocity = jnp.where(core == 0, mine[0], theirs[0])
            epsilon = jnp.where(core == 0, mine[1], theirs[1])
            delta = jnp.where(core == 0, theirs[0], mine[0])
            angle = jnp.where(core == 0, theirs[1], mine[1])
            square = velocity * velocity
            sine, cosine = sine_cosine(angle)
            k = t * TX + i
            out[0, k] = square * (1.0 + 2.0 * epsilon)
            out[1, k] = square * jnp.sqrt(1.0 + 2.0 * delta)
            out[2, k] = square
            out[3, k] = sine * sine
            out[4, k] = cosine * cosine
            out[5, k] = 2.0 * sine * cosine
            return carry

        lax.fori_loop(0, TX, tile, 0)


HBM = pl.BlockSpec(memory_space=pltpu.HBM)
LIMIT = pltpu.CompilerParams(vmem_limit_bytes=4 * 1024 * 1024)


def in_hbm(value):
    return pltpu.with_memory_space_constraint(value, pltpu.HBM)


def call(kernel, n_in, outs, scratch=()):
    return pl.pallas_call(
        kernel,
        out_shape=[jax.ShapeDtypeStruct(s, F32) for s in outs],
        in_specs=[SMEM] + [VMEM] * n_in,
        out_specs=[VMEM] * len(outs),
        scratch_shapes=[pltpu.VMEM(s, F32) for s in scratch],
        compiler_params=LIMIT,
    )


TILE = (2, TX, AY, AZ)
PART = (TX, HALF_Y, AZ)


def turn_model(value, x_hi, turn_z, turn_y):
    def roll(v, by):
        return send(v, rolled(-by, -by)) if by else v

    def columns(v, r):
        if r == 1:
            return jnp.where(x_hi == 1, v, roll(v, 1))
        if r % 2 == 0:
            return roll(v, r // 2)
        return send(v, rolled(-(r // 2 + 1), -(r // 2)))

    value = lax.switch(turn_z[0], [lambda v, k=k: roll(v, 4 * k) for k in range(4)], value)
    return lax.switch(turn_y[0], [lambda v, r=r: columns(v, r) for r in range(8)], value)


def turn_image(value, x_hi, free_turn):
    def roll(v, by):
        if by % 16 == 0:
            return v
        return roll(roll(v, 8), 7) if by == 15 else send(v, rolled(by, by))

    def columns(v, r):
        low, high = (r + 1) // 2, r // 2
        if r % 2 == 0:
            return roll(v, high)
        if r in (1, 15, 17, 29, 31):
            return jnp.where(x_hi == 1, roll(v, high), roll(v, low))
        return send(v, rolled(low, high))

    return lax.switch(free_turn[0], [lambda v, r=r: columns(v, r) for r in range(32)], value)


def local(
    velocity,
    thomsen_epsilon,
    thomsen_delta,
    tilt_angle,
    fwd_now,
    fwd_before,
    adj_now,
    adj_before,
    wavelet,
    traces,
    offsets,
    source_cell,
    receiver_cell,
):
    shot, aper = lax.axis_index("shot"), lax.axis_index("aper")
    ids = jnp.stack([shot, aper]).astype(jnp.int32)
    swap, up, down = other_core(), rolled(1, 1), rolled(-1, -1)

    plan, turn_all, turn_z, turn_y, own, other = pl.pallas_call(
        plan_kernel,
        out_shape=[jax.ShapeDtypeStruct((n,), jnp.int32) for n in (40, 1, 1, 1)] + [jax.ShapeDtypeStruct(TILE, F32)] * 2,
        in_specs=[SMEM] * 2 + [HBM] * 4,
        out_specs=[SMEM] * 4 + [VMEM] * 2,
        scratch_shapes=[pltpu.SemaphoreType.DMA((4,))],
        compiler_params=LIMIT,
    )(ids, offsets, *(in_hbm(v) for v in (velocity, thomsen_epsilon, thomsen_delta, tilt_angle)))
    came = send(other, swap)
    one, two = pl.pallas_call(
        state_kernel,
        out_shape=[jax.ShapeDtypeStruct((2,) + TILE, F32)] * 2,
        in_specs=[SMEM] + [HBM] * 4,
        out_specs=[VMEM] * 2,
        scratch_shapes=[pltpu.SemaphoreType.DMA((4,))],
        compiler_params=LIMIT,
    )(plan, *(in_hbm(v) for v in (fwd_now, adj_now, fwd_before, adj_before)))
    got_one, got_two = send(one, state_first()), send(two, state_second())

    last, free = call(rows_kernel, 2, [TILE] * 2)(plan, own, came)
    last_came = send(last, up)
    free_came = turn_model(free, aper % 2, turn_z, turn_y)
    rows = call(send_kernel, 5, [TILE] * 4)(plan, own, came, last, last_came, free_came)
    got = [send(rows[by], across(by)) for by in range(1, 4)]
    lo, hi, lo_b, hi_b = call(block_kernel, 3, [TILE] * 4)(plan, two, got_one, got_two)
    low, high = send(hi, up), send(lo, down)
    tiles = call(tiles_kernel, 6, [(2,) + TILE])(plan, rows[0], *got, low, high)[0]
    coef = call(coef_kernel, 2, [(6, 8, AY, AZ)])(plan, tiles, send(tiles, swap))[0]

    inj = pl.pallas_call(
        inject_kernel,
        out_shape=[jax.ShapeDtypeStruct((8, AY, AZ), F32)] * STEPS,
        in_specs=[SMEM] * 3 + [VMEM] * 2,
        out_specs=[VMEM] * STEPS,
        compiler_params=LIMIT,
    )(plan, source_cell, wavelet, jnp.transpose(receiver_cell, (2, 0, 1)), traces)

    shared = None
    for k in range(STEPS - 1):
        if k > 0:
            low, high = send(hi, up), send(lo, down)
        outs = [TILE, TILE] + ([(2, 2, TX, AY, AZ)] if k == 1 else [])
        new = call(step_kernel, 8, outs, [(2, 4 * TX, AY, AZ)])(
            plan, lo, hi, lo_b, hi_b, low, high, coef, inj[k]
        )
        if k == 1:
            shared = send(new[2], swap)
        lo_b, hi_b, lo, hi = lo, hi, new[0], new[1]
    low, high = send(hi, up), send(lo, down)
    keep, give = call(
        last_kernel, 9, [(2,) + PART] * 2, [(2, 4 * TX, AY, AZ), (2, TX, AY, AZ)]
    )(plan, lo, hi, lo_b, hi_b, low, high, coef, inj[STEPS - 1], shared)

    parts = call(total_kernel, 2, [PART] * 4)(plan, keep, send(give, swap))
    got = [send(parts[by], across(by)) for by in range(1, 4)]
    straight, last, free = call(owners_kernel, 4, [(2,) + PART] * 3)(plan, parts[0], *got)
    last_came = send(last, down)
    free_came = turn_image(free, aper % 2, turn_all)
    keep, give = call(image_kernel, 4, [PART] * 2)(plan, straight, last, last_came, free_came)
    return call(join_kernel, 2, [(TX, AY, AZ)])(plan, keep, send(give, swap))[0]


def solution(mesh):
    model = P(("shot", "aper"), None, None)
    field = P("shot", None, "aper", None, None)
    return jax.shard_map(
        local,
        mesh=mesh,
        in_specs=(model,) * 4 + (field,) * 4 + (P(),) * 5,
        out_specs=model,
        check_vma=False,
    )
```

```python
import jax
import jax.numpy as jnp
from jax import lax
from jax.experimental import pallas as pl
from jax.experimental.pallas import tpu as pltpu
from jax.sharding import PartitionSpec as P

second_coef = (-205.0 / 72.0, 8.0 / 5.0, -1.0 / 5.0, 8.0 / 315.0, -1.0 / 560.0)
first_coef = (4.0 / 5.0, -1.0 / 5.0, 4.0 / 105.0, -1.0 / 280.0)

AXES = ("shot", "aper")
STEPS = 4
TX = 4
AY = 32
AZ = 256
HALF = 128
HALF_Y = AY // 2
F32 = jnp.float32
VMEM = pl.BlockSpec(memory_space=pltpu.VMEM)
SMEM = pl.BlockSpec(memory_space=pltpu.SMEM)


def device(x, core, y, z):
    return ((x % 2) * 2 + core) * 32 + ((z % 4) * 4 + y % 4) * 2 + x // 2


def everyone():
    return [(x, c, y, z) for x in range(4) for c in range(2) for y in range(4) for z in range(4)]


def pairs_of(rule):
    pairs = [(device(*d), device(*rule(*d))) for d in everyone()]
    assert sorted(t for _, t in pairs) == list(range(128))
    assert all(s != t for s, t in pairs)
    return pairs


def send(value, pairs):
    return lax.ppermute(value, AXES, pairs)


def other_core():
    return pairs_of(lambda x, c, y, z: (x, 1 - c, y, z))


def state_first():
    def rule(x, c, y, z):
        t = {(0, 0): (0, 1), (0, 1): (1, 1), (1, 0): (0, 0), (1, 1): (1, 0)}[(x // 2, c)]
        return (2 * t[0] + x % 2, t[1], y, z)

    return pairs_of(rule)


def state_second():
    return [
        (device(x, c, y, z), device((x + 2) % 4, 1 - c, y, z)) for x, c, y, z in everyone() if x // 2 != c
    ]


def across(by):
    return pairs_of(lambda x, c, y, z: ((x + by) % 4, c, y, z))


def rolled(by_low, by_high):
    def rule(x, c, y, z):
        j = (4 * z + y + (by_high if x // 2 else by_low)) % 16
        return (x, c, j % 4, j // 4)

    return pairs_of(rule)


def z_plus(pair, d, lane):
    a, b = pair
    ra, rb = pltpu.roll(a, HALF - d, 1), pltpu.roll(b, HALF - d, 1)
    keep = lane < HALF - d
    return jnp.where(keep, ra, rb), jnp.where(keep, rb, 0.0)


def z_minus(pair, d, lane):
    a, b = pair
    ra, rb = pltpu.roll(a, d, 1), pltpu.roll(b, d, 1)
    keep = lane >= d
    return jnp.where(keep, ra, 0.0), jnp.where(keep, rb, ra)


def second_z(pair, lane):
    out = [second_coef[0] * v for v in pair]
    for d in range(1, 5):
        up, down = z_plus(pair, d, lane), z_minus(pair, d, lane)
        out = [o + second_coef[d] * (u + w) for o, u, w in zip(out, up, down)]
    return out


def first_z(pair, lane):
    out = None
    for d in range(1, 5):
        up, down = z_plus(pair, d, lane), z_minus(pair, d, lane)
        term = [first_coef[d - 1] * (u - w) for u, w in zip(up, down)]
        out = term if out is None else [o + t for o, t in zip(out, term)]
    return out


def second_y(pair, row):
    out = []
    for f in pair:
        acc = second_coef[0] * f
        for d in range(1, 5):
            up = jnp.where(row < AY - d, pltpu.roll(f, AY - d, 0), 0.0)
            down = jnp.where(row >= d, pltpu.roll(f, d, 0), 0.0)
            acc = acc + second_coef[d] * (up + down)
        out.append(acc)
    return out


CORE, X_HI, BLOCK, STAYS, PARITY_LAST, PARITY_FREE, GROUP = range(7)
PARITY, ROLE_TO, SIDE, SOURCE, OWNER, ROLE_FROM = 12, 16, 20, 24, 28, 32


def plan_values(ids, offsets):
    shot, aper = ids[0], ids[1]
    core, x_lo, x_hi = shot & 1, shot >> 1, aper & 1
    x = 2 * x_hi + x_lo
    z, y = aper >> 3, (aper >> 1) & 3
    block = 4 * z + y
    turns = [o & 31 for o in offsets]

    def of(values, g):
        return jnp.where(g < 2, jnp.where(g == 0, values[0], values[1]), jnp.where(g == 2, values[2], values[3]))

    def first(flags):
        return jnp.where(flags[0], 0, jnp.where(flags[1], 1, jnp.where(flags[2], 2, 3)))

    def group_of(x):
        return 2 * (x & 1) + (x >> 1)

    last = first([t == 31 for t in turns])
    free = 6 - first([o == 0 for o in offsets]) - first([o == 96 for o in offsets]) - last
    free_turn = of(turns, free)

    def role_of(g):
        return jnp.where(g == last, 1, jnp.where((g == free) & (free_turn != 0), 2, 0))

    def row_of(g):
        o = of(offsets, g)
        return (o + 2 * block + (x_hi ^ (o & 1))) >> 5

    def parity_before(g):
        o = of(offsets, g)
        return ((o >> 5) + (2 * block + x_hi < (o & 31)).astype(jnp.int32)) & 1

    group = group_of(x)
    offset = of(offsets, group)
    out = {
        CORE: core,
        X_HI: x_hi,
        BLOCK: block,
        GROUP: group,
        STAYS: (x_hi == core).astype(jnp.int32),
        PARITY_LAST: parity_before(last),
        PARITY_FREE: parity_before(free),
    }
    for by in range(4):
        to, came = group_of((x + by) & 3), group_of((x - by) & 3)
        out[PARITY + by] = parity_before(to)
        out[ROLE_TO + by] = role_of(to)
        out[SIDE + by] = (((x + by) & 3) >> 1) ^ (offset & 1)
        out[OWNER + by] = row_of(came) - 2 * x_lo
        out[ROLE_FROM + by] = role_of(came)
    for h in range(2):
        row = (offset + 2 * block + h) >> 5
        out[SOURCE + h] = (x - (2 * (h ^ (offset & 1)) + (row >> 1))) & 3
    return out, free_turn


def fetch(which, choices, sems):
    for k, (a, b, out) in enumerate(choices):

        @pl.when(which)
        def _(a=a, out=out, k=k):
            pltpu.make_async_copy(a, out, sems.at[k]).start()

        @pl.when(jnp.logical_not(which))
        def _(b=b, out=out, k=k):
            pltpu.make_async_copy(b, out, sems.at[k]).start()

    return [pltpu.make_async_copy(a, out, sems.at[k]) for k, (a, _, out) in enumerate(choices)]


def plan_kernel(ids, offsets, velocity, epsilon, delta, angle, plan, turn_all, turn_z, turn_y, own, other, sems):
    copies = fetch(
        ids[0] & 1 == 0,
        (
            (delta, velocity, other.at[0]),
            (angle, epsilon, other.at[1]),
            (velocity, delta, own.at[0]),
            (epsilon, angle, own.at[1]),
        ),
        sems,
    )
    values, free_turn = plan_values(ids, [offsets[g] for g in range(4)])
    for k, v in values.items():
        plan[k] = v
    turn_all[0] = free_turn
    turn_z[0] = free_turn >> 3
    turn_y[0] = free_turn & 7
    for copy in copies:
        copy.wait()


def state_kernel(plan, fwd_now, adj_now, fwd_before, adj_before, one, two, sems):
    copies = fetch(
        plan[X_HI] == 0,
        (
            (adj_now.at[0], fwd_now.at[0], one.at[0]),
            (fwd_now.at[0], adj_now.at[0], two.at[0]),
            (adj_before.at[0], fwd_before.at[0], one.at[1]),
            (fwd_before.at[0], adj_before.at[0], two.at[1]),
        ),
        sems,
    )
    for copy in copies:
        copy.wait()


def rows_kernel(plan, own, came, last, free):
    mine_last, mine_free = plan[PARITY_LAST] == plan[CORE], plan[PARITY_FREE] == plan[CORE]
    for f in range(2):
        for i in range(TX):
            a, b = own[f, i], came[f, i]
            last[f, i] = jnp.where(mine_last, a, b)
            free[f, i] = jnp.where(mine_free, a, b)


def block_kernel(plan, kept, one, two, *outs):
    first, stays = plan[CORE] == 0, plan[STAYS] == 1
    for t in range(2):
        lo, hi = outs[2 * t : 2 + 2 * t]
        for p in range(2):
            for i in range(TX):
                a, b = one[t, p, i], jnp.where(stays, kept[t, p, i], two[t, p, i])
                lo[p, i] = jnp.where(first, b, a)
                hi[p, i] = jnp.where(first, a, b)


def send_kernel(plan, own, came, last, last_came, free_came, *outs):
    high = plan[X_HI] == 1
    mine = [plan[PARITY + by] == plan[CORE] for by in range(4)]
    role = [plan[ROLE_TO + by] for by in range(4)]
    for f in range(2):
        for i in range(TX):
            a, b = own[f, i], came[f, i]
            turned_last = jnp.where(high, last_came[f, i], last[f, i])
            turned_free = free_came[f, i]
            for by in range(4):
                straight = jnp.where(mine[by], a, b)
                turned = jnp.where(role[by] == 1, turned_last, turned_free)
                outs[by][f, i] = jnp.where(role[by] == 0, straight, turned)


def tiles_kernel(plan, kept, got_1, got_2, got_3, low, high, near, inj, out):
    del low, high, near, inj
    source = [plan[SOURCE + h] for h in range(2)]
    for f in range(2):
        for i in range(TX):
            rows = [kept[f, i], got_1[f, i], got_2[f, i], got_3[f, i]]
            for h in range(2):
                a = jnp.where(source[h] == 0, rows[0], rows[1])
                b = jnp.where(source[h] == 2, rows[2], rows[3])
                out[h, f, i] = jnp.where(source[h] < 2, a, b)


HALVES = (pl.ds(0, HALF), pl.ds(HALF, HALF))


def gathered(terms):
    out = None
    for c, pair in terms:
        scaled = [c * v for v in pair]
        out = scaled if out is None else [o + v for o, v in zip(out, scaled)]
    return out


def near_kernel(lo, hi, out):
    lane = lax.broadcasted_iota(jnp.int32, (AY, HALF), 1)
    row = lax.broadcasted_iota(jnp.int32, (AY, HALF), 0)

    def value(p, r):
        ref = (lo, hi)[r // TX]
        return [ref[p, r % TX, :, h] for h in HALVES]

    for r in range(2 * TX):
        for p in range(2):
            mid = value(p, r)
            curve, slope = [(second_coef[0], mid)], []
            for d in range(1, 5):
                if r + d < 2 * TX:
                    curve.append((second_coef[d], value(p, r + d)))
                    slope.append((first_coef[d - 1], value(p, r + d)))
                if r - d >= 0:
                    curve.append((second_coef[d], value(p, r - d)))
                    slope.append((-first_coef[d - 1], value(p, r - d)))
            depth = second_z(mid, lane)
            results = [gathered(curve), gathered(slope), depth]
            if p == 0:
                results.append([a + b for a, b in zip(depth, second_y(mid, row))])
            for k, pair in enumerate(results):
                for h, v in zip(HALVES, pair):
                    out[4 * p + k, r, :, h] = v


def far_rows(plan, near, lo, hi, lo_b, hi_b, low, high, coef, inj, emit):
    lane = lax.broadcasted_iota(jnp.int32, (AY, HALF), 1)
    first = jnp.where(plan[BLOCK] == 0, 0.0, 1.0)
    last = jnp.where(plan[BLOCK] == 15, 0.0, 1.0)
    for r in range(2 * TX):
        t, i = r // TX, r % TX
        mid_ref, back = ((lo, lo_b), (hi, hi_b))[t]
        sums = []
        for p in range(2):
            if t == 0:
                terms = [(d, low, TX + i - d, -1.0, first) for d in range(i + 1, 5)]
            else:
                terms = [(d, high, i + d - TX, 1.0, last) for d in range(TX - i, 5)]
            curve, slope = [], []
            for d, ref, k, sign, inside in terms:
                pair = [ref[p, k, :, h] for h in HALVES]
                curve.append((second_coef[d] * inside, pair))
                slope.append((sign * first_coef[d - 1] * inside, pair))
            curve = [a + near[4 * p, r, :, h] for h, a in zip(HALVES, gathered(curve))]
            slope = [a + near[4 * p + 1, r, :, h] for h, a in zip(HALVES, gathered(slope))]
            sums.append((curve, first_z(slope, lane)))
        (xp, cp), (xq, cq) = sums
        for s, h in enumerate(HALVES):
            aniso, coupled, square = coef[0, r, :, h], coef[1, r, :, h], coef[2, r, :, h]
            sine, cosine, double = coef[3, r, :, h], coef[4, r, :, h], coef[5, r, :, h]
            axial_p = sine * xp[s] + cosine * near[2, r, :, h] + double * cp[s]
            plane_p = xp[s] + near[3, r, :, h] - axial_p
            axial_q = sine * xq[s] + cosine * near[6, r, :, h] + double * cq[s]
            add = inj[r, :, h]
            new_p = 2.0 * mid_ref[0, i, :, h] - back[0, i, :, h] + aniso * plane_p + coupled * axial_q + add
            new_q = 2.0 * mid_ref[1, i, :, h] - back[1, i, :, h] + coupled * plane_p + square * axial_q + add
            emit(t, i, h, new_p, new_q)


def step_kernel(plan, near, lo, hi, lo_b, hi_b, low, high, coef, inj, new_lo, new_hi, *packed):
    def emit(t, i, h, new_p, new_q):
        out = (new_lo, new_hi)[t]
        out[0, i, :, h] = new_p
        out[1, i, :, h] = new_q
        for p in packed:
            p[0, t, i, :, h] = (lo, hi)[t][0, i, :, h]
            p[1, t, i, :, h] = new_p

    far_rows(plan, near, lo, hi, lo_b, hi_b, low, high, coef, inj, emit)


def last_kernel(plan, near, lo, hi, lo_b, hi_b, low, high, coef, inj, other, keep, give, part):
    def emit(t, i, h, new_p, new_q):
        del new_q
        part[t, i, :, h] = new_p * other[0, t, i, :, h] + (lo, hi)[t][0, i, :, h] * other[1, t, i, :, h]

    far_rows(plan, near, lo, hi, lo_b, hi_b, low, high, coef, inj, emit)
    first = plan[CORE] == 0
    for t in range(2):
        for i in range(TX):
            low_y, high_y = part[t, i, :HALF_Y], part[t, i, HALF_Y:]
            keep[t, i] = jnp.where(first, low_y, high_y)
            give[t, i] = jnp.where(first, high_y, low_y)


def total_kernel(plan, keep, came, *outs):
    for i in range(TX):
        lo = keep[0, i] + came[0, i]
        hi = keep[1, i] + came[1, i]
        for by in range(4):
            outs[by][i] = jnp.where(plan[SIDE + by] == 0, lo, hi)


def owners_kernel(plan, kept, got_1, got_2, got_3, straight, last, free):
    for i in range(TX):
        parts = [kept[i], got_1[i], got_2[i], got_3[i]]
        for k, out in enumerate((straight, last, free)):
            for core in range(2):
                acc = jnp.zeros_like(parts[0])
                for by in range(4):
                    ours = (plan[OWNER + by] == core) & (plan[ROLE_FROM + by] == k)
                    acc = acc + jnp.where(ours, parts[by], 0.0)
                out[core, i] = acc


def image_kernel(plan, straight, last, last_came, free_came, keep, give):
    high, first = plan[X_HI] == 1, plan[CORE] == 0
    for i in range(TX):
        sums = []
        for core in range(2):
            turned = jnp.where(high, last_came[core, i], last[core, i])
            sums.append(straight[core, i] + turned + free_came[core, i])
        keep[i] = jnp.where(first, sums[0], sums[1])
        give[i] = jnp.where(first, sums[1], sums[0])


def join_kernel(plan, keep, came, out):
    first = plan[CORE] == 0
    for i in range(TX):
        out[i, :HALF_Y] = jnp.where(first, keep[i], came[i])
        out[i, HALF_Y:] = jnp.where(first, came[i], keep[i])


def inject_kernel(plan, source, wavelet, cells, traces, *outs):
    group, forward, base = plan[GROUP], plan[CORE] == 0, 8 * plan[BLOCK]
    count = cells.shape[2]
    lane = lax.broadcasted_iota(jnp.int32, (1, count), 1)
    x, y, depth = (
        jnp.where(
            forward,
            jnp.where(lane == 0, source[group, f], -1),
            cells[f, pl.ds(group, 1), :],
        )
        for f in range(3)
    )
    here = (x >= base) & (x < base + 8)
    spot = jnp.where(here, (x - base) * AY + y, -1)
    which = (lax.broadcasted_iota(jnp.int32, (8 * AY, count), 0) == spot).astype(F32)
    level = lax.broadcasted_iota(jnp.int32, (AZ, count), 0) == depth
    for k in range(STEPS):
        amounts = jnp.where(forward, wavelet[group, k], traces[group, pl.ds(k, 1), :])
        values = jnp.where(level, amounts, 0.0)
        flat = lax.dot_general(
            which,
            values,
            (((1,), (1,)), ((), ())),
            precision=lax.Precision.HIGHEST,
            preferred_element_type=F32,
        )
        for i in range(8):
            outs[k][i] = flat[i * AY : (i + 1) * AY, :]


def sine_cosine(angle):
    sq = angle * angle
    sine = -1.0 / 39916800.0
    for c in (1.0 / 362880.0, -1.0 / 5040.0, 1.0 / 120.0, -1.0 / 6.0, 1.0):
        sine = sine * sq + c
    cosine = 1.0 / 479001600.0
    for c in (-1.0 / 3628800.0, 1.0 / 40320.0, -1.0 / 720.0, 1.0 / 24.0, -0.5, 1.0):
        cosine = cosine * sq + c
    return sine * angle, cosine


def coef_kernel(plan, own, other, out):
    core = plan[CORE]
    for t in range(2):

        def tile(i, carry, t=t):
            mine = [own[t, f, i] for f in range(2)]
            theirs = [other[t, f, i] for f in range(2)]
            velocity = jnp.where(core == 0, mine[0], theirs[0])
            epsilon = jnp.where(core == 0, mine[1], theirs[1])
            delta = jnp.where(core == 0, theirs[0], mine[0])
            angle = jnp.where(core == 0, theirs[1], mine[1])
            square = velocity * velocity
            sine, cosine = sine_cosine(angle)
            k = t * TX + i
            out[0, k] = square * (1.0 + 2.0 * epsilon)
            out[1, k] = square * jnp.sqrt(1.0 + 2.0 * delta)
            out[2, k] = square
            out[3, k] = sine * sine
            out[4, k] = cosine * cosine
            out[5, k] = 2.0 * sine * cosine
            return carry

        lax.fori_loop(0, TX, tile, 0)


HBM = pl.BlockSpec(memory_space=pltpu.HBM)
LIMIT = pltpu.CompilerParams(vmem_limit_bytes=4 * 1024 * 1024)


def in_hbm(value):
    return pltpu.with_memory_space_constraint(value, pltpu.HBM)


def call(kernel, n_in, outs, scratch=()):
    return pl.pallas_call(
        kernel,
        out_shape=[jax.ShapeDtypeStruct(s, F32) for s in outs],
        in_specs=[SMEM] + [VMEM] * n_in,
        out_specs=[VMEM] * len(outs),
        scratch_shapes=[pltpu.VMEM(s, F32) for s in scratch],
        compiler_params=LIMIT,
    )


TILE = (2, TX, AY, AZ)
PART = (TX, HALF_Y, AZ)


def turn_model(value, x_hi, turn_z, turn_y):
    def roll(v, by):
        return send(v, rolled(-by, -by)) if by else v

    def columns(v, r):
        if r == 1:
            return jnp.where(x_hi == 1, v, roll(v, 1))
        if r % 2 == 0:
            return roll(v, r // 2)
        return send(v, rolled(-(r // 2 + 1), -(r // 2)))

    value = lax.switch(turn_z[0], [lambda v, k=k: roll(v, 4 * k) for k in range(4)], value)
    return lax.switch(turn_y[0], [lambda v, r=r: columns(v, r) for r in range(8)], value)


def turn_image(value, x_hi, free_turn):
    def roll(v, by):
        if by % 16 == 0:
            return v
        return roll(roll(v, 8), 7) if by == 15 else send(v, rolled(by, by))

    def columns(v, r):
        low, high = (r + 1) // 2, r // 2
        if r % 2 == 0:
            return roll(v, high)
        if r in (1, 15, 17, 29, 31):
            return jnp.where(x_hi == 1, roll(v, high), roll(v, low))
        return send(v, rolled(low, high))

    return lax.switch(free_turn[0], [lambda v, r=r: columns(v, r) for r in range(32)], value)


def local(
    velocity,
    thomsen_epsilon,
    thomsen_delta,
    tilt_angle,
    fwd_now,
    fwd_before,
    adj_now,
    adj_before,
    wavelet,
    traces,
    offsets,
    source_cell,
    receiver_cell,
):
    shot, aper = lax.axis_index("shot"), lax.axis_index("aper")
    ids = jnp.stack([shot, aper]).astype(jnp.int32)
    swap, up, down = other_core(), rolled(1, 1), rolled(-1, -1)

    plan, turn_all, turn_z, turn_y, own, other = pl.pallas_call(
        plan_kernel,
        out_shape=[jax.ShapeDtypeStruct((n,), jnp.int32) for n in (40, 1, 1, 1)] + [jax.ShapeDtypeStruct(TILE, F32)] * 2,
        in_specs=[SMEM] * 2 + [HBM] * 4,
        out_specs=[SMEM] * 4 + [VMEM] * 2,
        scratch_shapes=[pltpu.SemaphoreType.DMA((4,))],
        compiler_params=LIMIT,
    )(ids, offsets, *(in_hbm(v) for v in (velocity, thomsen_epsilon, thomsen_delta, tilt_angle)))
    came = send(other, swap)
    one, two = pl.pallas_call(
        state_kernel,
        out_shape=[jax.ShapeDtypeStruct((2,) + TILE, F32)] * 2,
        in_specs=[SMEM] + [HBM] * 4,
        out_specs=[VMEM] * 2,
        scratch_shapes=[pltpu.SemaphoreType.DMA((4,))],
        compiler_params=LIMIT,
    )(plan, *(in_hbm(v) for v in (fwd_now, adj_now, fwd_before, adj_before)))
    got_one, got_two = send(one, state_first()), send(two, state_second())

    last, free = call(rows_kernel, 2, [TILE] * 2)(plan, own, came)
    last_came = send(last, up)
    free_came = turn_model(free, aper % 2, turn_z, turn_y)
    rows = call(send_kernel, 5, [TILE] * 4)(plan, own, came, last, last_came, free_came)
    got = [send(rows[by], across(by)) for by in range(1, 4)]
    lo, hi, lo_b, hi_b = call(block_kernel, 3, [TILE] * 4)(plan, two, got_one, got_two)
    inj = pl.pallas_call(
        inject_kernel,
        out_shape=[jax.ShapeDtypeStruct((8, AY, AZ), F32)] * STEPS,
        in_specs=[SMEM] * 3 + [VMEM] * 2,
        out_specs=[VMEM] * STEPS,
        compiler_params=LIMIT,
    )(plan, source_cell, wavelet, jnp.transpose(receiver_cell, (2, 0, 1)), traces)

    near_call = pl.pallas_call(
        near_kernel,
        out_shape=jax.ShapeDtypeStruct((7, 8, AY, AZ), F32),
        in_specs=[VMEM] * 2,
        out_specs=VMEM,
        compiler_params=LIMIT,
    )
    near = near_call(lo, hi)
    low, high = send(hi, up), send(lo, down)
    tiles = call(tiles_kernel, 8, [(2,) + TILE])(
        plan, rows[0], *got, low, high, near, inj[0]
    )[0]
    coef = call(coef_kernel, 2, [(6, 8, AY, AZ)])(plan, tiles, send(tiles, swap))[0]

    shared = None
    for k in range(STEPS - 1):
        if k > 0:
            low, high = send(hi, up), send(lo, down)
            near = near_call(lo, hi)
        outs = [TILE, TILE] + ([(2, 2, TX, AY, AZ)] if k == 1 else [])
        new = call(step_kernel, 9, outs)(plan, near, lo, hi, lo_b, hi_b, low, high, coef, inj[k])
        if k == 1:
            shared = send(new[2], swap)
        lo_b, hi_b, lo, hi = lo, hi, new[0], new[1]
    low, high = send(hi, up), send(lo, down)
    near = near_call(lo, hi)
    keep, give = call(last_kernel, 10, [(2,) + PART] * 2, [(2, TX, AY, AZ)])(
        plan, near, lo, hi, lo_b, hi_b, low, high, coef, inj[STEPS - 1], shared
    )

    parts = call(total_kernel, 2, [PART] * 4)(plan, keep, send(give, swap))
    got = [send(parts[by], across(by)) for by in range(1, 4)]
    straight, last, free = call(owners_kernel, 4, [(2,) + PART] * 3)(plan, parts[0], *got)
    last_came = send(last, down)
    free_came = turn_image(free, aper % 2, turn_all)
    keep, give = call(image_kernel, 4, [PART] * 2)(plan, straight, last, last_came, free_came)
    return call(join_kernel, 2, [(TX, AY, AZ)])(plan, keep, send(give, swap))[0]


def solution(mesh):
    model = P(("shot", "aper"), None, None)
    field = P("shot", None, "aper", None, None)
    return jax.shard_map(
        local,
        mesh=mesh,
        in_specs=(model,) * 4 + (field,) * 4 + (P(),) * 5,
        out_specs=model,
        check_vma=False,
    )
```

```python
import jax
import jax.numpy as jnp
from jax import lax
from jax.experimental import pallas as pl
from jax.experimental.pallas import tpu as pltpu
from jax.sharding import PartitionSpec as P

second_coef = (-205.0 / 72.0, 8.0 / 5.0, -1.0 / 5.0, 8.0 / 315.0, -1.0 / 560.0)
first_coef = (4.0 / 5.0, -1.0 / 5.0, 4.0 / 105.0, -1.0 / 280.0)

AXES = ("shot", "aper")
STEPS = 4
TX = 4
AY = 32
AZ = 256
HALF = 128
HALF_Y = AY // 2
F32 = jnp.float32
VMEM = pl.BlockSpec(memory_space=pltpu.VMEM)
SMEM = pl.BlockSpec(memory_space=pltpu.SMEM)


def device(x, core, y, z):
    return ((x % 2) * 2 + core) * 32 + ((z % 4) * 4 + y % 4) * 2 + x // 2


def everyone():
    return [(x, c, y, z) for x in range(4) for c in range(2) for y in range(4) for z in range(4)]


def pairs_of(rule):
    pairs = [(device(*d), device(*rule(*d))) for d in everyone()]
    assert sorted(t for _, t in pairs) == list(range(128))
    assert all(s != t for s, t in pairs)
    return pairs


def send(value, pairs):
    return lax.ppermute(value, AXES, pairs)


def other_core():
    return pairs_of(lambda x, c, y, z: (x, 1 - c, y, z))


def state_first():
    def rule(x, c, y, z):
        t = {(0, 0): (0, 1), (0, 1): (1, 1), (1, 0): (0, 0), (1, 1): (1, 0)}[(x // 2, c)]
        return (2 * t[0] + x % 2, t[1], y, z)

    return pairs_of(rule)


def state_second():
    return [
        (device(x, c, y, z), device((x + 2) % 4, 1 - c, y, z)) for x, c, y, z in everyone() if x // 2 != c
    ]


def across(by):
    return pairs_of(lambda x, c, y, z: ((x + by) % 4, c, y, z))


def rolled(by_low, by_high):
    def rule(x, c, y, z):
        j = (4 * z + y + (by_high if x // 2 else by_low)) % 16
        return (x, c, j % 4, j // 4)

    return pairs_of(rule)


def z_plus(pair, d, lane):
    a, b = pair
    ra, rb = pltpu.roll(a, HALF - d, 1), pltpu.roll(b, HALF - d, 1)
    keep = lane < HALF - d
    return jnp.where(keep, ra, rb), jnp.where(keep, rb, 0.0)


def z_minus(pair, d, lane):
    a, b = pair
    ra, rb = pltpu.roll(a, d, 1), pltpu.roll(b, d, 1)
    keep = lane >= d
    return jnp.where(keep, ra, 0.0), jnp.where(keep, rb, ra)


def second_z(pair, lane):
    out = [second_coef[0] * v for v in pair]
    for d in range(1, 5):
        up, down = z_plus(pair, d, lane), z_minus(pair, d, lane)
        out = [o + second_coef[d] * (u + w) for o, u, w in zip(out, up, down)]
    return out


def first_z(pair, lane):
    out = None
    for d in range(1, 5):
        up, down = z_plus(pair, d, lane), z_minus(pair, d, lane)
        term = [first_coef[d - 1] * (u - w) for u, w in zip(up, down)]
        out = term if out is None else [o + t for o, t in zip(out, term)]
    return out


def second_y(pair, row):
    out = []
    for f in pair:
        acc = second_coef[0] * f
        for d in range(1, 5):
            up = jnp.where(row < AY - d, pltpu.roll(f, AY - d, 0), 0.0)
            down = jnp.where(row >= d, pltpu.roll(f, d, 0), 0.0)
            acc = acc + second_coef[d] * (up + down)
        out.append(acc)
    return out


CORE, X_HI, BLOCK, STAYS, PARITY_LAST, PARITY_FREE, GROUP = range(7)
PARITY, ROLE_TO, SIDE, SOURCE, OWNER, ROLE_FROM = 12, 16, 20, 24, 28, 32


def plan_values(ids, offsets):
    shot, aper = ids[0], ids[1]
    core, x_lo, x_hi = shot & 1, shot >> 1, aper & 1
    x = 2 * x_hi + x_lo
    z, y = aper >> 3, (aper >> 1) & 3
    block = 4 * z + y
    turns = [o & 31 for o in offsets]

    def of(values, g):
        return jnp.where(g < 2, jnp.where(g == 0, values[0], values[1]), jnp.where(g == 2, values[2], values[3]))

    def first(flags):
        return jnp.where(flags[0], 0, jnp.where(flags[1], 1, jnp.where(flags[2], 2, 3)))

    def group_of(x):
        return 2 * (x & 1) + (x >> 1)

    last = first([t == 31 for t in turns])
    free = 6 - first([o == 0 for o in offsets]) - first([o == 96 for o in offsets]) - last
    free_turn = of(turns, free)

    def role_of(g):
        return jnp.where(g == last, 1, jnp.where((g == free) & (free_turn != 0), 2, 0))

    def row_of(g):
        o = of(offsets, g)
        return (o + 2 * block + (x_hi ^ (o & 1))) >> 5

    def parity_before(g):
        o = of(offsets, g)
        return ((o >> 5) + (2 * block + x_hi < (o & 31)).astype(jnp.int32)) & 1

    group = group_of(x)
    offset = of(offsets, group)
    out = {
        CORE: core,
        X_HI: x_hi,
        BLOCK: block,
        GROUP: group,
        STAYS: (x_hi == core).astype(jnp.int32),
        PARITY_LAST: parity_before(last),
        PARITY_FREE: parity_before(free),
    }
    for by in range(4):
        to, came = group_of((x + by) & 3), group_of((x - by) & 3)
        out[PARITY + by] = parity_before(to)
        out[ROLE_TO + by] = role_of(to)
        out[SIDE + by] = (((x + by) & 3) >> 1) ^ (offset & 1)
        out[OWNER + by] = row_of(came) - 2 * x_lo
        out[ROLE_FROM + by] = role_of(came)
    for h in range(2):
        row = (offset + 2 * block + h) >> 5
        out[SOURCE + h] = (x - (2 * (h ^ (offset & 1)) + (row >> 1))) & 3
    return out, free_turn


def fetch(which, choices, sems):
    for k, (a, b, out) in enumerate(choices):

        @pl.when(which)
        def _(a=a, out=out, k=k):
            pltpu.make_async_copy(a, out, sems.at[k]).start()

        @pl.when(jnp.logical_not(which))
        def _(b=b, out=out, k=k):
            pltpu.make_async_copy(b, out, sems.at[k]).start()

    return [pltpu.make_async_copy(a, out, sems.at[k]) for k, (a, _, out) in enumerate(choices)]


def plan_kernel(ids, offsets, velocity, epsilon, delta, angle, plan, turn_all, turn_z, turn_y, own, other, sems):
    copies = fetch(
        ids[0] & 1 == 0,
        (
            (delta, velocity, other.at[0]),
            (angle, epsilon, other.at[1]),
            (velocity, delta, own.at[0]),
            (epsilon, angle, own.at[1]),
        ),
        sems,
    )
    values, free_turn = plan_values(ids, [offsets[g] for g in range(4)])
    for k, v in values.items():
        plan[k] = v
    turn_all[0] = free_turn
    turn_z[0] = free_turn >> 3
    turn_y[0] = free_turn & 7
    for copy in copies:
        copy.wait()


def state_kernel(plan, fwd_now, adj_now, fwd_before, adj_before, one, two, sems):
    copies = fetch(
        plan[X_HI] == 0,
        (
            (adj_now.at[0], fwd_now.at[0], one.at[0]),
            (fwd_now.at[0], adj_now.at[0], two.at[0]),
            (adj_before.at[0], fwd_before.at[0], one.at[1]),
            (fwd_before.at[0], adj_before.at[0], two.at[1]),
        ),
        sems,
    )
    for copy in copies:
        copy.wait()


def rows_kernel(plan, own, came, last, free):
    mine_last, mine_free = plan[PARITY_LAST] == plan[CORE], plan[PARITY_FREE] == plan[CORE]
    for f in range(2):
        for i in range(TX):
            a, b = own[f, i], came[f, i]
            last[f, i] = jnp.where(mine_last, a, b)
            free[f, i] = jnp.where(mine_free, a, b)


def block_kernel(plan, kept, one, two, *outs):
    first, stays = plan[CORE] == 0, plan[STAYS] == 1
    for t in range(2):
        lo, hi = outs[2 * t : 2 + 2 * t]
        for p in range(2):
            for i in range(TX):
                a, b = one[t, p, i], jnp.where(stays, kept[t, p, i], two[t, p, i])
                lo[p, i] = jnp.where(first, b, a)
                hi[p, i] = jnp.where(first, a, b)


def send_kernel(plan, own, came, last, last_came, free_came, *outs):
    high = plan[X_HI] == 1
    mine = [plan[PARITY + by] == plan[CORE] for by in range(4)]
    role = [plan[ROLE_TO + by] for by in range(4)]
    for f in range(2):
        for i in range(TX):
            a, b = own[f, i], came[f, i]
            turned_last = jnp.where(high, last_came[f, i], last[f, i])
            turned_free = free_came[f, i]
            for by in range(4):
                straight = jnp.where(mine[by], a, b)
                turned = jnp.where(role[by] == 1, turned_last, turned_free)
                outs[by][f, i] = jnp.where(role[by] == 0, straight, turned)


def tiles_kernel(plan, kept, got_1, got_2, got_3, low, high, near, inj, out):
    del low, high, near, inj
    source = [plan[SOURCE + h] for h in range(2)]
    for f in range(2):
        for i in range(TX):
            rows = [kept[f, i], got_1[f, i], got_2[f, i], got_3[f, i]]
            for h in range(2):
                a = jnp.where(source[h] == 0, rows[0], rows[1])
                b = jnp.where(source[h] == 2, rows[2], rows[3])
                out[h, f, i] = jnp.where(source[h] < 2, a, b)


HALVES = (pl.ds(0, HALF), pl.ds(HALF, HALF))


def by_distance(table, d):
    out = 0.0
    for k in range(1, 5):
        out = jnp.where(d == k, table[k], out)
    return out


def near_kernel(lo, hi, out, ext):
    lane = lax.broadcasted_iota(jnp.int32, (AY, HALF), 1)
    row = lax.broadcasted_iota(jnp.int32, (AY, HALF), 0)
    for p in range(2):
        for i in range(TX):
            ext[p, i] = jnp.zeros((AY, AZ), F32)
            ext[p, TX + i] = lo[p, i]
            ext[p, 2 * TX + i] = hi[p, i]
            ext[p, 3 * TX + i] = jnp.zeros((AY, AZ), F32)

    def one(r, carry):
        for p in range(2):
            mid = [ext[p, r + TX, :, h] for h in HALVES]
            for s, h in enumerate(HALVES):
                curve, slope = second_coef[0] * mid[s], None
                for d in range(1, 5):
                    ahead, behind = ext[p, r + TX + d, :, h], ext[p, r + TX - d, :, h]
                    curve = curve + second_coef[d] * (ahead + behind)
                    term = first_coef[d - 1] * (ahead - behind)
                    slope = term if slope is None else slope + term
                out[4 * p, r, :, h] = curve
                out[4 * p + 1, r, :, h] = slope
            depth = second_z(mid, lane)
            for s, h in enumerate(HALVES):
                out[4 * p + 2, r, :, h] = depth[s]
            if p == 0:
                across = second_y(mid, row)
                for s, h in enumerate(HALVES):
                    out[3, r, :, h] = depth[s] + across[s]
        return carry

    lax.fori_loop(0, 2 * TX, one, 0)


def far_rows(plan, near, lo, hi, lo_b, hi_b, low, high, coef, inj, emit):
    lane = lax.broadcasted_iota(jnp.int32, (AY, HALF), 1)
    first_of = (0.0,) + first_coef
    for t, (mid_ref, back, halo) in enumerate(((lo, lo_b, low), (hi, hi_b, high))):
        inside = jnp.where(plan[BLOCK] == (0, 15)[t], 0.0, 1.0)

        def one(i, carry, t=t, mid_ref=mid_ref, back=back, halo=halo, inside=inside):
            r = t * TX + i
            scales = []
            for k in range(TX):
                d = TX + (i - k if t == 0 else k - i)
                sign = inside * (-1.0, 1.0)[t]
                scales.append((inside * by_distance(second_coef, d), sign * by_distance(first_of, d)))
            sums = []
            for p in range(2):
                curve, slope = [], []
                for h in HALVES:
                    c, s = near[4 * p, r, :, h], near[4 * p + 1, r, :, h]
                    for k in range(TX):
                        value = halo[p, k, :, h]
                        c = c + scales[k][0] * value
                        s = s + scales[k][1] * value
                    curve.append(c)
                    slope.append(s)
                sums.append((curve, first_z(slope, lane)))
            (xp, cp), (xq, cq) = sums
            for s, h in enumerate(HALVES):
                aniso, coupled, square = coef[0, r, :, h], coef[1, r, :, h], coef[2, r, :, h]
                sine, cosine, double = coef[3, r, :, h], coef[4, r, :, h], coef[5, r, :, h]
                axial_p = sine * xp[s] + cosine * near[2, r, :, h] + double * cp[s]
                plane_p = xp[s] + near[3, r, :, h] - axial_p
                axial_q = sine * xq[s] + cosine * near[6, r, :, h] + double * cq[s]
                add = inj[r, :, h]
                new_p = 2.0 * mid_ref[0, i, :, h] - back[0, i, :, h] + aniso * plane_p + coupled * axial_q + add
                new_q = 2.0 * mid_ref[1, i, :, h] - back[1, i, :, h] + coupled * plane_p + square * axial_q + add
                emit(t, i, h, new_p, new_q)
            return carry

        lax.fori_loop(0, TX, one, 0)


def step_kernel(plan, near, lo, hi, lo_b, hi_b, low, high, coef, inj, new_lo, new_hi, *packed):
    def emit(t, i, h, new_p, new_q):
        out = (new_lo, new_hi)[t]
        out[0, i, :, h] = new_p
        out[1, i, :, h] = new_q
        for p in packed:
            p[0, t, i, :, h] = (lo, hi)[t][0, i, :, h]
            p[1, t, i, :, h] = new_p

    far_rows(plan, near, lo, hi, lo_b, hi_b, low, high, coef, inj, emit)


def last_kernel(plan, near, lo, hi, lo_b, hi_b, low, high, coef, inj, other, keep, give, part):
    def emit(t, i, h, new_p, new_q):
        del new_q
        part[t, i, :, h] = new_p * other[0, t, i, :, h] + (lo, hi)[t][0, i, :, h] * other[1, t, i, :, h]

    far_rows(plan, near, lo, hi, lo_b, hi_b, low, high, coef, inj, emit)
    first = plan[CORE] == 0
    for t in range(2):
        for i in range(TX):
            low_y, high_y = part[t, i, :HALF_Y], part[t, i, HALF_Y:]
            keep[t, i] = jnp.where(first, low_y, high_y)
            give[t, i] = jnp.where(first, high_y, low_y)


def total_kernel(plan, keep, came, *outs):
    for i in range(TX):
        lo = keep[0, i] + came[0, i]
        hi = keep[1, i] + came[1, i]
        for by in range(4):
            outs[by][i] = jnp.where(plan[SIDE + by] == 0, lo, hi)


def owners_kernel(plan, kept, got_1, got_2, got_3, straight, last, free):
    for i in range(TX):
        parts = [kept[i], got_1[i], got_2[i], got_3[i]]
        for k, out in enumerate((straight, last, free)):
            for core in range(2):
                acc = jnp.zeros_like(parts[0])
                for by in range(4):
                    ours = (plan[OWNER + by] == core) & (plan[ROLE_FROM + by] == k)
                    acc = acc + jnp.where(ours, parts[by], 0.0)
                out[core, i] = acc


def image_kernel(plan, straight, last, last_came, free_came, keep, give):
    high, first = plan[X_HI] == 1, plan[CORE] == 0
    for i in range(TX):
        sums = []
        for core in range(2):
            turned = jnp.where(high, last_came[core, i], last[core, i])
            sums.append(straight[core, i] + turned + free_came[core, i])
        keep[i] = jnp.where(first, sums[0], sums[1])
        give[i] = jnp.where(first, sums[1], sums[0])


def join_kernel(plan, keep, came, out):
    first = plan[CORE] == 0
    for i in range(TX):
        out[i, :HALF_Y] = jnp.where(first, keep[i], came[i])
        out[i, HALF_Y:] = jnp.where(first, came[i], keep[i])


def inject_kernel(plan, source, wavelet, cells, traces, *outs):
    group, forward, base = plan[GROUP], plan[CORE] == 0, 8 * plan[BLOCK]
    count = cells.shape[2]
    lane = lax.broadcasted_iota(jnp.int32, (1, count), 1)
    x, y, depth = (
        jnp.where(
            forward,
            jnp.where(lane == 0, source[group, f], -1),
            cells[f, pl.ds(group, 1), :],
        )
        for f in range(3)
    )
    here = (x >= base) & (x < base + 8)
    spot = jnp.where(here, (x - base) * AY + y, -1)
    which = (lax.broadcasted_iota(jnp.int32, (8 * AY, count), 0) == spot).astype(F32)
    level = lax.broadcasted_iota(jnp.int32, (AZ, count), 0) == depth
    for k in range(STEPS):
        amounts = jnp.where(forward, wavelet[group, k], traces[group, pl.ds(k, 1), :])
        values = jnp.where(level, amounts, 0.0)
        flat = lax.dot_general(
            which,
            values,
            (((1,), (1,)), ((), ())),
            precision=lax.Precision.HIGHEST,
            preferred_element_type=F32,
        )
        for i in range(8):
            outs[k][i] = flat[i * AY : (i + 1) * AY, :]


def sine_cosine(angle):
    sq = angle * angle
    sine = -1.0 / 39916800.0
    for c in (1.0 / 362880.0, -1.0 / 5040.0, 1.0 / 120.0, -1.0 / 6.0, 1.0):
        sine = sine * sq + c
    cosine = 1.0 / 479001600.0
    for c in (-1.0 / 3628800.0, 1.0 / 40320.0, -1.0 / 720.0, 1.0 / 24.0, -0.5, 1.0):
        cosine = cosine * sq + c
    return sine * angle, cosine


def coef_kernel(plan, own, other, out):
    core = plan[CORE]
    for t in range(2):

        def tile(i, carry, t=t):
            mine = [own[t, f, i] for f in range(2)]
            theirs = [other[t, f, i] for f in range(2)]
            velocity = jnp.where(core == 0, mine[0], theirs[0])
            epsilon = jnp.where(core == 0, mine[1], theirs[1])
            delta = jnp.where(core == 0, theirs[0], mine[0])
            angle = jnp.where(core == 0, theirs[1], mine[1])
            square = velocity * velocity
            sine, cosine = sine_cosine(angle)
            k = t * TX + i
            out[0, k] = square * (1.0 + 2.0 * epsilon)
            out[1, k] = square * jnp.sqrt(1.0 + 2.0 * delta)
            out[2, k] = square
            out[3, k] = sine * sine
            out[4, k] = cosine * cosine
            out[5, k] = 2.0 * sine * cosine
            return carry

        lax.fori_loop(0, TX, tile, 0)


HBM = pl.BlockSpec(memory_space=pltpu.HBM)
LIMIT = pltpu.CompilerParams(vmem_limit_bytes=4 * 1024 * 1024)


def in_hbm(value):
    return pltpu.with_memory_space_constraint(value, pltpu.HBM)


def call(kernel, n_in, outs, scratch=()):
    return pl.pallas_call(
        kernel,
        out_shape=[jax.ShapeDtypeStruct(s, F32) for s in outs],
        in_specs=[SMEM] + [VMEM] * n_in,
        out_specs=[VMEM] * len(outs),
        scratch_shapes=[pltpu.VMEM(s, F32) for s in scratch],
        compiler_params=LIMIT,
    )


TILE = (2, TX, AY, AZ)
PART = (TX, HALF_Y, AZ)


def turn_model(value, x_hi, turn_z, turn_y):
    def roll(v, by):
        return send(v, rolled(-by, -by)) if by else v

    def columns(v, r):
        if r == 1:
            return jnp.where(x_hi == 1, v, roll(v, 1))
        if r % 2 == 0:
            return roll(v, r // 2)
        return send(v, rolled(-(r // 2 + 1), -(r // 2)))

    value = lax.switch(turn_z[0], [lambda v, k=k: roll(v, 4 * k) for k in range(4)], value)
    return lax.switch(turn_y[0], [lambda v, r=r: columns(v, r) for r in range(8)], value)


def turn_image(value, x_hi, free_turn):
    def roll(v, by):
        if by % 16 == 0:
            return v
        return roll(roll(v, 8), 7) if by == 15 else send(v, rolled(by, by))

    def columns(v, r):
        low, high = (r + 1) // 2, r // 2
        if r % 2 == 0:
            return roll(v, high)
        if r in (1, 15, 17, 29, 31):
            return jnp.where(x_hi == 1, roll(v, high), roll(v, low))
        return send(v, rolled(low, high))

    return lax.switch(free_turn[0], [lambda v, r=r: columns(v, r) for r in range(32)], value)


def local(
    velocity,
    thomsen_epsilon,
    thomsen_delta,
    tilt_angle,
    fwd_now,
    fwd_before,
    adj_now,
    adj_before,
    wavelet,
    traces,
    offsets,
    source_cell,
    receiver_cell,
):
    shot, aper = lax.axis_index("shot"), lax.axis_index("aper")
    ids = jnp.stack([shot, aper]).astype(jnp.int32)
    swap, up, down = other_core(), rolled(1, 1), rolled(-1, -1)

    plan, turn_all, turn_z, turn_y, own, other = pl.pallas_call(
        plan_kernel,
        out_shape=[jax.ShapeDtypeStruct((n,), jnp.int32) for n in (40, 1, 1, 1)] + [jax.ShapeDtypeStruct(TILE, F32)] * 2,
        in_specs=[SMEM] * 2 + [HBM] * 4,
        out_specs=[SMEM] * 4 + [VMEM] * 2,
        scratch_shapes=[pltpu.SemaphoreType.DMA((4,))],
        compiler_params=LIMIT,
    )(ids, offsets, *(in_hbm(v) for v in (velocity, thomsen_epsilon, thomsen_delta, tilt_angle)))
    came = send(other, swap)
    one, two = pl.pallas_call(
        state_kernel,
        out_shape=[jax.ShapeDtypeStruct((2,) + TILE, F32)] * 2,
        in_specs=[SMEM] + [HBM] * 4,
        out_specs=[VMEM] * 2,
        scratch_shapes=[pltpu.SemaphoreType.DMA((4,))],
        compiler_params=LIMIT,
    )(plan, *(in_hbm(v) for v in (fwd_now, adj_now, fwd_before, adj_before)))
    got_one, got_two = send(one, state_first()), send(two, state_second())

    last, free = call(rows_kernel, 2, [TILE] * 2)(plan, own, came)
    last_came = send(last, up)
    free_came = turn_model(free, aper % 2, turn_z, turn_y)
    rows = call(send_kernel, 5, [TILE] * 4)(plan, own, came, last, last_came, free_came)
    got = [send(rows[by], across(by)) for by in range(1, 4)]
    lo, hi, lo_b, hi_b = call(block_kernel, 3, [TILE] * 4)(plan, two, got_one, got_two)
    inj = pl.pallas_call(
        inject_kernel,
        out_shape=[jax.ShapeDtypeStruct((8, AY, AZ), F32)] * STEPS,
        in_specs=[SMEM] * 3 + [VMEM] * 2,
        out_specs=[VMEM] * STEPS,
        compiler_params=LIMIT,
    )(plan, source_cell, wavelet, jnp.transpose(receiver_cell, (2, 0, 1)), traces)

    near_call = pl.pallas_call(
        near_kernel,
        out_shape=jax.ShapeDtypeStruct((7, 8, AY, AZ), F32),
        in_specs=[VMEM] * 2,
        out_specs=VMEM,
        scratch_shapes=[pltpu.VMEM((2, 4 * TX, AY, AZ), F32)],
        compiler_params=LIMIT,
    )
    near = near_call(lo, hi)
    low, high = send(hi, up), send(lo, down)
    tiles = call(tiles_kernel, 8, [(2,) + TILE])(
        plan, rows[0], *got, low, high, near, inj[0]
    )[0]
    coef = call(coef_kernel, 2, [(6, 8, AY, AZ)])(plan, tiles, send(tiles, swap))[0]

    shared = None
    for k in range(STEPS - 1):
        if k > 0:
            low, high = send(hi, up), send(lo, down)
            near = near_call(lo, hi)
        outs = [TILE, TILE] + ([(2, 2, TX, AY, AZ)] if k == 1 else [])
        new = call(step_kernel, 9, outs)(plan, near, lo, hi, lo_b, hi_b, low, high, coef, inj[k])
        if k == 1:
            shared = send(new[2], swap)
        lo_b, hi_b, lo, hi = lo, hi, new[0], new[1]
    low, high = send(hi, up), send(lo, down)
    near = near_call(lo, hi)
    keep, give = call(last_kernel, 10, [(2,) + PART] * 2, [(2, TX, AY, AZ)])(
        plan, near, lo, hi, lo_b, hi_b, low, high, coef, inj[STEPS - 1], shared
    )

    parts = call(total_kernel, 2, [PART] * 4)(plan, keep, send(give, swap))
    got = [send(parts[by], across(by)) for by in range(1, 4)]
    straight, last, free = call(owners_kernel, 4, [(2,) + PART] * 3)(plan, parts[0], *got)
    last_came = send(last, down)
    free_came = turn_image(free, aper % 2, turn_all)
    keep, give = call(image_kernel, 4, [PART] * 2)(plan, straight, last, last_came, free_came)
    return call(join_kernel, 2, [(TX, AY, AZ)])(plan, keep, send(give, swap))[0]


def solution(mesh):
    model = P(("shot", "aper"), None, None)
    field = P("shot", None, "aper", None, None)
    return jax.shard_map(
        local,
        mesh=mesh,
        in_specs=(model,) * 4 + (field,) * 4 + (P(),) * 5,
        out_specs=model,
        check_vma=False,
    )
```

```python
import jax
import jax.numpy as jnp
from jax import lax
from jax.experimental import pallas as pl
from jax.experimental.pallas import tpu as pltpu
from jax.sharding import PartitionSpec as P

second_coef = (-205.0 / 72.0, 8.0 / 5.0, -1.0 / 5.0, 8.0 / 315.0, -1.0 / 560.0)
first_coef = (4.0 / 5.0, -1.0 / 5.0, 4.0 / 105.0, -1.0 / 280.0)

AXES = ("shot", "aper")
STEPS = 4
TX = 4
AY = 32
AZ = 256
HALF = 128
HALF_Y = AY // 2
F32 = jnp.float32
VMEM = pl.BlockSpec(memory_space=pltpu.VMEM)
SMEM = pl.BlockSpec(memory_space=pltpu.SMEM)


def device(x, core, y, z):
    return ((x % 2) * 2 + core) * 32 + ((z % 4) * 4 + y % 4) * 2 + x // 2


def everyone():
    return [(x, c, y, z) for x in range(4) for c in range(2) for y in range(4) for z in range(4)]


def pairs_of(rule):
    pairs = [(device(*d), device(*rule(*d))) for d in everyone()]
    assert sorted(t for _, t in pairs) == list(range(128))
    assert all(s != t for s, t in pairs)
    return pairs


def send(value, pairs):
    return lax.ppermute(value, AXES, pairs)


def other_core():
    return pairs_of(lambda x, c, y, z: (x, 1 - c, y, z))


def state_first():
    def rule(x, c, y, z):
        t = {(0, 0): (0, 1), (0, 1): (1, 1), (1, 0): (0, 0), (1, 1): (1, 0)}[(x // 2, c)]
        return (2 * t[0] + x % 2, t[1], y, z)

    return pairs_of(rule)


def state_second():
    return [
        (device(x, c, y, z), device((x + 2) % 4, 1 - c, y, z)) for x, c, y, z in everyone() if x // 2 != c
    ]


def across(by):
    return pairs_of(lambda x, c, y, z: ((x + by) % 4, c, y, z))


def rolled(by_low, by_high):
    def rule(x, c, y, z):
        j = (4 * z + y + (by_high if x // 2 else by_low)) % 16
        return (x, c, j % 4, j // 4)

    return pairs_of(rule)


def z_plus(pair, d, lane):
    a, b = pair
    ra, rb = pltpu.roll(a, HALF - d, 1), pltpu.roll(b, HALF - d, 1)
    keep = lane < HALF - d
    return jnp.where(keep, ra, rb), jnp.where(keep, rb, 0.0)


def z_minus(pair, d, lane):
    a, b = pair
    ra, rb = pltpu.roll(a, d, 1), pltpu.roll(b, d, 1)
    keep = lane >= d
    return jnp.where(keep, ra, 0.0), jnp.where(keep, rb, ra)


def second_z(pair, lane):
    out = [second_coef[0] * v for v in pair]
    for d in range(1, 5):
        up, down = z_plus(pair, d, lane), z_minus(pair, d, lane)
        out = [o + second_coef[d] * (u + w) for o, u, w in zip(out, up, down)]
    return out


def first_z(pair, lane):
    out = None
    for d in range(1, 5):
        up, down = z_plus(pair, d, lane), z_minus(pair, d, lane)
        term = [first_coef[d - 1] * (u - w) for u, w in zip(up, down)]
        out = term if out is None else [o + t for o, t in zip(out, term)]
    return out


def second_y(pair, row):
    out = []
    for f in pair:
        acc = second_coef[0] * f
        for d in range(1, 5):
            up = jnp.where(row < AY - d, pltpu.roll(f, AY - d, 0), 0.0)
            down = jnp.where(row >= d, pltpu.roll(f, d, 0), 0.0)
            acc = acc + second_coef[d] * (up + down)
        out.append(acc)
    return out


CORE, X_HI, BLOCK, STAYS, PARITY_LAST, PARITY_FREE, GROUP = range(7)
PARITY, ROLE_TO, SIDE, SOURCE, OWNER, ROLE_FROM = 12, 16, 20, 24, 28, 32


def plan_values(ids, offsets):
    shot, aper = ids[0], ids[1]
    core, x_lo, x_hi = shot & 1, shot >> 1, aper & 1
    x = 2 * x_hi + x_lo
    z, y = aper >> 3, (aper >> 1) & 3
    block = 4 * z + y
    turns = [o & 31 for o in offsets]

    def of(values, g):
        return jnp.where(g < 2, jnp.where(g == 0, values[0], values[1]), jnp.where(g == 2, values[2], values[3]))

    def first(flags):
        return jnp.where(flags[0], 0, jnp.where(flags[1], 1, jnp.where(flags[2], 2, 3)))

    def group_of(x):
        return 2 * (x & 1) + (x >> 1)

    last = first([t == 31 for t in turns])
    free = 6 - first([o == 0 for o in offsets]) - first([o == 96 for o in offsets]) - last
    free_turn = of(turns, free)

    def role_of(g):
        return jnp.where(g == last, 1, jnp.where((g == free) & (free_turn != 0), 2, 0))

    def row_of(g):
        o = of(offsets, g)
        return (o + 2 * block + (x_hi ^ (o & 1))) >> 5

    def parity_before(g):
        o = of(offsets, g)
        return ((o >> 5) + (2 * block + x_hi < (o & 31)).astype(jnp.int32)) & 1

    group = group_of(x)
    offset = of(offsets, group)
    out = {
        CORE: core,
        X_HI: x_hi,
        BLOCK: block,
        GROUP: group,
        STAYS: (x_hi == core).astype(jnp.int32),
        PARITY_LAST: parity_before(last),
        PARITY_FREE: parity_before(free),
    }
    for by in range(4):
        to, came = group_of((x + by) & 3), group_of((x - by) & 3)
        out[PARITY + by] = parity_before(to)
        out[ROLE_TO + by] = role_of(to)
        out[SIDE + by] = (((x + by) & 3) >> 1) ^ (offset & 1)
        out[OWNER + by] = row_of(came) - 2 * x_lo
        out[ROLE_FROM + by] = role_of(came)
    for h in range(2):
        row = (offset + 2 * block + h) >> 5
        out[SOURCE + h] = (x - (2 * (h ^ (offset & 1)) + (row >> 1))) & 3
    return out, free_turn


def fetch(which, choices, sems):
    for k, (a, b, out) in enumerate(choices):

        @pl.when(which)
        def _(a=a, out=out, k=k):
            pltpu.make_async_copy(a, out, sems.at[k]).start()

        @pl.when(jnp.logical_not(which))
        def _(b=b, out=out, k=k):
            pltpu.make_async_copy(b, out, sems.at[k]).start()

    return [pltpu.make_async_copy(a, out, sems.at[k]) for k, (a, _, out) in enumerate(choices)]


def plan_kernel(
    ids,
    offsets,
    velocity,
    epsilon,
    delta,
    angle,
    fwd_now,
    adj_now,
    fwd_before,
    adj_before,
    plan,
    turn_all,
    turn_z,
    turn_y,
    own,
    other,
    one,
    two,
    one_b,
    two_b,
    model_sems,
    state_sems,
):
    model = fetch(
        ids[0] & 1 == 0,
        (
            (delta, velocity, other.at[0]),
            (angle, epsilon, other.at[1]),
            (velocity, delta, own.at[0]),
            (epsilon, angle, own.at[1]),
        ),
        model_sems,
    )
    state = fetch(
        ids[1] & 1 == 0,
        (
            (adj_now.at[0], fwd_now.at[0], one),
            (fwd_now.at[0], adj_now.at[0], two),
            (adj_before.at[0], fwd_before.at[0], one_b),
            (fwd_before.at[0], adj_before.at[0], two_b),
        ),
        state_sems,
    )
    values, free_turn = plan_values(ids, [offsets[g] for g in range(4)])
    for k, v in values.items():
        plan[k] = v
    turn_all[0] = free_turn
    turn_z[0] = free_turn >> 3
    turn_y[0] = free_turn & 7
    for copy in model + state:
        copy.wait()


def rows_kernel(plan, own, came, last, free):
    mine_last, mine_free = plan[PARITY_LAST] == plan[CORE], plan[PARITY_FREE] == plan[CORE]
    for f in range(2):
        for i in range(TX):
            a, b = own[f, i], came[f, i]
            last[f, i] = jnp.where(mine_last, a, b)
            free[f, i] = jnp.where(mine_free, a, b)


def block_kernel(plan, kept, one, two, lo, hi):
    first, stays = plan[CORE] == 0, plan[STAYS] == 1
    for p in range(2):
        for i in range(TX):
            a, b = one[p, i], jnp.where(stays, kept[p, i], two[p, i])
            lo[p, i] = jnp.where(first, b, a)
            hi[p, i] = jnp.where(first, a, b)


def send_kernel(plan, own, came, last, last_came, free_came, *outs):
    high = plan[X_HI] == 1
    mine = [plan[PARITY + by] == plan[CORE] for by in range(4)]
    role = [plan[ROLE_TO + by] for by in range(4)]
    for f in range(2):
        for i in range(TX):
            a, b = own[f, i], came[f, i]
            turned_last = jnp.where(high, last_came[f, i], last[f, i])
            turned_free = free_came[f, i]
            for by in range(4):
                straight = jnp.where(mine[by], a, b)
                turned = jnp.where(role[by] == 1, turned_last, turned_free)
                outs[by][f, i] = jnp.where(role[by] == 0, straight, turned)


def tiles_kernel(plan, kept, got_1, got_2, got_3, low, high, lo_b, near, inj, out):
    del low, high, lo_b, near, inj
    source = [plan[SOURCE + h] for h in range(2)]
    for f in range(2):
        for i in range(TX):
            rows = [kept[f, i], got_1[f, i], got_2[f, i], got_3[f, i]]
            for h in range(2):
                a = jnp.where(source[h] == 0, rows[0], rows[1])
                b = jnp.where(source[h] == 2, rows[2], rows[3])
                out[h, f, i] = jnp.where(source[h] < 2, a, b)


HALVES = (pl.ds(0, HALF), pl.ds(HALF, HALF))


def by_distance(table, d):
    out = 0.0
    for k in range(1, 5):
        out = jnp.where(d == k, table[k], out)
    return out


def near_kernel(lo, hi, out, ext):
    lane = lax.broadcasted_iota(jnp.int32, (AY, HALF), 1)
    row = lax.broadcasted_iota(jnp.int32, (AY, HALF), 0)
    for p in range(2):
        for i in range(TX):
            ext[p, i] = jnp.zeros((AY, AZ), F32)
            ext[p, TX + i] = lo[p, i]
            ext[p, 2 * TX + i] = hi[p, i]
            ext[p, 3 * TX + i] = jnp.zeros((AY, AZ), F32)

    def one(r, carry):
        for p in range(2):
            mid = [ext[p, r + TX, :, h] for h in HALVES]
            for s, h in enumerate(HALVES):
                curve, slope = second_coef[0] * mid[s], None
                for d in range(1, 5):
                    ahead, behind = ext[p, r + TX + d, :, h], ext[p, r + TX - d, :, h]
                    curve = curve + second_coef[d] * (ahead + behind)
                    term = first_coef[d - 1] * (ahead - behind)
                    slope = term if slope is None else slope + term
                out[4 * p, r, :, h] = curve
                out[4 * p + 1, r, :, h] = slope
            depth = second_z(mid, lane)
            for s, h in enumerate(HALVES):
                out[4 * p + 2, r, :, h] = depth[s]
            if p == 0:
                across = second_y(mid, row)
                for s, h in enumerate(HALVES):
                    out[3, r, :, h] = depth[s] + across[s]
        return carry

    lax.fori_loop(0, 2 * TX, one, 0)


def far_rows(plan, near, lo, hi, lo_b, hi_b, low, high, coef, inj, emit):
    lane = lax.broadcasted_iota(jnp.int32, (AY, HALF), 1)
    first_of = (0.0,) + first_coef
    for t, (mid_ref, back, halo) in enumerate(((lo, lo_b, low), (hi, hi_b, high))):
        inside = jnp.where(plan[BLOCK] == (0, 15)[t], 0.0, 1.0)

        def one(i, carry, t=t, mid_ref=mid_ref, back=back, halo=halo, inside=inside):
            r = t * TX + i
            scales = []
            for k in range(TX):
                d = TX + (i - k if t == 0 else k - i)
                sign = inside * (-1.0, 1.0)[t]
                scales.append((inside * by_distance(second_coef, d), sign * by_distance(first_of, d)))
            sums = []
            for p in range(2):
                curve, slope = [], []
                for h in HALVES:
                    c, s = near[4 * p, r, :, h], near[4 * p + 1, r, :, h]
                    for k in range(TX):
                        value = halo[p, k, :, h]
                        c = c + scales[k][0] * value
                        s = s + scales[k][1] * value
                    curve.append(c)
                    slope.append(s)
                sums.append((curve, first_z(slope, lane)))
            (xp, cp), (xq, cq) = sums
            for s, h in enumerate(HALVES):
                aniso, coupled, square = coef[0, r, :, h], coef[1, r, :, h], coef[2, r, :, h]
                sine, cosine, double = coef[3, r, :, h], coef[4, r, :, h], coef[5, r, :, h]
                axial_p = sine * xp[s] + cosine * near[2, r, :, h] + double * cp[s]
                plane_p = xp[s] + near[3, r, :, h] - axial_p
                axial_q = sine * xq[s] + cosine * near[6, r, :, h] + double * cq[s]
                add = inj[r, :, h]
                new_p = 2.0 * mid_ref[0, i, :, h] - back[0, i, :, h] + aniso * plane_p + coupled * axial_q + add
                new_q = 2.0 * mid_ref[1, i, :, h] - back[1, i, :, h] + coupled * plane_p + square * axial_q + add
                emit(t, i, h, new_p, new_q)
            return carry

        lax.fori_loop(0, TX, one, 0)


def step_kernel(plan, near, lo, hi, lo_b, hi_b, low, high, coef, inj, new_lo, new_hi, *packed):
    def emit(t, i, h, new_p, new_q):
        out = (new_lo, new_hi)[t]
        out[0, i, :, h] = new_p
        out[1, i, :, h] = new_q
        for p in packed:
            p[0, t, i, :, h] = (lo, hi)[t][0, i, :, h]
            p[1, t, i, :, h] = new_p

    far_rows(plan, near, lo, hi, lo_b, hi_b, low, high, coef, inj, emit)


def last_kernel(plan, near, lo, hi, lo_b, hi_b, low, high, coef, inj, other, keep, give, part):
    def emit(t, i, h, new_p, new_q):
        del new_q
        part[t, i, :, h] = new_p * other[0, t, i, :, h] + (lo, hi)[t][0, i, :, h] * other[1, t, i, :, h]

    far_rows(plan, near, lo, hi, lo_b, hi_b, low, high, coef, inj, emit)
    first = plan[CORE] == 0
    for t in range(2):
        for i in range(TX):
            low_y, high_y = part[t, i, :HALF_Y], part[t, i, HALF_Y:]
            keep[t, i] = jnp.where(first, low_y, high_y)
            give[t, i] = jnp.where(first, high_y, low_y)


def total_kernel(plan, keep, came, *outs):
    for i in range(TX):
        lo = keep[0, i] + came[0, i]
        hi = keep[1, i] + came[1, i]
        for by in range(4):
            outs[by][i] = jnp.where(plan[SIDE + by] == 0, lo, hi)


def owners_kernel(plan, kept, got_1, got_2, got_3, straight, last, free):
    for i in range(TX):
        parts = [kept[i], got_1[i], got_2[i], got_3[i]]
        for k, out in enumerate((straight, last, free)):
            for core in range(2):
                acc = jnp.zeros_like(parts[0])
                for by in range(4):
                    ours = (plan[OWNER + by] == core) & (plan[ROLE_FROM + by] == k)
                    acc = acc + jnp.where(ours, parts[by], 0.0)
                out[core, i] = acc


def image_kernel(plan, straight, last, last_came, free_came, keep, give):
    high, first = plan[X_HI] == 1, plan[CORE] == 0
    for i in range(TX):
        sums = []
        for core in range(2):
            turned = jnp.where(high, last_came[core, i], last[core, i])
            sums.append(straight[core, i] + turned + free_came[core, i])
        keep[i] = jnp.where(first, sums[0], sums[1])
        give[i] = jnp.where(first, sums[1], sums[0])


def join_kernel(plan, keep, came, out):
    first = plan[CORE] == 0
    for i in range(TX):
        out[i, :HALF_Y] = jnp.where(first, keep[i], came[i])
        out[i, HALF_Y:] = jnp.where(first, came[i], keep[i])


def inject_kernel(plan, source, wavelet, cells, traces, *outs):
    group, forward, base = plan[GROUP], plan[CORE] == 0, 8 * plan[BLOCK]
    count = cells.shape[2]
    lane = lax.broadcasted_iota(jnp.int32, (1, count), 1)
    x, y, depth = (
        jnp.where(
            forward,
            jnp.where(lane == 0, source[group, f], -1),
            cells[f, pl.ds(group, 1), :],
        )
        for f in range(3)
    )
    here = (x >= base) & (x < base + 8)
    spot = jnp.where(here, (x - base) * AY + y, -1)
    which = (lax.broadcasted_iota(jnp.int32, (8 * AY, count), 0) == spot).astype(F32)
    level = lax.broadcasted_iota(jnp.int32, (AZ, count), 0) == depth
    for k in range(STEPS):
        amounts = jnp.where(forward, wavelet[group, k], traces[group, pl.ds(k, 1), :])
        values = jnp.where(level, amounts, 0.0)
        flat = lax.dot_general(
            which,
            values,
            (((1,), (1,)), ((), ())),
            precision=lax.Precision.HIGHEST,
            preferred_element_type=F32,
        )
        for i in range(8):
            outs[k][i] = flat[i * AY : (i + 1) * AY, :]


def sine_cosine(angle):
    sq = angle * angle
    sine = -1.0 / 39916800.0
    for c in (1.0 / 362880.0, -1.0 / 5040.0, 1.0 / 120.0, -1.0 / 6.0, 1.0):
        sine = sine * sq + c
    cosine = 1.0 / 479001600.0
    for c in (-1.0 / 3628800.0, 1.0 / 40320.0, -1.0 / 720.0, 1.0 / 24.0, -0.5, 1.0):
        cosine = cosine * sq + c
    return sine * angle, cosine


def coef_kernel(plan, own, other, out):
    core = plan[CORE]
    for t in range(2):

        def tile(i, carry, t=t):
            mine = [own[t, f, i] for f in range(2)]
            theirs = [other[t, f, i] for f in range(2)]
            velocity = jnp.where(core == 0, mine[0], theirs[0])
            epsilon = jnp.where(core == 0, mine[1], theirs[1])
            delta = jnp.where(core == 0, theirs[0], mine[0])
            angle = jnp.where(core == 0, theirs[1], mine[1])
            square = velocity * velocity
            sine, cosine = sine_cosine(angle)
            k = t * TX + i
            out[0, k] = square * (1.0 + 2.0 * epsilon)
            out[1, k] = square * jnp.sqrt(1.0 + 2.0 * delta)
            out[2, k] = square
            out[3, k] = sine * sine
            out[4, k] = cosine * cosine
            out[5, k] = 2.0 * sine * cosine
            return carry

        lax.fori_loop(0, TX, tile, 0)


HBM = pl.BlockSpec(memory_space=pltpu.HBM)
LIMIT = pltpu.CompilerParams(vmem_limit_bytes=4 * 1024 * 1024)


def in_hbm(value):
    return pltpu.with_memory_space_constraint(value, pltpu.HBM)


def call(kernel, n_in, outs, scratch=()):
    return pl.pallas_call(
        kernel,
        out_shape=[jax.ShapeDtypeStruct(s, F32) for s in outs],
        in_specs=[SMEM] + [VMEM] * n_in,
        out_specs=[VMEM] * len(outs),
        scratch_shapes=[pltpu.VMEM(s, F32) for s in scratch],
        compiler_params=LIMIT,
    )


TILE = (2, TX, AY, AZ)
PART = (TX, HALF_Y, AZ)


def roll_model(value, by):
    return send(value, rolled(-by, -by)) if by else value


def turn_model_z(value, turn_z):
    return lax.switch(turn_z[0], [lambda v, k=k: roll_model(v, 4 * k) for k in range(4)], value)


def turn_model_y(value, x_hi, turn_y):
    def columns(v, r):
        if r == 1:
            return jnp.where(x_hi == 1, v, roll_model(v, 1))
        if r % 2 == 0:
            return roll_model(v, r // 2)
        return send(v, rolled(-(r // 2 + 1), -(r // 2)))

    return lax.switch(turn_y[0], [lambda v, r=r: columns(v, r) for r in range(8)], value)


def turn_image(value, x_hi, free_turn):
    def roll(v, by):
        if by % 16 == 0:
            return v
        return roll(roll(v, 8), 7) if by == 15 else send(v, rolled(by, by))

    def columns(v, r):
        low, high = (r + 1) // 2, r // 2
        if r % 2 == 0:
            return roll(v, high)
        if r in (1, 3, 5, 15, 17, 25, 27, 29, 31):
            return jnp.where(x_hi == 1, roll(v, high), roll(v, low))
        return send(v, rolled(low, high))

    return lax.switch(free_turn[0], [lambda v, r=r: columns(v, r) for r in range(32)], value)


def local(
    velocity,
    thomsen_epsilon,
    thomsen_delta,
    tilt_angle,
    fwd_now,
    fwd_before,
    adj_now,
    adj_before,
    wavelet,
    traces,
    offsets,
    source_cell,
    receiver_cell,
):
    shot, aper = lax.axis_index("shot"), lax.axis_index("aper")
    ids = jnp.stack([shot, aper]).astype(jnp.int32)
    swap, up, down = other_core(), rolled(1, 1), rolled(-1, -1)

    plan, turn_all, turn_z, turn_y, own, other, one, two, one_b, two_b = pl.pallas_call(
        plan_kernel,
        out_shape=[jax.ShapeDtypeStruct((n,), jnp.int32) for n in (40, 1, 1, 1)]
        + [jax.ShapeDtypeStruct(TILE, F32)] * 6,
        in_specs=[SMEM] * 2 + [HBM] * 8,
        out_specs=[SMEM] * 4 + [VMEM] * 6,
        scratch_shapes=[pltpu.SemaphoreType.DMA((4,))] * 2,
        compiler_params=LIMIT,
    )(
        ids,
        offsets,
        *(in_hbm(v) for v in (velocity, thomsen_epsilon, thomsen_delta, tilt_angle)),
        *(in_hbm(v) for v in (fwd_now, adj_now, fwd_before, adj_before)),
    )
    came = send(other, swap)
    got_one, got_two = send(one, state_first()), send(two, state_second())

    last, free = call(rows_kernel, 2, [TILE] * 2)(plan, own, came)
    last_came = send(last, up)
    free = turn_model_z(free, turn_z)
    free, got_one, got_two = lax.optimization_barrier((free, got_one, got_two))
    lo, hi = call(block_kernel, 3, [TILE] * 2)(plan, two, got_one, got_two)
    low, high = send(hi, up), send(lo, down)
    free, lo, hi = lax.optimization_barrier((free, lo, hi))
    free_came = turn_model_y(free, aper % 2, turn_y)
    rows = call(send_kernel, 5, [TILE] * 4)(plan, own, came, last, last_came, free_came)
    got = [send(rows[by], across(by)) for by in range(1, 4)]
    got_one, got_two = send(one_b, state_first()), send(two_b, state_second())
    lo_b, hi_b = call(block_kernel, 3, [TILE] * 2)(plan, two_b, got_one, got_two)
    inj = pl.pallas_call(
        inject_kernel,
        out_shape=[jax.ShapeDtypeStruct((8, AY, AZ), F32)] * STEPS,
        in_specs=[SMEM] * 3 + [VMEM] * 2,
        out_specs=[VMEM] * STEPS,
        compiler_params=LIMIT,
    )(plan, source_cell, wavelet, jnp.transpose(receiver_cell, (2, 0, 1)), traces)

    near_call = pl.pallas_call(
        near_kernel,
        out_shape=jax.ShapeDtypeStruct((7, 8, AY, AZ), F32),
        in_specs=[VMEM] * 2,
        out_specs=VMEM,
        scratch_shapes=[pltpu.VMEM((2, 4 * TX, AY, AZ), F32)],
        compiler_params=LIMIT,
    )
    near = near_call(lo, hi)
    tiles = call(tiles_kernel, 9, [(2,) + TILE])(
        plan, rows[0], *got, low, high, lo_b, near, inj[0]
    )[0]
    coef = call(coef_kernel, 2, [(6, 8, AY, AZ)])(plan, tiles, send(tiles, swap))[0]

    shared = None
    for k in range(STEPS - 1):
        if k > 0:
            low, high = send(hi, up), send(lo, down)
            near = near_call(lo, hi)
        outs = [TILE, TILE] + ([(2, 2, TX, AY, AZ)] if k == 1 else [])
        new = call(step_kernel, 9, outs)(plan, near, lo, hi, lo_b, hi_b, low, high, coef, inj[k])
        if k == 1:
            shared = send(new[2], swap)
        lo_b, hi_b, lo, hi = lo, hi, new[0], new[1]
    low, high = send(hi, up), send(lo, down)
    near = near_call(lo, hi)
    keep, give = call(last_kernel, 10, [(2,) + PART] * 2, [(2, TX, AY, AZ)])(
        plan, near, lo, hi, lo_b, hi_b, low, high, coef, inj[STEPS - 1], shared
    )

    parts = call(total_kernel, 2, [PART] * 4)(plan, keep, send(give, swap))
    got = [send(parts[by], across(by)) for by in range(1, 4)]
    straight, last, free = call(owners_kernel, 4, [(2,) + PART] * 3)(plan, parts[0], *got)
    last_came = send(last, down)
    free_came = turn_image(free, aper % 2, turn_all)
    keep, give = call(image_kernel, 4, [PART] * 2)(plan, straight, last, last_came, free_came)
    return call(join_kernel, 2, [(TX, AY, AZ)])(plan, keep, send(give, swap))[0]


def solution(mesh):
    model = P(("shot", "aper"), None, None)
    field = P("shot", None, "aper", None, None)
    return jax.shard_map(
        local,
        mesh=mesh,
        in_specs=(model,) * 4 + (field,) * 4 + (P(),) * 5,
        out_specs=model,
        check_vma=False,
    )
```

```python
import jax
import jax.numpy as jnp
from jax import lax
from jax.experimental import pallas as pl
from jax.experimental.pallas import tpu as pltpu
from jax.sharding import PartitionSpec as P

second_coef = (-205.0 / 72.0, 8.0 / 5.0, -1.0 / 5.0, 8.0 / 315.0, -1.0 / 560.0)
first_coef = (4.0 / 5.0, -1.0 / 5.0, 4.0 / 105.0, -1.0 / 280.0)

AXES = ("shot", "aper")
STEPS = 4
TX = 4
AY = 32
AZ = 256
HALF = 128
HALF_Y = AY // 2
F32 = jnp.float32
VMEM = pl.BlockSpec(memory_space=pltpu.VMEM)
SMEM = pl.BlockSpec(memory_space=pltpu.SMEM)


def device(x, core, y, z):
    return ((x % 2) * 2 + core) * 32 + ((z % 4) * 4 + y % 4) * 2 + x // 2


def everyone():
    return [(x, c, y, z) for x in range(4) for c in range(2) for y in range(4) for z in range(4)]


def pairs_of(rule):
    pairs = [(device(*d), device(*rule(*d))) for d in everyone()]
    assert sorted(t for _, t in pairs) == list(range(128))
    assert all(s != t for s, t in pairs)
    return pairs


def send(value, pairs):
    return lax.ppermute(value, AXES, pairs)


def other_core():
    return pairs_of(lambda x, c, y, z: (x, 1 - c, y, z))


def state_first():
    def rule(x, c, y, z):
        t = {(0, 0): (0, 1), (0, 1): (1, 1), (1, 0): (0, 0), (1, 1): (1, 0)}[(x // 2, c)]
        return (2 * t[0] + x % 2, t[1], y, z)

    return pairs_of(rule)


def state_second():
    return [
        (device(x, c, y, z), device((x + 2) % 4, 1 - c, y, z)) for x, c, y, z in everyone() if x // 2 != c
    ]


def across(by):
    return pairs_of(lambda x, c, y, z: ((x + by) % 4, c, y, z))


def rolled(by_low, by_high):
    def rule(x, c, y, z):
        j = (4 * z + y + (by_high if x // 2 else by_low)) % 16
        return (x, c, j % 4, j // 4)

    return pairs_of(rule)


def z_plus(pair, d, lane):
    a, b = pair
    ra, rb = pltpu.roll(a, HALF - d, 1), pltpu.roll(b, HALF - d, 1)
    keep = lane < HALF - d
    return jnp.where(keep, ra, rb), jnp.where(keep, rb, 0.0)


def z_minus(pair, d, lane):
    a, b = pair
    ra, rb = pltpu.roll(a, d, 1), pltpu.roll(b, d, 1)
    keep = lane >= d
    return jnp.where(keep, ra, 0.0), jnp.where(keep, rb, ra)


def second_z(pair, lane):
    out = [second_coef[0] * v for v in pair]
    for d in range(1, 5):
        up, down = z_plus(pair, d, lane), z_minus(pair, d, lane)
        out = [o + second_coef[d] * (u + w) for o, u, w in zip(out, up, down)]
    return out


def first_z(pair, lane):
    out = None
    for d in range(1, 5):
        up, down = z_plus(pair, d, lane), z_minus(pair, d, lane)
        term = [first_coef[d - 1] * (u - w) for u, w in zip(up, down)]
        out = term if out is None else [o + t for o, t in zip(out, term)]
    return out


def second_y(pair, row):
    out = []
    for f in pair:
        acc = second_coef[0] * f
        for d in range(1, 5):
            up = jnp.where(row < AY - d, pltpu.roll(f, AY - d, 0), 0.0)
            down = jnp.where(row >= d, pltpu.roll(f, d, 0), 0.0)
            acc = acc + second_coef[d] * (up + down)
        out.append(acc)
    return out


CORE, X_HI, BLOCK, STAYS, PARITY_LAST, PARITY_FREE, GROUP = range(7)
PARITY, ROLE_TO, SIDE, SOURCE, OWNER, ROLE_FROM = 12, 16, 20, 24, 28, 32


def plan_values(ids, offsets):
    shot, aper = ids[0], ids[1]
    core, x_lo, x_hi = shot & 1, shot >> 1, aper & 1
    x = 2 * x_hi + x_lo
    z, y = aper >> 3, (aper >> 1) & 3
    block = 4 * z + y
    turns = [o & 31 for o in offsets]

    def of(values, g):
        return jnp.where(g < 2, jnp.where(g == 0, values[0], values[1]), jnp.where(g == 2, values[2], values[3]))

    def first(flags):
        return jnp.where(flags[0], 0, jnp.where(flags[1], 1, jnp.where(flags[2], 2, 3)))

    def group_of(x):
        return 2 * (x & 1) + (x >> 1)

    last = first([t == 31 for t in turns])
    free = 6 - first([o == 0 for o in offsets]) - first([o == 96 for o in offsets]) - last
    free_turn = of(turns, free)

    def role_of(g):
        return jnp.where(g == last, 1, jnp.where((g == free) & (free_turn != 0), 2, 0))

    def row_of(g):
        o = of(offsets, g)
        return (o + 2 * block + (x_hi ^ (o & 1))) >> 5

    def parity_before(g):
        o = of(offsets, g)
        return ((o >> 5) + (2 * block + x_hi < (o & 31)).astype(jnp.int32)) & 1

    group = group_of(x)
    offset = of(offsets, group)
    out = {
        CORE: core,
        X_HI: x_hi,
        BLOCK: block,
        GROUP: group,
        STAYS: (x_hi == core).astype(jnp.int32),
        PARITY_LAST: parity_before(last),
        PARITY_FREE: parity_before(free),
    }
    for by in range(4):
        to, came = group_of((x + by) & 3), group_of((x - by) & 3)
        out[PARITY + by] = parity_before(to)
        out[ROLE_TO + by] = role_of(to)
        out[SIDE + by] = (((x + by) & 3) >> 1) ^ (offset & 1)
        out[OWNER + by] = row_of(came) - 2 * x_lo
        out[ROLE_FROM + by] = role_of(came)
    for h in range(2):
        row = (offset + 2 * block + h) >> 5
        out[SOURCE + h] = (x - (2 * (h ^ (offset & 1)) + (row >> 1))) & 3
    return out, free_turn


def fetch(which, choices, sems):
    for k, (a, b, out) in enumerate(choices):

        @pl.when(which)
        def _(a=a, out=out, k=k):
            pltpu.make_async_copy(a, out, sems.at[k]).start()

        @pl.when(jnp.logical_not(which))
        def _(b=b, out=out, k=k):
            pltpu.make_async_copy(b, out, sems.at[k]).start()

    return [pltpu.make_async_copy(a, out, sems.at[k]) for k, (a, _, out) in enumerate(choices)]


def plan_kernel(
    ids,
    offsets,
    velocity,
    epsilon,
    delta,
    angle,
    fwd_now,
    adj_now,
    fwd_before,
    adj_before,
    plan,
    turn_all,
    turn_z,
    turn_y,
    own,
    other,
    one,
    two,
    model_sems,
    state_sems,
):
    model = fetch(
        ids[0] & 1 == 0,
        (
            (delta, velocity, other.at[0]),
            (angle, epsilon, other.at[1]),
            (velocity, delta, own.at[0]),
            (epsilon, angle, own.at[1]),
        ),
        model_sems,
    )
    state = fetch(
        ids[1] & 1 == 0,
        (
            (adj_now.at[0], fwd_now.at[0], one.at[0]),
            (fwd_now.at[0], adj_now.at[0], two.at[0]),
            (adj_before.at[0], fwd_before.at[0], one.at[1]),
            (fwd_before.at[0], adj_before.at[0], two.at[1]),
        ),
        state_sems,
    )
    values, free_turn = plan_values(ids, [offsets[g] for g in range(4)])
    for k, v in values.items():
        plan[k] = v
    turn_all[0] = free_turn
    turn_z[0] = free_turn >> 3
    turn_y[0] = free_turn & 7
    for copy in model + state:
        copy.wait()


def rows_kernel(plan, own, came, last, free):
    mine_last, mine_free = plan[PARITY_LAST] == plan[CORE], plan[PARITY_FREE] == plan[CORE]
    for f in range(2):
        for i in range(TX):
            a, b = own[f, i], came[f, i]
            last[f, i] = jnp.where(mine_last, a, b)
            free[f, i] = jnp.where(mine_free, a, b)


def block_kernel(plan, kept, one, two, *outs):
    first, stays = plan[CORE] == 0, plan[STAYS] == 1
    for t in range(2):
        lo, hi = outs[2 * t : 2 + 2 * t]
        for p in range(2):
            for i in range(TX):
                a, b = one[t, p, i], jnp.where(stays, kept[t, p, i], two[t, p, i])
                lo[p, i] = jnp.where(first, b, a)
                hi[p, i] = jnp.where(first, a, b)


def send_kernel(plan, own, came, last, last_came, free_came, *outs):
    high = plan[X_HI] == 1
    mine = [plan[PARITY + by] == plan[CORE] for by in range(4)]
    role = [plan[ROLE_TO + by] for by in range(4)]
    for f in range(2):
        for i in range(TX):
            a, b = own[f, i], came[f, i]
            turned_last = jnp.where(high, last_came[f, i], last[f, i])
            turned_free = free_came[f, i]
            for by in range(4):
                straight = jnp.where(mine[by], a, b)
                turned = jnp.where(role[by] == 1, turned_last, turned_free)
                outs[by][f, i] = jnp.where(role[by] == 0, straight, turned)


def tiles_kernel(plan, kept, got_1, got_2, got_3, low, high, near, inj, out):
    del low, high, near, inj
    source = [plan[SOURCE + h] for h in range(2)]
    for f in range(2):
        for i in range(TX):
            rows = [kept[f, i], got_1[f, i], got_2[f, i], got_3[f, i]]
            for h in range(2):
                a = jnp.where(source[h] == 0, rows[0], rows[1])
                b = jnp.where(source[h] == 2, rows[2], rows[3])
                out[h, f, i] = jnp.where(source[h] < 2, a, b)


HALVES = (pl.ds(0, HALF), pl.ds(HALF, HALF))


def by_distance(table, d):
    out = 0.0
    for k in range(1, 5):
        out = jnp.where(d == k, table[k], out)
    return out


def near_kernel(lo, hi, out, ext):
    lane = lax.broadcasted_iota(jnp.int32, (AY, HALF), 1)
    row = lax.broadcasted_iota(jnp.int32, (AY, HALF), 0)
    for p in range(2):
        for i in range(TX):
            ext[p, i] = jnp.zeros((AY, AZ), F32)
            ext[p, TX + i] = lo[p, i]
            ext[p, 2 * TX + i] = hi[p, i]
            ext[p, 3 * TX + i] = jnp.zeros((AY, AZ), F32)

    def one(r, carry):
        for p in range(2):
            mid = [ext[p, r + TX, :, h] for h in HALVES]
            for s, h in enumerate(HALVES):
                curve, slope = second_coef[0] * mid[s], None
                for d in range(1, 5):
                    ahead, behind = ext[p, r + TX + d, :, h], ext[p, r + TX - d, :, h]
                    curve = curve + second_coef[d] * (ahead + behind)
                    term = first_coef[d - 1] * (ahead - behind)
                    slope = term if slope is None else slope + term
                out[4 * p, r, :, h] = curve
                out[4 * p + 1, r, :, h] = slope
            depth = second_z(mid, lane)
            for s, h in enumerate(HALVES):
                out[4 * p + 2, r, :, h] = depth[s]
            if p == 0:
                across = second_y(mid, row)
                for s, h in enumerate(HALVES):
                    out[3, r, :, h] = depth[s] + across[s]
        return carry

    lax.fori_loop(0, 2 * TX, one, 0)


def far_rows(plan, near, lo, hi, lo_b, hi_b, low, high, coef, inj, emit):
    lane = lax.broadcasted_iota(jnp.int32, (AY, HALF), 1)
    first_of = (0.0,) + first_coef
    for t, (mid_ref, back, halo) in enumerate(((lo, lo_b, low), (hi, hi_b, high))):
        inside = jnp.where(plan[BLOCK] == (0, 15)[t], 0.0, 1.0)

        def one(i, carry, t=t, mid_ref=mid_ref, back=back, halo=halo, inside=inside):
            r = t * TX + i
            scales = []
            for k in range(TX):
                d = TX + (i - k if t == 0 else k - i)
                sign = inside * (-1.0, 1.0)[t]
                scales.append((inside * by_distance(second_coef, d), sign * by_distance(first_of, d)))
            sums = []
            for p in range(2):
                curve, slope = [], []
                for h in HALVES:
                    c, s = near[4 * p, r, :, h], near[4 * p + 1, r, :, h]
                    for k in range(TX):
                        value = halo[p, k, :, h]
                        c = c + scales[k][0] * value
                        s = s + scales[k][1] * value
                    curve.append(c)
                    slope.append(s)
                sums.append((curve, first_z(slope, lane)))
            (xp, cp), (xq, cq) = sums
            for s, h in enumerate(HALVES):
                aniso, coupled, square = coef[0, r, :, h], coef[1, r, :, h], coef[2, r, :, h]
                sine, cosine, double = coef[3, r, :, h], coef[4, r, :, h], coef[5, r, :, h]
                axial_p = sine * xp[s] + cosine * near[2, r, :, h] + double * cp[s]
                plane_p = xp[s] + near[3, r, :, h] - axial_p
                axial_q = sine * xq[s] + cosine * near[6, r, :, h] + double * cq[s]
                add = inj[r, :, h]
                new_p = 2.0 * mid_ref[0, i, :, h] - back[0, i, :, h] + aniso * plane_p + coupled * axial_q + add
                new_q = 2.0 * mid_ref[1, i, :, h] - back[1, i, :, h] + coupled * plane_p + square * axial_q + add
                emit(t, i, h, new_p, new_q)
            return carry

        lax.fori_loop(0, TX, one, 0, unroll=4)


def step_kernel(plan, near, lo, hi, lo_b, hi_b, low, high, coef, inj, new_lo, new_hi, *packed):
    def emit(t, i, h, new_p, new_q):
        out = (new_lo, new_hi)[t]
        out[0, i, :, h] = new_p
        out[1, i, :, h] = new_q
        for p in packed:
            p[0, t, i, :, h] = (lo, hi)[t][0, i, :, h]
            p[1, t, i, :, h] = new_p

    far_rows(plan, near, lo, hi, lo_b, hi_b, low, high, coef, inj, emit)


def last_kernel(plan, near, lo, hi, lo_b, hi_b, low, high, coef, inj, other, keep, give, part):
    def emit(t, i, h, new_p, new_q):
        del new_q
        part[t, i, :, h] = new_p * other[0, t, i, :, h] + (lo, hi)[t][0, i, :, h] * other[1, t, i, :, h]

    far_rows(plan, near, lo, hi, lo_b, hi_b, low, high, coef, inj, emit)
    first = plan[CORE] == 0
    for t in range(2):
        for i in range(TX):
            low_y, high_y = part[t, i, :HALF_Y], part[t, i, HALF_Y:]
            keep[t, i] = jnp.where(first, low_y, high_y)
            give[t, i] = jnp.where(first, high_y, low_y)


def total_kernel(plan, keep, came, *outs):
    for i in range(TX):
        lo = keep[0, i] + came[0, i]
        hi = keep[1, i] + came[1, i]
        for by in range(4):
            outs[by][i] = jnp.where(plan[SIDE + by] == 0, lo, hi)


def owners_kernel(plan, kept, got_1, got_2, got_3, straight, last, free):
    for i in range(TX):
        parts = [kept[i], got_1[i], got_2[i], got_3[i]]
        for k, out in enumerate((straight, last, free)):
            for core in range(2):
                acc = jnp.zeros_like(parts[0])
                for by in range(4):
                    ours = (plan[OWNER + by] == core) & (plan[ROLE_FROM + by] == k)
                    acc = acc + jnp.where(ours, parts[by], 0.0)
                out[core, i] = acc


def image_kernel(plan, straight, last, last_came, free_came, keep, give):
    high, first = plan[X_HI] == 1, plan[CORE] == 0
    for i in range(TX):
        sums = []
        for core in range(2):
            turned = jnp.where(high, last_came[core, i], last[core, i])
            sums.append(straight[core, i] + turned + free_came[core, i])
        keep[i] = jnp.where(first, sums[0], sums[1])
        give[i] = jnp.where(first, sums[1], sums[0])


def join_kernel(plan, keep, came, out):
    first = plan[CORE] == 0
    for i in range(TX):
        out[i, :HALF_Y] = jnp.where(first, keep[i], came[i])
        out[i, HALF_Y:] = jnp.where(first, came[i], keep[i])


def inject_kernel(plan, source, wavelet, cells, traces, *outs):
    group, forward, base = plan[GROUP], plan[CORE] == 0, 8 * plan[BLOCK]
    count = cells.shape[2]
    lane = lax.broadcasted_iota(jnp.int32, (1, count), 1)
    x, y, depth = (
        jnp.where(
            forward,
            jnp.where(lane == 0, source[group, f], -1),
            cells[f, pl.ds(group, 1), :],
        )
        for f in range(3)
    )
    here = (x >= base) & (x < base + 8)
    spot = jnp.where(here, (x - base) * AY + y, -1)
    which = (lax.broadcasted_iota(jnp.int32, (8 * AY, count), 0) == spot).astype(F32)
    level = lax.broadcasted_iota(jnp.int32, (AZ, count), 0) == depth
    for k in range(STEPS):
        amounts = jnp.where(forward, wavelet[group, k], traces[group, pl.ds(k, 1), :])
        values = jnp.where(level, amounts, 0.0)
        flat = lax.dot_general(
            which,
            values,
            (((1,), (1,)), ((), ())),
            precision=lax.Precision.HIGHEST,
            preferred_element_type=F32,
        )
        for i in range(8):
            outs[k][i] = flat[i * AY : (i + 1) * AY, :]


def sine_cosine(angle):
    sq = angle * angle
    sine = -1.0 / 39916800.0
    for c in (1.0 / 362880.0, -1.0 / 5040.0, 1.0 / 120.0, -1.0 / 6.0, 1.0):
        sine = sine * sq + c
    cosine = 1.0 / 479001600.0
    for c in (-1.0 / 3628800.0, 1.0 / 40320.0, -1.0 / 720.0, 1.0 / 24.0, -0.5, 1.0):
        cosine = cosine * sq + c
    return sine * angle, cosine


def coef_kernel(plan, own, other, out):
    core = plan[CORE]
    for t in range(2):

        def tile(i, carry, t=t):
            mine = [own[t, f, i] for f in range(2)]
            theirs = [other[t, f, i] for f in range(2)]
            velocity = jnp.where(core == 0, mine[0], theirs[0])
            epsilon = jnp.where(core == 0, mine[1], theirs[1])
            delta = jnp.where(core == 0, theirs[0], mine[0])
            angle = jnp.where(core == 0, theirs[1], mine[1])
            square = velocity * velocity
            sine, cosine = sine_cosine(angle)
            k = t * TX + i
            out[0, k] = square * (1.0 + 2.0 * epsilon)
            out[1, k] = square * jnp.sqrt(1.0 + 2.0 * delta)
            out[2, k] = square
            out[3, k] = sine * sine
            out[4, k] = cosine * cosine
            out[5, k] = 2.0 * sine * cosine
            return carry

        lax.fori_loop(0, TX, tile, 0)


HBM = pl.BlockSpec(memory_space=pltpu.HBM)
LIMIT = pltpu.CompilerParams(vmem_limit_bytes=4 * 1024 * 1024)


def in_hbm(value):
    return pltpu.with_memory_space_constraint(value, pltpu.HBM)


def call(kernel, n_in, outs, scratch=()):
    return pl.pallas_call(
        kernel,
        out_shape=[jax.ShapeDtypeStruct(s, F32) for s in outs],
        in_specs=[SMEM] + [VMEM] * n_in,
        out_specs=[VMEM] * len(outs),
        scratch_shapes=[pltpu.VMEM(s, F32) for s in scratch],
        compiler_params=LIMIT,
    )


TILE = (2, TX, AY, AZ)
PART = (TX, HALF_Y, AZ)


def turn_model(value, x_hi, turn_z, turn_y):
    def roll(v, by):
        return send(v, rolled(-by, -by)) if by else v

    def columns(v, r):
        if r == 1:
            return jnp.where(x_hi == 1, v, roll(v, 1))
        if r % 2 == 0:
            return roll(v, r // 2)
        return send(v, rolled(-(r // 2 + 1), -(r // 2)))

    value = lax.switch(turn_z[0], [lambda v, k=k: roll(v, 4 * k) for k in range(4)], value)
    return lax.switch(turn_y[0], [lambda v, r=r: columns(v, r) for r in range(8)], value)


def turn_image(value, x_hi, free_turn):
    def roll(v, by):
        if by % 16 == 0:
            return v
        return roll(roll(v, 8), 7) if by == 15 else send(v, rolled(by, by))

    def columns(v, r):
        low, high = (r + 1) // 2, r // 2
        if r % 2 == 0:
            return roll(v, high)
        if r in (1, 15, 17, 29, 31):
            return jnp.where(x_hi == 1, roll(v, high), roll(v, low))
        return send(v, rolled(low, high))

    return lax.switch(free_turn[0], [lambda v, r=r: columns(v, r) for r in range(32)], value)


def local(
    velocity,
    thomsen_epsilon,
    thomsen_delta,
    tilt_angle,
    fwd_now,
    fwd_before,
    adj_now,
    adj_before,
    wavelet,
    traces,
    offsets,
    source_cell,
    receiver_cell,
):
    shot, aper = lax.axis_index("shot"), lax.axis_index("aper")
    ids = jnp.stack([shot, aper]).astype(jnp.int32)
    swap, up, down = other_core(), rolled(1, 1), rolled(-1, -1)

    plan, turn_all, turn_z, turn_y, own, other, one, two = pl.pallas_call(
        plan_kernel,
        out_shape=[jax.ShapeDtypeStruct((n,), jnp.int32) for n in (40, 1, 1, 1)]
        + [jax.ShapeDtypeStruct(TILE, F32)] * 2
        + [jax.ShapeDtypeStruct((2,) + TILE, F32)] * 2,
        in_specs=[SMEM] * 2 + [HBM] * 8,
        out_specs=[SMEM] * 4 + [VMEM] * 4,
        scratch_shapes=[pltpu.SemaphoreType.DMA((4,))] * 2,
        compiler_params=LIMIT,
    )(
        ids,
        offsets,
        *(in_hbm(v) for v in (velocity, thomsen_epsilon, thomsen_delta, tilt_angle)),
        *(in_hbm(v) for v in (fwd_now, adj_now, fwd_before, adj_before)),
    )
    came = send(other, swap)
    got_one, got_two = send(one, state_first()), send(two, state_second())

    last, free = call(rows_kernel, 2, [TILE] * 2)(plan, own, came)
    last_came = send(last, up)
    free_came = turn_model(free, aper % 2, turn_z, turn_y)
    rows = call(send_kernel, 5, [TILE] * 4)(plan, own, came, last, last_came, free_came)
    got = [send(rows[by], across(by)) for by in range(1, 4)]
    lo, hi, lo_b, hi_b = call(block_kernel, 3, [TILE] * 4)(plan, two, got_one, got_two)
    inj = pl.pallas_call(
        inject_kernel,
        out_shape=[jax.ShapeDtypeStruct((8, AY, AZ), F32)] * STEPS,
        in_specs=[SMEM] * 3 + [VMEM] * 2,
        out_specs=[VMEM] * STEPS,
        compiler_params=LIMIT,
    )(plan, source_cell, wavelet, jnp.transpose(receiver_cell, (2, 0, 1)), traces)

    near_call = pl.pallas_call(
        near_kernel,
        out_shape=jax.ShapeDtypeStruct((7, 8, AY, AZ), F32),
        in_specs=[VMEM] * 2,
        out_specs=VMEM,
        scratch_shapes=[pltpu.VMEM((2, 4 * TX, AY, AZ), F32)],
        compiler_params=LIMIT,
    )
    near = near_call(lo, hi)
    low, high = send(hi, up), send(lo, down)
    tiles = call(tiles_kernel, 8, [(2,) + TILE])(
        plan, rows[0], *got, low, high, near, inj[0]
    )[0]
    coef = call(coef_kernel, 2, [(6, 8, AY, AZ)])(plan, tiles, send(tiles, swap))[0]

    shared = None
    for k in range(STEPS - 1):
        if k > 0:
            low, high = send(hi, up), send(lo, down)
            near = near_call(lo, hi)
        outs = [TILE, TILE] + ([(2, 2, TX, AY, AZ)] if k == 1 else [])
        new = call(step_kernel, 9, outs)(plan, near, lo, hi, lo_b, hi_b, low, high, coef, inj[k])
        if k == 1:
            shared = send(new[2], swap)
        lo_b, hi_b, lo, hi = lo, hi, new[0], new[1]
    low, high = send(hi, up), send(lo, down)
    near = near_call(lo, hi)
    keep, give = call(last_kernel, 10, [(2,) + PART] * 2, [(2, TX, AY, AZ)])(
        plan, near, lo, hi, lo_b, hi_b, low, high, coef, inj[STEPS - 1], shared
    )

    parts = call(total_kernel, 2, [PART] * 4)(plan, keep, send(give, swap))
    got = [send(parts[by], across(by)) for by in range(1, 4)]
    straight, last, free = call(owners_kernel, 4, [(2,) + PART] * 3)(plan, parts[0], *got)
    last_came = send(last, down)
    free_came = turn_image(free, aper % 2, turn_all)
    keep, give = call(image_kernel, 4, [PART] * 2)(plan, straight, last, last_came, free_came)
    return call(join_kernel, 2, [(TX, AY, AZ)])(plan, keep, send(give, swap))[0]


def solution(mesh):
    model = P(("shot", "aper"), None, None)
    field = P("shot", None, "aper", None, None)
    return jax.shard_map(
        local,
        mesh=mesh,
        in_specs=(model,) * 4 + (field,) * 4 + (P(),) * 5,
        out_specs=model,
        check_vma=False,
    )
```

```python
import functools

import jax
import jax.numpy as jnp
from jax import lax
from jax.experimental import pallas as pl
from jax.experimental.pallas import tpu as pltpu
from jax.sharding import PartitionSpec as P

second_coef = (-205.0 / 72.0, 8.0 / 5.0, -1.0 / 5.0, 8.0 / 315.0, -1.0 / 560.0)
first_coef = (4.0 / 5.0, -1.0 / 5.0, 4.0 / 105.0, -1.0 / 280.0)

AXES = ("shot", "aper")
STEPS = 4
TX = 4
AY = 32
AZ = 256
HALF = 128
HALF_Y = AY // 2
F32 = jnp.float32
VMEM = pl.BlockSpec(memory_space=pltpu.VMEM)
SMEM = pl.BlockSpec(memory_space=pltpu.SMEM)


def device(x, core, y, z):
    return ((x % 2) * 2 + core) * 32 + ((z % 4) * 4 + y % 4) * 2 + x // 2


def everyone():
    return [(x, c, y, z) for x in range(4) for c in range(2) for y in range(4) for z in range(4)]


def pairs_of(rule):
    pairs = [(device(*d), device(*rule(*d))) for d in everyone()]
    assert sorted(t for _, t in pairs) == list(range(128))
    assert all(s != t for s, t in pairs)
    return pairs


def send(value, pairs):
    return lax.ppermute(value, AXES, pairs)


def other_core():
    return pairs_of(lambda x, c, y, z: (x, 1 - c, y, z))


def state_first():
    def rule(x, c, y, z):
        t = {(0, 0): (0, 1), (0, 1): (1, 1), (1, 0): (0, 0), (1, 1): (1, 0)}[(x // 2, c)]
        return (2 * t[0] + x % 2, t[1], y, z)

    return pairs_of(rule)


def state_second():
    return [
        (device(x, c, y, z), device((x + 2) % 4, 1 - c, y, z)) for x, c, y, z in everyone() if x // 2 != c
    ]


def across(by):
    return pairs_of(lambda x, c, y, z: ((x + by) % 4, c, y, z))


def rolled(by_low, by_high):
    def rule(x, c, y, z):
        j = (4 * z + y + (by_high if x // 2 else by_low)) % 16
        return (x, c, j % 4, j // 4)

    return pairs_of(rule)


def z_plus(pair, d, lane):
    a, b = pair
    ra, rb = pltpu.roll(a, HALF - d, 1), pltpu.roll(b, HALF - d, 1)
    keep = lane < HALF - d
    return jnp.where(keep, ra, rb), jnp.where(keep, rb, 0.0)


def z_minus(pair, d, lane):
    a, b = pair
    ra, rb = pltpu.roll(a, d, 1), pltpu.roll(b, d, 1)
    keep = lane >= d
    return jnp.where(keep, ra, 0.0), jnp.where(keep, rb, ra)


def second_z(pair, lane):
    out = [second_coef[0] * v for v in pair]
    for d in range(1, 5):
        up, down = z_plus(pair, d, lane), z_minus(pair, d, lane)
        out = [o + second_coef[d] * (u + w) for o, u, w in zip(out, up, down)]
    return out


def first_z(pair, lane):
    out = None
    for d in range(1, 5):
        up, down = z_plus(pair, d, lane), z_minus(pair, d, lane)
        term = [first_coef[d - 1] * (u - w) for u, w in zip(up, down)]
        out = term if out is None else [o + t for o, t in zip(out, term)]
    return out


def second_y(pair, row):
    out = []
    for f in pair:
        acc = second_coef[0] * f
        for d in range(1, 5):
            up = jnp.where(row < AY - d, pltpu.roll(f, AY - d, 0), 0.0)
            down = jnp.where(row >= d, pltpu.roll(f, d, 0), 0.0)
            acc = acc + second_coef[d] * (up + down)
        out.append(acc)
    return out


CORE, X_HI, BLOCK, STAYS, PARITY_LAST, PARITY_FREE, GROUP = range(7)
PARITY, ROLE_TO, SIDE, SOURCE, OWNER, ROLE_FROM = 12, 16, 20, 24, 28, 32


def plan_values(ids, offsets):
    shot, aper = ids[0], ids[1]
    core, x_lo, x_hi = shot & 1, shot >> 1, aper & 1
    x = 2 * x_hi + x_lo
    z, y = aper >> 3, (aper >> 1) & 3
    block = 4 * z + y
    turns = [o & 31 for o in offsets]

    def of(values, g):
        return jnp.where(g < 2, jnp.where(g == 0, values[0], values[1]), jnp.where(g == 2, values[2], values[3]))

    def first(flags):
        return jnp.where(flags[0], 0, jnp.where(flags[1], 1, jnp.where(flags[2], 2, 3)))

    def group_of(x):
        return 2 * (x & 1) + (x >> 1)

    last = first([t == 31 for t in turns])
    free = 6 - first([o == 0 for o in offsets]) - first([o == 96 for o in offsets]) - last
    free_turn = of(turns, free)

    def role_of(g):
        return jnp.where(g == last, 1, jnp.where((g == free) & (free_turn != 0), 2, 0))

    def row_of(g):
        o = of(offsets, g)
        return (o + 2 * block + (x_hi ^ (o & 1))) >> 5

    def parity_before(g):
        o = of(offsets, g)
        return ((o >> 5) + (2 * block + x_hi < (o & 31)).astype(jnp.int32)) & 1

    group = group_of(x)
    offset = of(offsets, group)
    out = {
        CORE: core,
        X_HI: x_hi,
        BLOCK: block,
        GROUP: group,
        STAYS: (x_hi == core).astype(jnp.int32),
        PARITY_LAST: parity_before(last),
        PARITY_FREE: parity_before(free),
    }
    for by in range(4):
        to, came = group_of((x + by) & 3), group_of((x - by) & 3)
        out[PARITY + by] = parity_before(to)
        out[ROLE_TO + by] = role_of(to)
        out[SIDE + by] = (((x + by) & 3) >> 1) ^ (offset & 1)
        out[OWNER + by] = row_of(came) - 2 * x_lo
        out[ROLE_FROM + by] = role_of(came)
    for h in range(2):
        row = (offset + 2 * block + h) >> 5
        out[SOURCE + h] = (x - (2 * (h ^ (offset & 1)) + (row >> 1))) & 3
    return out, free_turn


def fetch(which, choices, sems):
    for k, (a, b, out) in enumerate(choices):

        @pl.when(which)
        def _(a=a, out=out, k=k):
            pltpu.make_async_copy(a, out, sems.at[k]).start()

        @pl.when(jnp.logical_not(which))
        def _(b=b, out=out, k=k):
            pltpu.make_async_copy(b, out, sems.at[k]).start()

    return [pltpu.make_async_copy(a, out, sems.at[k]) for k, (a, _, out) in enumerate(choices)]


def plan_kernel(
    ids,
    offsets,
    velocity,
    epsilon,
    delta,
    angle,
    fwd_now,
    adj_now,
    fwd_before,
    adj_before,
    plan,
    turn_all,
    turn_z,
    turn_y,
    own,
    other,
    one,
    two,
    model_sems,
    state_sems,
):
    model = fetch(
        ids[0] & 1 == 0,
        (
            (delta, velocity, other.at[0]),
            (angle, epsilon, other.at[1]),
            (velocity, delta, own.at[0]),
            (epsilon, angle, own.at[1]),
        ),
        model_sems,
    )
    state = fetch(
        ids[1] & 1 == 0,
        (
            (adj_now.at[0], fwd_now.at[0], one.at[0]),
            (fwd_now.at[0], adj_now.at[0], two.at[0]),
            (adj_before.at[0], fwd_before.at[0], one.at[1]),
            (fwd_before.at[0], adj_before.at[0], two.at[1]),
        ),
        state_sems,
    )
    values, free_turn = plan_values(ids, [offsets[g] for g in range(4)])
    for k, v in values.items():
        plan[k] = v
    turn_all[0] = free_turn
    turn_z[0] = free_turn >> 3
    turn_y[0] = free_turn & 7
    for copy in model + state:
        copy.wait()


def rows_kernel(plan, own, came, last, free):
    mine_last, mine_free = plan[PARITY_LAST] == plan[CORE], plan[PARITY_FREE] == plan[CORE]
    for f in range(2):
        for i in range(TX):
            a, b = own[f, i], came[f, i]
            last[f, i] = jnp.where(mine_last, a, b)
            free[f, i] = jnp.where(mine_free, a, b)


def block_kernel(plan, kept, one, two, *outs):
    first, stays = plan[CORE] == 0, plan[STAYS] == 1
    for t in range(2):
        lo, hi = outs[2 * t : 2 + 2 * t]
        for p in range(2):
            for i in range(TX):
                a, b = one[t, p, i], jnp.where(stays, kept[t, p, i], two[t, p, i])
                lo[p, i] = jnp.where(first, b, a)
                hi[p, i] = jnp.where(first, a, b)


def send_kernel(plan, own, came, last, last_came, free_came, *outs):
    high = plan[X_HI] == 1
    mine = [plan[PARITY + by] == plan[CORE] for by in range(4)]
    role = [plan[ROLE_TO + by] for by in range(4)]
    for f in range(2):
        for i in range(TX):
            a, b = own[f, i], came[f, i]
            turned_last = jnp.where(high, last_came[f, i], last[f, i])
            turned_free = free_came[f, i]
            for by in range(4):
                straight = jnp.where(mine[by], a, b)
                turned = jnp.where(role[by] == 1, turned_last, turned_free)
                outs[by][f, i] = jnp.where(role[by] == 0, straight, turned)


def tiles_kernel(plan, kept, got_1, got_2, got_3, low, high, near, inj, out):
    del low, high, near, inj
    source = [plan[SOURCE + h] for h in range(2)]
    for f in range(2):
        for i in range(TX):
            rows = [kept[f, i], got_1[f, i], got_2[f, i], got_3[f, i]]
            for h in range(2):
                a = jnp.where(source[h] == 0, rows[0], rows[1])
                b = jnp.where(source[h] == 2, rows[2], rows[3])
                out[h, f, i] = jnp.where(source[h] < 2, a, b)


HALVES = (pl.ds(0, HALF), pl.ds(HALF, HALF))


def by_distance(table, d):
    out = 0.0
    for k in range(1, 5):
        out = jnp.where(d == k, table[k], out)
    return out


def near_kernel(lo, hi, out, ext):
    lane = lax.broadcasted_iota(jnp.int32, (AY, HALF), 1)
    row = lax.broadcasted_iota(jnp.int32, (AY, HALF), 0)
    for p in range(2):
        for i in range(TX):
            ext[p, i] = jnp.zeros((AY, AZ), F32)
            ext[p, TX + i] = lo[p, i]
            ext[p, 2 * TX + i] = hi[p, i]
            ext[p, 3 * TX + i] = jnp.zeros((AY, AZ), F32)

    def one(r, carry):
        for p in range(2):
            mid = [ext[p, r + TX, :, h] for h in HALVES]
            for s, h in enumerate(HALVES):
                curve, slope = second_coef[0] * mid[s], None
                for d in range(1, 5):
                    ahead, behind = ext[p, r + TX + d, :, h], ext[p, r + TX - d, :, h]
                    curve = curve + second_coef[d] * (ahead + behind)
                    term = first_coef[d - 1] * (ahead - behind)
                    slope = term if slope is None else slope + term
                out[4 * p, r, :, h] = curve
                out[4 * p + 1, r, :, h] = slope
            depth = second_z(mid, lane)
            for s, h in enumerate(HALVES):
                out[4 * p + 2, r, :, h] = depth[s]
            if p == 0:
                across = second_y(mid, row)
                for s, h in enumerate(HALVES):
                    out[3, r, :, h] = depth[s] + across[s]
        return carry

    lax.fori_loop(0, 2 * TX, one, 0)


def far_rows(plan, near, tiles, coef, inj, emit):
    lane = lax.broadcasted_iota(jnp.int32, (AY, HALF), 1)
    first_of = (0.0,) + first_coef
    for t, mid_ref, back, halo in tiles:
        inside = jnp.where(plan[BLOCK] == (0, 15)[t], 0.0, 1.0)

        def one(i, carry, t=t, mid_ref=mid_ref, back=back, halo=halo, inside=inside):
            r = t * TX + i
            scales = []
            for k in range(TX):
                d = TX + (i - k if t == 0 else k - i)
                sign = inside * (-1.0, 1.0)[t]
                scales.append((inside * by_distance(second_coef, d), sign * by_distance(first_of, d)))
            sums = []
            for p in range(2):
                curve, slope = [], []
                for h in HALVES:
                    c, s = near[4 * p, r, :, h], near[4 * p + 1, r, :, h]
                    for k in range(TX):
                        value = halo[p, k, :, h]
                        c = c + scales[k][0] * value
                        s = s + scales[k][1] * value
                    curve.append(c)
                    slope.append(s)
                sums.append((curve, first_z(slope, lane)))
            (xp, cp), (xq, cq) = sums
            for s, h in enumerate(HALVES):
                aniso, coupled, square = coef[0, r, :, h], coef[1, r, :, h], coef[2, r, :, h]
                sine, cosine, double = coef[3, r, :, h], coef[4, r, :, h], coef[5, r, :, h]
                axial_p = sine * xp[s] + cosine * near[2, r, :, h] + double * cp[s]
                plane_p = xp[s] + near[3, r, :, h] - axial_p
                axial_q = sine * xq[s] + cosine * near[6, r, :, h] + double * cq[s]
                add = inj[r, :, h]
                new_p = 2.0 * mid_ref[0, i, :, h] - back[0, i, :, h] + aniso * plane_p + coupled * axial_q + add
                new_q = 2.0 * mid_ref[1, i, :, h] - back[1, i, :, h] + coupled * plane_p + square * axial_q + add
                emit(t, i, h, new_p, new_q)
            return carry

        lax.fori_loop(0, TX, one, 0, unroll=4)


def step_kernel(tile, plan, near, now, before, halo, coef, inj, new, *packed):
    def emit(t, i, h, new_p, new_q):
        new[0, i, :, h] = new_p
        new[1, i, :, h] = new_q
        for p in packed:
            p[0, i, :, h] = now[0, i, :, h]
            p[1, i, :, h] = new_p

    far_rows(plan, near, ((tile, now, before, halo),), coef, inj, emit)


def joining_kernel(plan, near, now, before, halo, coef, inj, hi_packed, new, packed):
    def emit(t, i, h, new_p, new_q):
        new[0, i, :, h] = new_p
        new[1, i, :, h] = new_q
        packed[0, 0, i, :, h] = now[0, i, :, h]
        packed[0, 1, i, :, h] = new_p

    for k in range(2):
        for i in range(TX):
            packed[1, k, i] = hi_packed[k, i]
    far_rows(plan, near, ((0, now, before, halo),), coef, inj, emit)


def last_kernel(plan, near, lo, hi, lo_b, hi_b, low, high, coef, inj, other, keep, give, part):
    def emit(t, i, h, new_p, new_q):
        del new_q
        part[t, i, :, h] = new_p * other[t, 0, i, :, h] + (lo, hi)[t][0, i, :, h] * other[t, 1, i, :, h]

    far_rows(plan, near, ((0, lo, lo_b, low), (1, hi, hi_b, high)), coef, inj, emit)
    first = plan[CORE] == 0
    for t in range(2):
        for i in range(TX):
            low_y, high_y = part[t, i, :HALF_Y], part[t, i, HALF_Y:]
            keep[t, i] = jnp.where(first, low_y, high_y)
            give[t, i] = jnp.where(first, high_y, low_y)


def total_kernel(plan, keep, came, *outs):
    for i in range(TX):
        lo = keep[0, i] + came[0, i]
        hi = keep[1, i] + came[1, i]
        for by in range(4):
            outs[by][i] = jnp.where(plan[SIDE + by] == 0, lo, hi)


def owners_kernel(plan, kept, got_1, got_2, got_3, straight, last, free):
    for i in range(TX):
        parts = [kept[i], got_1[i], got_2[i], got_3[i]]
        for k, out in enumerate((straight, last, free)):
            for core in range(2):
                acc = jnp.zeros_like(parts[0])
                for by in range(4):
                    ours = (plan[OWNER + by] == core) & (plan[ROLE_FROM + by] == k)
                    acc = acc + jnp.where(ours, parts[by], 0.0)
                out[core, i] = acc


def image_kernel(plan, straight, last, last_came, free_came, keep, give):
    high, first = plan[X_HI] == 1, plan[CORE] == 0
    for i in range(TX):
        sums = []
        for core in range(2):
            turned = jnp.where(high, last_came[core, i], last[core, i])
            sums.append(straight[core, i] + turned + free_came[core, i])
        keep[i] = jnp.where(first, sums[0], sums[1])
        give[i] = jnp.where(first, sums[1], sums[0])


def join_kernel(plan, keep, came, out):
    first = plan[CORE] == 0
    for i in range(TX):
        out[i, :HALF_Y] = jnp.where(first, keep[i], came[i])
        out[i, HALF_Y:] = jnp.where(first, came[i], keep[i])


def inject_kernel(plan, source, wavelet, cells, traces, *outs):
    group, forward, base = plan[GROUP], plan[CORE] == 0, 8 * plan[BLOCK]
    count = cells.shape[2]
    lane = lax.broadcasted_iota(jnp.int32, (1, count), 1)
    x, y, depth = (
        jnp.where(
            forward,
            jnp.where(lane == 0, source[group, f], -1),
            cells[f, pl.ds(group, 1), :],
        )
        for f in range(3)
    )
    here = (x >= base) & (x < base + 8)
    spot = jnp.where(here, (x - base) * AY + y, -1)
    which = (lax.broadcasted_iota(jnp.int32, (8 * AY, count), 0) == spot).astype(F32)
    level = lax.broadcasted_iota(jnp.int32, (AZ, count), 0) == depth
    for k in range(STEPS):
        amounts = jnp.where(forward, wavelet[group, k], traces[group, pl.ds(k, 1), :])
        values = jnp.where(level, amounts, 0.0)
        flat = lax.dot_general(
            which,
            values,
            (((1,), (1,)), ((), ())),
            precision=lax.Precision.HIGHEST,
            preferred_element_type=F32,
        )
        for i in range(8):
            outs[k][i] = flat[i * AY : (i + 1) * AY, :]


def sine_cosine(angle):
    sq = angle * angle
    sine = -1.0 / 39916800.0
    for c in (1.0 / 362880.0, -1.0 / 5040.0, 1.0 / 120.0, -1.0 / 6.0, 1.0):
        sine = sine * sq + c
    cosine = 1.0 / 479001600.0
    for c in (-1.0 / 3628800.0, 1.0 / 40320.0, -1.0 / 720.0, 1.0 / 24.0, -0.5, 1.0):
        cosine = cosine * sq + c
    return sine * angle, cosine


def coef_kernel(plan, own, other, out):
    core = plan[CORE]
    for t in range(2):

        def tile(i, carry, t=t):
            mine = [own[t, f, i] for f in range(2)]
            theirs = [other[t, f, i] for f in range(2)]
            velocity = jnp.where(core == 0, mine[0], theirs[0])
            epsilon = jnp.where(core == 0, mine[1], theirs[1])
            delta = jnp.where(core == 0, theirs[0], mine[0])
            angle = jnp.where(core == 0, theirs[1], mine[1])
            square = velocity * velocity
            sine, cosine = sine_cosine(angle)
            k = t * TX + i
            out[0, k] = square * (1.0 + 2.0 * epsilon)
            out[1, k] = square * jnp.sqrt(1.0 + 2.0 * delta)
            out[2, k] = square
            out[3, k] = sine * sine
            out[4, k] = cosine * cosine
            out[5, k] = 2.0 * sine * cosine
            return carry

        lax.fori_loop(0, TX, tile, 0)


HBM = pl.BlockSpec(memory_space=pltpu.HBM)
LIMIT = pltpu.CompilerParams(vmem_limit_bytes=4 * 1024 * 1024)


def in_hbm(value):
    return pltpu.with_memory_space_constraint(value, pltpu.HBM)


def call(kernel, n_in, outs, scratch=()):
    return pl.pallas_call(
        kernel,
        out_shape=[jax.ShapeDtypeStruct(s, F32) for s in outs],
        in_specs=[SMEM] + [VMEM] * n_in,
        out_specs=[VMEM] * len(outs),
        scratch_shapes=[pltpu.VMEM(s, F32) for s in scratch],
        compiler_params=LIMIT,
    )


TILE = (2, TX, AY, AZ)
PART = (TX, HALF_Y, AZ)


def turn_model(value, x_hi, turn_z, turn_y):
    def roll(v, by):
        return send(v, rolled(-by, -by)) if by else v

    def columns(v, r):
        if r == 1:
            return jnp.where(x_hi == 1, v, roll(v, 1))
        if r % 2 == 0:
            return roll(v, r // 2)
        return send(v, rolled(-(r // 2 + 1), -(r // 2)))

    value = lax.switch(turn_z[0], [lambda v, k=k: roll(v, 4 * k) for k in range(4)], value)
    return lax.switch(turn_y[0], [lambda v, r=r: columns(v, r) for r in range(8)], value)


def turn_image(value, x_hi, free_turn):
    def roll(v, by):
        if by % 16 == 0:
            return v
        return roll(roll(v, 8), 7) if by == 15 else send(v, rolled(by, by))

    def columns(v, r):
        low, high = (r + 1) // 2, r // 2
        if r % 2 == 0:
            return roll(v, high)
        if r in (1, 5, 15, 17, 29, 31):
            return jnp.where(x_hi == 1, roll(v, high), roll(v, low))
        return send(v, rolled(low, high))

    return lax.switch(free_turn[0], [lambda v, r=r: columns(v, r) for r in range(32)], value)


def local(
    velocity,
    thomsen_epsilon,
    thomsen_delta,
    tilt_angle,
    fwd_now,
    fwd_before,
    adj_now,
    adj_before,
    wavelet,
    traces,
    offsets,
    source_cell,
    receiver_cell,
):
    shot, aper = lax.axis_index("shot"), lax.axis_index("aper")
    ids = jnp.stack([shot, aper]).astype(jnp.int32)
    swap, up, down = other_core(), rolled(1, 1), rolled(-1, -1)

    plan, turn_all, turn_z, turn_y, own, other, one, two = pl.pallas_call(
        plan_kernel,
        out_shape=[jax.ShapeDtypeStruct((n,), jnp.int32) for n in (40, 1, 1, 1)]
        + [jax.ShapeDtypeStruct(TILE, F32)] * 2
        + [jax.ShapeDtypeStruct((2,) + TILE, F32)] * 2,
        in_specs=[SMEM] * 2 + [HBM] * 8,
        out_specs=[SMEM] * 4 + [VMEM] * 4,
        scratch_shapes=[pltpu.SemaphoreType.DMA((4,))] * 2,
        compiler_params=LIMIT,
    )(
        ids,
        offsets,
        *(in_hbm(v) for v in (velocity, thomsen_epsilon, thomsen_delta, tilt_angle)),
        *(in_hbm(v) for v in (fwd_now, adj_now, fwd_before, adj_before)),
    )
    came = send(other, swap)
    got_one, got_two = send(one, state_first()), send(two, state_second())

    last, free = call(rows_kernel, 2, [TILE] * 2)(plan, own, came)
    last_came = send(last, up)
    free_came = turn_model(free, aper % 2, turn_z, turn_y)
    rows = call(send_kernel, 5, [TILE] * 4)(plan, own, came, last, last_came, free_came)
    got = [send(rows[by], across(by)) for by in range(1, 4)]
    lo, hi, lo_b, hi_b = call(block_kernel, 3, [TILE] * 4)(plan, two, got_one, got_two)
    inj = pl.pallas_call(
        inject_kernel,
        out_shape=[jax.ShapeDtypeStruct((8, AY, AZ), F32)] * STEPS,
        in_specs=[SMEM] * 3 + [VMEM] * 2,
        out_specs=[VMEM] * STEPS,
        compiler_params=LIMIT,
    )(plan, source_cell, wavelet, jnp.transpose(receiver_cell, (2, 0, 1)), traces)

    near_call = pl.pallas_call(
        near_kernel,
        out_shape=jax.ShapeDtypeStruct((7, 8, AY, AZ), F32),
        in_specs=[VMEM] * 2,
        out_specs=VMEM,
        scratch_shapes=[pltpu.VMEM((2, 4 * TX, AY, AZ), F32)],
        compiler_params=LIMIT,
    )
    near = near_call(lo, hi)
    low, high = send(hi, up), send(lo, down)
    tiles = call(tiles_kernel, 8, [(2,) + TILE])(
        plan, rows[0], *got, low, high, near, inj[0]
    )[0]
    coef = call(coef_kernel, 2, [(6, 8, AY, AZ)])(plan, tiles, send(tiles, swap))[0]

    shared = None
    for k in range(STEPS - 1):
        if k > 0:
            low, high = send(hi, up), send(lo, down)
            near = near_call(lo, hi)
        outs = [TILE] * (2 if k == 1 else 1)
        new_hi = call(functools.partial(step_kernel, 1), 6, outs)(plan, near, hi, hi_b, high, coef, inj[k])
        if k == 1:
            new_lo = call(joining_kernel, 7, [TILE, (2,) + TILE])(
                plan, near, lo, lo_b, low, coef, inj[k], new_hi[1]
            )
            shared = send(new_lo[1], swap)
        else:
            new_lo = call(functools.partial(step_kernel, 0), 6, outs)(plan, near, lo, lo_b, low, coef, inj[k])
        lo_b, hi_b, lo, hi = lo, hi, new_lo[0], new_hi[0]
    low, high = send(hi, up), send(lo, down)
    near = near_call(lo, hi)
    keep, give = call(last_kernel, 10, [(2,) + PART] * 2, [(2, TX, AY, AZ)])(
        plan, near, lo, hi, lo_b, hi_b, low, high, coef, inj[STEPS - 1], shared
    )

    parts = call(total_kernel, 2, [PART] * 4)(plan, keep, send(give, swap))
    got = [send(parts[by], across(by)) for by in range(1, 4)]
    straight, last, free = call(owners_kernel, 4, [(2,) + PART] * 3)(plan, parts[0], *got)
    last_came = send(last, down)
    free_came = turn_image(free, aper % 2, turn_all)
    keep, give = call(image_kernel, 4, [PART] * 2)(plan, straight, last, last_came, free_came)
    return call(join_kernel, 2, [(TX, AY, AZ)])(plan, keep, send(give, swap))[0]


def solution(mesh):
    model = P(("shot", "aper"), None, None)
    field = P("shot", None, "aper", None, None)
    return jax.shard_map(
        local,
        mesh=mesh,
        in_specs=(model,) * 4 + (field,) * 4 + (P(),) * 5,
        out_specs=model,
        check_vma=False,
    )
```

```python
import functools

import jax
import jax.numpy as jnp
from jax import lax
from jax.experimental import pallas as pl
from jax.experimental.pallas import tpu as pltpu
from jax.sharding import PartitionSpec as P

second_coef = (-205.0 / 72.0, 8.0 / 5.0, -1.0 / 5.0, 8.0 / 315.0, -1.0 / 560.0)
first_coef = (4.0 / 5.0, -1.0 / 5.0, 4.0 / 105.0, -1.0 / 280.0)

AXES = ("shot", "aper")
STEPS = 4
TX = 4
AY = 32
AZ = 256
HALF = 128
HALF_Y = AY // 2
F32 = jnp.float32
VMEM = pl.BlockSpec(memory_space=pltpu.VMEM)
SMEM = pl.BlockSpec(memory_space=pltpu.SMEM)


def device(x, core, y, z):
    return ((x % 2) * 2 + core) * 32 + ((z % 4) * 4 + y % 4) * 2 + x // 2


def everyone():
    return [(x, c, y, z) for x in range(4) for c in range(2) for y in range(4) for z in range(4)]


def pairs_of(rule):
    pairs = [(device(*d), device(*rule(*d))) for d in everyone()]
    assert sorted(t for _, t in pairs) == list(range(128))
    assert all(s != t for s, t in pairs)
    return pairs


def send(value, pairs):
    return lax.ppermute(value, AXES, pairs)


def other_core():
    return pairs_of(lambda x, c, y, z: (x, 1 - c, y, z))


def state_first():
    def rule(x, c, y, z):
        t = {(0, 0): (0, 1), (0, 1): (1, 1), (1, 0): (0, 0), (1, 1): (1, 0)}[(x // 2, c)]
        return (2 * t[0] + x % 2, t[1], y, z)

    return pairs_of(rule)


def state_second():
    return [
        (device(x, c, y, z), device((x + 2) % 4, 1 - c, y, z)) for x, c, y, z in everyone() if x // 2 != c
    ]


def across(by):
    return pairs_of(lambda x, c, y, z: ((x + by) % 4, c, y, z))


def rolled(by_low, by_high):
    def rule(x, c, y, z):
        j = (4 * z + y + (by_high if x // 2 else by_low)) % 16
        return (x, c, j % 4, j // 4)

    return pairs_of(rule)


def z_plus(pair, d, lane):
    a, b = pair
    ra, rb = pltpu.roll(a, HALF - d, 1), pltpu.roll(b, HALF - d, 1)
    keep = lane < HALF - d
    return jnp.where(keep, ra, rb), jnp.where(keep, rb, 0.0)


def z_minus(pair, d, lane):
    a, b = pair
    ra, rb = pltpu.roll(a, d, 1), pltpu.roll(b, d, 1)
    keep = lane >= d
    return jnp.where(keep, ra, 0.0), jnp.where(keep, rb, ra)


def second_z(pair, lane):
    out = [second_coef[0] * v for v in pair]
    for d in range(1, 5):
        up, down = z_plus(pair, d, lane), z_minus(pair, d, lane)
        out = [o + second_coef[d] * (u + w) for o, u, w in zip(out, up, down)]
    return out


def first_z(pair, lane):
    out = None
    for d in range(1, 5):
        up, down = z_plus(pair, d, lane), z_minus(pair, d, lane)
        term = [first_coef[d - 1] * (u - w) for u, w in zip(up, down)]
        out = term if out is None else [o + t for o, t in zip(out, term)]
    return out


def second_y(pair, row):
    out = []
    for f in pair:
        acc = second_coef[0] * f
        for d in range(1, 5):
            up = jnp.where(row < AY - d, pltpu.roll(f, AY - d, 0), 0.0)
            down = jnp.where(row >= d, pltpu.roll(f, d, 0), 0.0)
            acc = acc + second_coef[d] * (up + down)
        out.append(acc)
    return out


CORE, X_HI, BLOCK, STAYS, PARITY_LAST, PARITY_FREE, GROUP = range(7)
PARITY, ROLE_TO, SIDE, SOURCE, OWNER, ROLE_FROM = 12, 16, 20, 24, 28, 32


def plan_values(ids, offsets):
    shot, aper = ids[0], ids[1]
    core, x_lo, x_hi = shot & 1, shot >> 1, aper & 1
    x = 2 * x_hi + x_lo
    z, y = aper >> 3, (aper >> 1) & 3
    block = 4 * z + y
    turns = [o & 31 for o in offsets]

    def of(values, g):
        return jnp.where(g < 2, jnp.where(g == 0, values[0], values[1]), jnp.where(g == 2, values[2], values[3]))

    def first(flags):
        return jnp.where(flags[0], 0, jnp.where(flags[1], 1, jnp.where(flags[2], 2, 3)))

    def group_of(x):
        return 2 * (x & 1) + (x >> 1)

    last = first([t == 31 for t in turns])
    free = 6 - first([o == 0 for o in offsets]) - first([o == 96 for o in offsets]) - last
    free_turn = of(turns, free)

    def role_of(g):
        return jnp.where(g == last, 1, jnp.where((g == free) & (free_turn != 0), 2, 0))

    def row_of(g):
        o = of(offsets, g)
        return (o + 2 * block + (x_hi ^ (o & 1))) >> 5

    def parity_before(g):
        o = of(offsets, g)
        return ((o >> 5) + (2 * block + x_hi < (o & 31)).astype(jnp.int32)) & 1

    group = group_of(x)
    offset = of(offsets, group)
    out = {
        CORE: core,
        X_HI: x_hi,
        BLOCK: block,
        GROUP: group,
        STAYS: (x_hi == core).astype(jnp.int32),
        PARITY_LAST: parity_before(last),
        PARITY_FREE: parity_before(free),
    }
    for by in range(4):
        to, came = group_of((x + by) & 3), group_of((x - by) & 3)
        out[PARITY + by] = parity_before(to)
        out[ROLE_TO + by] = role_of(to)
        out[SIDE + by] = (((x + by) & 3) >> 1) ^ (offset & 1)
        out[OWNER + by] = row_of(came) - 2 * x_lo
        out[ROLE_FROM + by] = role_of(came)
    for h in range(2):
        row = (offset + 2 * block + h) >> 5
        out[SOURCE + h] = (x - (2 * (h ^ (offset & 1)) + (row >> 1))) & 3
    return out, free_turn


def fetch(which, choices, sems):
    for k, (a, b, out) in enumerate(choices):

        @pl.when(which)
        def _(a=a, out=out, k=k):
            pltpu.make_async_copy(a, out, sems.at[k]).start()

        @pl.when(jnp.logical_not(which))
        def _(b=b, out=out, k=k):
            pltpu.make_async_copy(b, out, sems.at[k]).start()

    return [pltpu.make_async_copy(a, out, sems.at[k]) for k, (a, _, out) in enumerate(choices)]


def plan_kernel(
    ids,
    offsets,
    velocity,
    epsilon,
    delta,
    angle,
    fwd_now,
    adj_now,
    fwd_before,
    adj_before,
    plan,
    turn_all,
    turn_z,
    turn_y,
    own,
    other,
    one,
    two,
    model_sems,
    state_sems,
):
    model = fetch(
        ids[0] & 1 == 0,
        (
            (delta, velocity, other.at[0]),
            (angle, epsilon, other.at[1]),
            (velocity, delta, own.at[0]),
            (epsilon, angle, own.at[1]),
        ),
        model_sems,
    )
    state = fetch(
        ids[1] & 1 == 0,
        (
            (adj_now.at[0], fwd_now.at[0], one.at[0]),
            (fwd_now.at[0], adj_now.at[0], two.at[0]),
            (adj_before.at[0], fwd_before.at[0], one.at[1]),
            (fwd_before.at[0], adj_before.at[0], two.at[1]),
        ),
        state_sems,
    )
    values, free_turn = plan_values(ids, [offsets[g] for g in range(4)])
    for k, v in values.items():
        plan[k] = v
    turn_all[0] = free_turn
    turn_z[0] = free_turn >> 3
    turn_y[0] = free_turn & 7
    for copy in model + state:
        copy.wait()


def rows_kernel(plan, own, came, last, free):
    mine_last, mine_free = plan[PARITY_LAST] == plan[CORE], plan[PARITY_FREE] == plan[CORE]
    for f in range(2):
        for i in range(TX):
            a, b = own[f, i], came[f, i]
            last[f, i] = jnp.where(mine_last, a, b)
            free[f, i] = jnp.where(mine_free, a, b)


def block_kernel(plan, kept, one, two, *outs):
    first, stays = plan[CORE] == 0, plan[STAYS] == 1
    for t in range(2):
        lo, hi = outs[2 * t : 2 + 2 * t]
        for p in range(2):
            for i in range(TX):
                a, b = one[t, p, i], jnp.where(stays, kept[t, p, i], two[t, p, i])
                lo[p, i] = jnp.where(first, b, a)
                hi[p, i] = jnp.where(first, a, b)


def send_kernel(plan, own, came, last, last_came, free_came, *outs):
    high = plan[X_HI] == 1
    mine = [plan[PARITY + by] == plan[CORE] for by in range(4)]
    role = [plan[ROLE_TO + by] for by in range(4)]
    for f in range(2):
        for i in range(TX):
            a, b = own[f, i], came[f, i]
            turned_last = jnp.where(high, last_came[f, i], last[f, i])
            turned_free = free_came[f, i]
            for by in range(4):
                straight = jnp.where(mine[by], a, b)
                turned = jnp.where(role[by] == 1, turned_last, turned_free)
                outs[by][f, i] = jnp.where(role[by] == 0, straight, turned)


def tiles_kernel(plan, kept, got_1, got_2, got_3, low, high, near, inj, out):
    del low, high, near, inj
    source = [plan[SOURCE + h] for h in range(2)]
    for f in range(2):
        for i in range(TX):
            rows = [kept[f, i], got_1[f, i], got_2[f, i], got_3[f, i]]
            for h in range(2):
                a = jnp.where(source[h] == 0, rows[0], rows[1])
                b = jnp.where(source[h] == 2, rows[2], rows[3])
                out[h, f, i] = jnp.where(source[h] < 2, a, b)


HALVES = (pl.ds(0, HALF), pl.ds(HALF, HALF))


def by_distance(table, d):
    out = 0.0
    for k in range(1, 5):
        out = jnp.where(d == k, table[k], out)
    return out


def near_kernel(lo, hi, out, ext):
    lane = lax.broadcasted_iota(jnp.int32, (AY, HALF), 1)
    row = lax.broadcasted_iota(jnp.int32, (AY, HALF), 0)
    for p in range(2):
        for i in range(TX):
            ext[p, i] = jnp.zeros((AY, AZ), F32)
            ext[p, TX + i] = lo[p, i]
            ext[p, 2 * TX + i] = hi[p, i]
            ext[p, 3 * TX + i] = jnp.zeros((AY, AZ), F32)

    def one(r, carry):
        for p in range(2):
            mid = [ext[p, r + TX, :, h] for h in HALVES]
            for s, h in enumerate(HALVES):
                curve, slope = second_coef[0] * mid[s], None
                for d in range(1, 5):
                    ahead, behind = ext[p, r + TX + d, :, h], ext[p, r + TX - d, :, h]
                    curve = curve + second_coef[d] * (ahead + behind)
                    term = first_coef[d - 1] * (ahead - behind)
                    slope = term if slope is None else slope + term
                out[4 * p, r, :, h] = curve
                out[4 * p + 1, r, :, h] = slope
            depth = second_z(mid, lane)
            for s, h in enumerate(HALVES):
                out[4 * p + 2, r, :, h] = depth[s]
            if p == 0:
                across = second_y(mid, row)
                for s, h in enumerate(HALVES):
                    out[3, r, :, h] = depth[s] + across[s]
        return carry

    lax.fori_loop(0, 2 * TX, one, 0)


def far_rows(plan, near, tiles, coef, inj, emit):
    lane = lax.broadcasted_iota(jnp.int32, (AY, HALF), 1)
    first_of = (0.0,) + first_coef
    for t, mid_ref, back, halo in tiles:
        inside = jnp.where(plan[BLOCK] == (0, 15)[t], 0.0, 1.0)

        def one(i, carry, t=t, mid_ref=mid_ref, back=back, halo=halo, inside=inside):
            r = t * TX + i
            scales = []
            for k in range(TX):
                d = TX + (i - k if t == 0 else k - i)
                sign = inside * (-1.0, 1.0)[t]
                scales.append((inside * by_distance(second_coef, d), sign * by_distance(first_of, d)))
            sums = []
            for p in range(2):
                curve, slope = [], []
                for h in HALVES:
                    c, s = near[4 * p, r, :, h], near[4 * p + 1, r, :, h]
                    for k in range(TX):
                        value = halo[p, k, :, h]
                        c = c + scales[k][0] * value
                        s = s + scales[k][1] * value
                    curve.append(c)
                    slope.append(s)
                sums.append((curve, first_z(slope, lane)))
            (xp, cp), (xq, cq) = sums
            for s, h in enumerate(HALVES):
                aniso, coupled, square = coef[0, r, :, h], coef[1, r, :, h], coef[2, r, :, h]
                sine, cosine, double = coef[3, r, :, h], coef[4, r, :, h], coef[5, r, :, h]
                axial_p = sine * xp[s] + cosine * near[2, r, :, h] + double * cp[s]
                plane_p = xp[s] + near[3, r, :, h] - axial_p
                axial_q = sine * xq[s] + cosine * near[6, r, :, h] + double * cq[s]
                add = inj[r, :, h]
                new_p = 2.0 * mid_ref[0, i, :, h] - back[0, i, :, h] + aniso * plane_p + coupled * axial_q + add
                new_q = 2.0 * mid_ref[1, i, :, h] - back[1, i, :, h] + coupled * plane_p + square * axial_q + add
                emit(t, i, h, new_p, new_q)
            return carry

        lax.fori_loop(0, TX, one, 0, unroll=4)


def step_kernel(tile, plan, near, now, before, halo, coef, inj, new, *packed):
    def emit(t, i, h, new_p, new_q):
        new[0, i, :, h] = new_p
        new[1, i, :, h] = new_q
        for p in packed:
            p[0, i, :, h] = now[0, i, :, h]
            p[1, i, :, h] = new_p

    far_rows(plan, near, ((tile, now, before, halo),), coef, inj, emit)


def joining_kernel(plan, near, now, before, halo, coef, inj, hi_packed, new, packed):
    def emit(t, i, h, new_p, new_q):
        new[0, i, :, h] = new_p
        new[1, i, :, h] = new_q
        packed[0, 0, i, :, h] = now[0, i, :, h]
        packed[0, 1, i, :, h] = new_p

    for k in range(2):
        for i in range(TX):
            packed[1, k, i] = hi_packed[k, i]
    far_rows(plan, near, ((0, now, before, halo),), coef, inj, emit)


def last_hi_kernel(plan, near, hi, hi_b, high, coef, inj, other, part):
    def emit(t, i, h, new_p, new_q):
        del new_q
        part[i, :, h] = new_p * other[1, 0, i, :, h] + hi[0, i, :, h] * other[1, 1, i, :, h]

    far_rows(plan, near, ((1, hi, hi_b, high),), coef, inj, emit)


def last_kernel(plan, near, lo, lo_b, low, coef, inj, other, part_hi, keep, give, part_lo):
    def emit(t, i, h, new_p, new_q):
        del new_q
        part_lo[i, :, h] = new_p * other[0, 0, i, :, h] + lo[0, i, :, h] * other[0, 1, i, :, h]

    far_rows(plan, near, ((0, lo, lo_b, low),), coef, inj, emit)
    part = (part_lo, part_hi)
    first = plan[CORE] == 0
    for t in range(2):
        for i in range(TX):
            low_y, high_y = part[t][i, :HALF_Y], part[t][i, HALF_Y:]
            keep[t, i] = jnp.where(first, low_y, high_y)
            give[t, i] = jnp.where(first, high_y, low_y)


def total_kernel(plan, keep, came, *outs):
    for i in range(TX):
        lo = keep[0, i] + came[0, i]
        hi = keep[1, i] + came[1, i]
        for by in range(4):
            outs[by][i] = jnp.where(plan[SIDE + by] == 0, lo, hi)


def owners_kernel(plan, kept, got_1, got_2, got_3, straight, last, free):
    for i in range(TX):
        parts = [kept[i], got_1[i], got_2[i], got_3[i]]
        for k, out in enumerate((straight, last, free)):
            for core in range(2):
                acc = jnp.zeros_like(parts[0])
                for by in range(4):
                    ours = (plan[OWNER + by] == core) & (plan[ROLE_FROM + by] == k)
                    acc = acc + jnp.where(ours, parts[by], 0.0)
                out[core, i] = acc


def image_kernel(plan, straight, last, last_came, free_came, keep, give):
    high, first = plan[X_HI] == 1, plan[CORE] == 0
    for i in range(TX):
        sums = []
        for core in range(2):
            turned = jnp.where(high, last_came[core, i], last[core, i])
            sums.append(straight[core, i] + turned + free_came[core, i])
        keep[i] = jnp.where(first, sums[0], sums[1])
        give[i] = jnp.where(first, sums[1], sums[0])


def join_kernel(plan, keep, came, out):
    first = plan[CORE] == 0
    for i in range(TX):
        out[i, :HALF_Y] = jnp.where(first, keep[i], came[i])
        out[i, HALF_Y:] = jnp.where(first, came[i], keep[i])


def inject_kernel(plan, source, wavelet, cells, traces, *outs):
    group, forward, base = plan[GROUP], plan[CORE] == 0, 8 * plan[BLOCK]
    count = cells.shape[2]
    lane = lax.broadcasted_iota(jnp.int32, (1, count), 1)
    x, y, depth = (
        jnp.where(
            forward,
            jnp.where(lane == 0, source[group, f], -1),
            cells[f, pl.ds(group, 1), :],
        )
        for f in range(3)
    )
    here = (x >= base) & (x < base + 8)
    spot = jnp.where(here, (x - base) * AY + y, -1)
    which = (lax.broadcasted_iota(jnp.int32, (8 * AY, count), 0) == spot).astype(F32)
    level = lax.broadcasted_iota(jnp.int32, (AZ, count), 0) == depth
    for k in range(STEPS):
        amounts = jnp.where(forward, wavelet[group, k], traces[group, pl.ds(k, 1), :])
        values = jnp.where(level, amounts, 0.0)
        flat = lax.dot_general(
            which,
            values,
            (((1,), (1,)), ((), ())),
            precision=lax.Precision.HIGHEST,
            preferred_element_type=F32,
        )
        for i in range(8):
            outs[k][i] = flat[i * AY : (i + 1) * AY, :]


def sine_cosine(angle):
    sq = angle * angle
    sine = -1.0 / 39916800.0
    for c in (1.0 / 362880.0, -1.0 / 5040.0, 1.0 / 120.0, -1.0 / 6.0, 1.0):
        sine = sine * sq + c
    cosine = 1.0 / 479001600.0
    for c in (-1.0 / 3628800.0, 1.0 / 40320.0, -1.0 / 720.0, 1.0 / 24.0, -0.5, 1.0):
        cosine = cosine * sq + c
    return sine * angle, cosine


def coef_kernel(plan, own, other, out):
    core = plan[CORE]
    for t in range(2):

        def tile(i, carry, t=t):
            mine = [own[t, f, i] for f in range(2)]
            theirs = [other[t, f, i] for f in range(2)]
            velocity = jnp.where(core == 0, mine[0], theirs[0])
            epsilon = jnp.where(core == 0, mine[1], theirs[1])
            delta = jnp.where(core == 0, theirs[0], mine[0])
            angle = jnp.where(core == 0, theirs[1], mine[1])
            square = velocity * velocity
            sine, cosine = sine_cosine(angle)
            k = t * TX + i
            out[0, k] = square * (1.0 + 2.0 * epsilon)
            out[1, k] = square * jnp.sqrt(1.0 + 2.0 * delta)
            out[2, k] = square
            out[3, k] = sine * sine
            out[4, k] = cosine * cosine
            out[5, k] = 2.0 * sine * cosine
            return carry

        lax.fori_loop(0, TX, tile, 0)


HBM = pl.BlockSpec(memory_space=pltpu.HBM)
LIMIT = pltpu.CompilerParams(vmem_limit_bytes=4 * 1024 * 1024)


def in_hbm(value):
    return pltpu.with_memory_space_constraint(value, pltpu.HBM)


def call(kernel, n_in, outs, scratch=()):
    return pl.pallas_call(
        kernel,
        out_shape=[jax.ShapeDtypeStruct(s, F32) for s in outs],
        in_specs=[SMEM] + [VMEM] * n_in,
        out_specs=[VMEM] * len(outs),
        scratch_shapes=[pltpu.VMEM(s, F32) for s in scratch],
        compiler_params=LIMIT,
    )


TILE = (2, TX, AY, AZ)
PART = (TX, HALF_Y, AZ)


def turn_model(value, x_hi, turn_z, turn_y):
    def roll(v, by):
        return send(v, rolled(-by, -by)) if by else v

    def columns(v, r):
        if r == 1:
            return jnp.where(x_hi == 1, v, roll(v, 1))
        if r % 2 == 0:
            return roll(v, r // 2)
        return send(v, rolled(-(r // 2 + 1), -(r // 2)))

    value = lax.switch(turn_z[0], [lambda v, k=k: roll(v, 4 * k) for k in range(4)], value)
    return lax.switch(turn_y[0], [lambda v, r=r: columns(v, r) for r in range(8)], value)


def turn_image(value, x_hi, free_turn):
    def roll(v, by):
        if by % 16 == 0:
            return v
        return roll(roll(v, 8), 7) if by == 15 else send(v, rolled(by, by))

    def columns(v, r):
        low, high = (r + 1) // 2, r // 2
        if r % 2 == 0:
            return roll(v, high)
        if r in (1, 5, 15, 17, 29, 31):
            return jnp.where(x_hi == 1, roll(v, high), roll(v, low))
        return send(v, rolled(low, high))

    return lax.switch(free_turn[0], [lambda v, r=r: columns(v, r) for r in range(32)], value)


def local(
    velocity,
    thomsen_epsilon,
    thomsen_delta,
    tilt_angle,
    fwd_now,
    fwd_before,
    adj_now,
    adj_before,
    wavelet,
    traces,
    offsets,
    source_cell,
    receiver_cell,
):
    shot, aper = lax.axis_index("shot"), lax.axis_index("aper")
    ids = jnp.stack([shot, aper]).astype(jnp.int32)
    swap, up, down = other_core(), rolled(1, 1), rolled(-1, -1)

    plan, turn_all, turn_z, turn_y, own, other, one, two = pl.pallas_call(
        plan_kernel,
        out_shape=[jax.ShapeDtypeStruct((n,), jnp.int32) for n in (40, 1, 1, 1)]
        + [jax.ShapeDtypeStruct(TILE, F32)] * 2
        + [jax.ShapeDtypeStruct((2,) + TILE, F32)] * 2,
        in_specs=[SMEM] * 2 + [HBM] * 8,
        out_specs=[SMEM] * 4 + [VMEM] * 4,
        scratch_shapes=[pltpu.SemaphoreType.DMA((4,))] * 2,
        compiler_params=LIMIT,
    )(
        ids,
        offsets,
        *(in_hbm(v) for v in (velocity, thomsen_epsilon, thomsen_delta, tilt_angle)),
        *(in_hbm(v) for v in (fwd_now, adj_now, fwd_before, adj_before)),
    )
    came = send(other, swap)
    got_one, got_two = send(one, state_first()), send(two, state_second())

    last, free = call(rows_kernel, 2, [TILE] * 2)(plan, own, came)
    last_came = send(last, up)
    free_came = turn_model(free, aper % 2, turn_z, turn_y)
    rows = call(send_kernel, 5, [TILE] * 4)(plan, own, came, last, last_came, free_came)
    got = [send(rows[by], across(by)) for by in range(1, 4)]
    lo, hi, lo_b, hi_b = call(block_kernel, 3, [TILE] * 4)(plan, two, got_one, got_two)
    inj = pl.pallas_call(
        inject_kernel,
        out_shape=[jax.ShapeDtypeStruct((8, AY, AZ), F32)] * STEPS,
        in_specs=[SMEM] * 3 + [VMEM] * 2,
        out_specs=[VMEM] * STEPS,
        compiler_params=LIMIT,
    )(plan, source_cell, wavelet, jnp.transpose(receiver_cell, (2, 0, 1)), traces)

    near_call = pl.pallas_call(
        near_kernel,
        out_shape=jax.ShapeDtypeStruct((7, 8, AY, AZ), F32),
        in_specs=[VMEM] * 2,
        out_specs=VMEM,
        scratch_shapes=[pltpu.VMEM((2, 4 * TX, AY, AZ), F32)],
        compiler_params=LIMIT,
    )
    near = near_call(lo, hi)
    low, high = send(hi, up), send(lo, down)
    tiles = call(tiles_kernel, 8, [(2,) + TILE])(
        plan, rows[0], *got, low, high, near, inj[0]
    )[0]
    coef = call(coef_kernel, 2, [(6, 8, AY, AZ)])(plan, tiles, send(tiles, swap))[0]

    shared = None
    for k in range(STEPS - 1):
        if k > 0:
            low, high = send(hi, up), send(lo, down)
            near = near_call(lo, hi)
        outs = [TILE] * (2 if k == 1 else 1)
        new_hi = call(functools.partial(step_kernel, 1), 6, outs)(plan, near, hi, hi_b, high, coef, inj[k])
        if k == 1:
            new_lo = call(joining_kernel, 7, [TILE, (2,) + TILE])(
                plan, near, lo, lo_b, low, coef, inj[k], new_hi[1]
            )
            shared = send(new_lo[1], swap)
        else:
            new_lo = call(functools.partial(step_kernel, 0), 6, outs)(plan, near, lo, lo_b, low, coef, inj[k])
        lo_b, hi_b, lo, hi = lo, hi, new_lo[0], new_hi[0]
    low, high = send(hi, up), send(lo, down)
    near = near_call(lo, hi)
    part_hi = call(last_hi_kernel, 7, [(TX, AY, AZ)])(plan, near, hi, hi_b, high, coef, inj[STEPS - 1], shared)[0]
    keep, give = call(last_kernel, 8, [(2,) + PART] * 2, [(TX, AY, AZ)])(
        plan, near, lo, lo_b, low, coef, inj[STEPS - 1], shared, part_hi
    )

    parts = call(total_kernel, 2, [PART] * 4)(plan, keep, send(give, swap))
    got = [send(parts[by], across(by)) for by in range(1, 4)]
    straight, last, free = call(owners_kernel, 4, [(2,) + PART] * 3)(plan, parts[0], *got)
    last_came = send(last, down)
    free_came = turn_image(free, aper % 2, turn_all)
    keep, give = call(image_kernel, 4, [PART] * 2)(plan, straight, last, last_came, free_came)
    return call(join_kernel, 2, [(TX, AY, AZ)])(plan, keep, send(give, swap))[0]


def solution(mesh):
    model = P(("shot", "aper"), None, None)
    field = P("shot", None, "aper", None, None)
    return jax.shard_map(
        local,
        mesh=mesh,
        in_specs=(model,) * 4 + (field,) * 4 + (P(),) * 5,
        out_specs=model,
        check_vma=False,
    )
```
